32 devices in a mesh: group: 2 (over core), shard: 4 (over y, x), tensor: 4 (over z).
Axes of the slice: x: 2, y: 2, z: 4, core: 2. Of those that a mesh axis runs over, the one named last changes fastest.
Arguments:
- attn_in_local: bfloat16 [2, 768, 2304], P('group', 'shard', 'tensor'), may hold values from -6 to 6
- attn_out_local: bfloat16 [2, 768, 768], P('group', 'shard', 'tensor'), may hold values from -6 to 6
- ffn_in_local: bfloat16 [2, 768, 3072], P('group', 'shard', 'tensor'), may hold values from -6 to 6
- ffn_out_local: bfloat16 [2, 3072, 768], P('group', 'shard', 'tensor'), may hold values from -6 to 6
- small_local: bfloat16 [2, 1920], P('group'), may hold values from -6 to 6
- dense_old: float32 [16, 442368], P(('shard', 'tensor'), 'group'), may hold values from -6 to 6
- dense_momentum: float32 [16, 442368], P(('shard', 'tensor'), 'group'), may hold values from -6 to 6
- small_old: float32 [1920], P('group'), may hold values from -6 to 6
- small_momentum: float32 [1920], P('group'), may hold values from -6 to 6
- embed_local: bfloat16 [2, 768, 8192], P('group', 'shard', 'tensor'), may hold values from -6 to 6
- embed_old: float32 [768, 8192], P('shard', 'tensor'), may hold values from -6 to 6
- basis: float32 [768, 64], P('shard'), may hold values from -0.21875 to 0.21875
- coeff_momentum: float32 [64, 8192], P(None, 'tensor'), may hold values from -6 to 6
Outputs:
- attn_in_next: float32 [768, 2304], P('shard', 'tensor')
- attn_out_next: float32 [768, 768], P('shard', 'tensor')
- ffn_in_next: float32 [768, 3072], P('shard', 'tensor')
- ffn_out_next: float32 [3072, 768], P('shard', 'tensor')
- dense_momentum_next: float32 [16, 442368], P(('shard', 'tensor'), 'group')
- small_next: float32 [1920], replicated
- small_momentum_next: float32 [1920], P('group')
- embed_next: float32 [768, 8192], P('shard', 'tensor')
- coeff_momentum_next: float32 [64, 8192], P(None, 'tensor')
The draws below stay inside these ranges and needn't reach their ends.
All inputs are finite; a program needn't handle non-finite values.
Results may differ from the reference program's by a relative error of at most 0.0003.
Values sent between devices are 32-bit elements; how exact they have to be, the bound alone decides.
No kernel may reach another device: no remote copies, remote signals or barrier semaphores. Data moves between devices by JAX's collectives and lax.ppermute only.
A program may use at most 64 MiB of HBM per device.

```python
import jax
import jax.numpy as jnp
from jax import lax

D = 768
FF = 3072
VOCAB = 8192
RANK = 64
SMALL = 1920
SHARDS = 16
FLAT = 442368
N_GROUP = 2
N_SHARD = 4
N_TENSOR = 4


def level_of(own_key, extent, shards, least, top_value):
    factor_of, own = 1.0, jax.random.fold_in(own_key, 6)
    for dim, parts in shards:
        steps = jnp.exp(jax.random.uniform(jax.random.fold_in(own, dim), (parts,), jnp.float32, least / len(shards), top_value / len(shards)))
        factor_of = factor_of * jnp.repeat(steps, extent[dim] // parts).reshape([-1 if axis == dim else 1 for axis in range(len(extent))])
    return factor_of


def bell_draw(stream_key, dims, width, limit, cuts=(), kind=jnp.bfloat16):
    drawn = width * jax.random.normal(stream_key, dims, jnp.float32)
    if cuts:
        drawn = drawn * level_of(stream_key, dims, cuts, -0.22, 0.18)
    return jnp.clip(drawn, -limit, limit).astype(kind)


def setup_inputs(seed: int = 0) -> dict:
    key_of = jax.random.split(jax.random.key(seed), 14)
    return {
        "attn_in_local": bell_draw(key_of[0], (N_GROUP, D, 3 * D), 1.0, 6.0, ((0, 2), (1, 4), (2, 4))),
        "attn_out_local": bell_draw(key_of[1], (N_GROUP, D, D), 1.0, 6.0, ((0, 2), (1, 4), (2, 4))),
        "ffn_in_local": bell_draw(key_of[2], (N_GROUP, D, FF), 1.0, 6.0, ((0, 2), (1, 4), (2, 4))),
        "ffn_out_local": bell_draw(key_of[3], (N_GROUP, FF, D), 1.0, 6.0, ((0, 2), (1, 4), (2, 4))),
        "small_local": bell_draw(key_of[4], (N_GROUP, SMALL), 1.0, 6.0, ((0, 2),)),
        "dense_old": bell_draw(key_of[5], (SHARDS, FLAT), 1.0, 6.0, ((0, 16), (1, 2)), jnp.float32),
        "dense_momentum": bell_draw(key_of[6], (SHARDS, FLAT), 1.0, 6.0, ((0, 16), (1, 2)), jnp.float32),
        "small_old": bell_draw(key_of[7], (SMALL,), 1.0, 6.0, ((0, 2),), jnp.float32),
        "small_momentum": bell_draw(key_of[8], (SMALL,), 1.0, 6.0, ((0, 2),), jnp.float32),
        "embed_local": bell_draw(key_of[9], (N_GROUP, D, VOCAB), 1.0, 6.0, ((0, 2), (1, 4), (2, 4))),
        "embed_old": bell_draw(key_of[10], (D, VOCAB), 1.0, 6.0, ((0, 4), (1, 4)), jnp.float32),
        "basis": bell_draw(key_of[11], (D, RANK), D ** -0.5, 0.21875, ((0, 4),), jnp.float32),
        "coeff_momentum": bell_draw(key_of[12], (RANK, VOCAB), 1.0, 6.0, ((1, 4),), jnp.float32),
    }


momentum_coef = 0.5
outer_rate = 0.7


def flatten_shards(matrices):
    pieces = []
    for matrix in matrices:
        row_count, col_count = matrix.shape
        blocks = matrix.reshape(N_SHARD, row_count // N_SHARD, N_TENSOR, col_count // N_TENSOR).transpose(0, 2, 1, 3)
        pieces.append(blocks.reshape(N_SHARD * N_TENSOR, -1))
    return jnp.concatenate(pieces, axis=1)


def unflatten_shards(flat, shapes):
    results = []
    offset = 0
    for row_count, col_count in shapes:
        block_size = (row_count // N_SHARD) * (col_count // N_TENSOR)
        piece = flat[:, offset:offset + block_size].reshape(N_SHARD, N_TENSOR, row_count // N_SHARD, col_count // N_TENSOR)
        results.append(piece.transpose(0, 2, 1, 3).reshape(row_count, col_count))
        offset = offset + block_size
    return results


def nesterov(old_value, momentum, delta):
    moved = momentum_coef * momentum + delta
    return old_value - outer_rate * (delta + momentum_coef * moved), moved


def reference(attn_in_local, attn_out_local, ffn_in_local, ffn_out_local, small_local, dense_old, dense_momentum, small_old, small_momentum, embed_local, embed_old, basis, coeff_momentum):
    dense_total = jnp.zeros(dense_old.shape, jnp.float32)
    small_total = jnp.zeros(small_old.shape, jnp.float32)
    coeff_total = jnp.zeros(coeff_momentum.shape, jnp.float32)
    for member in range(N_GROUP):
        flat = flatten_shards([attn_in_local[member], attn_out_local[member], ffn_in_local[member], ffn_out_local[member]])
        dense_total = dense_total + flat.astype(jnp.float32)
        small_total = small_total + small_local[member].astype(jnp.float32)
        difference = embed_old - embed_local[member].astype(jnp.float32)
        coeff_total = coeff_total + jnp.dot(basis.T, difference, precision=lax.Precision.HIGHEST, preferred_element_type=jnp.float32)
    dense_new, dense_moved = nesterov(dense_old, dense_momentum, dense_old - dense_total / N_GROUP)
    small_new, small_moved = nesterov(small_old, small_momentum, small_old - small_total / N_GROUP)
    shapes = [attn_in_local.shape[1:], attn_out_local.shape[1:], ffn_in_local.shape[1:], ffn_out_local.shape[1:]]
    attn_in_next, attn_out_next, ffn_in_next, ffn_out_next = unflatten_shards(dense_new, shapes)
    coeff = coeff_total / N_GROUP
    coeff_moved = momentum_coef * coeff_momentum + coeff
    update = coeff + momentum_coef * coeff_moved
    embed_next = embed_old - outer_rate * jnp.dot(basis, update, precision=lax.Precision.HIGHEST, preferred_element_type=jnp.float32)
    return (attn_in_next, attn_out_next, ffn_in_next, ffn_out_next, dense_moved, small_new, small_moved, embed_next, coeff_moved)
```

```python
import jax
import jax.numpy as jnp
from jax import lax
from jax.experimental import pallas as pl
from jax.experimental.pallas import tpu as pltpu
from jax.sharding import PartitionSpec as P

momentum_coef = 0.5
outer_rate = 0.7

f32 = jnp.float32
bf16 = jnp.bfloat16
LANES = 128
HALF = LANES // 2


def nesterov(old_value, momentum, delta):
    moved = momentum_coef * momentum + delta
    return (old_value - outer_rate * (delta + momentum_coef * moved), moved)


def general(
    attn_in_local,
    attn_out_local,
    ffn_in_local,
    ffn_out_local,
    small_local,
    dense_old,
    dense_momentum,
    small_old,
    small_momentum,
    embed_local,
    embed_old,
    basis,
    coeff_momentum,
):
    groups = lax.axis_size("group")
    matrices = (attn_in_local, attn_out_local, ffn_in_local, ffn_out_local)
    local_terms = jnp.concatenate([matrix[0].reshape(-1) for matrix in matrices]).astype(f32)
    small_terms = small_local[0].astype(f32)
    old_flat = dense_old[0]
    momentum_flat = dense_momentum[0]
    dense_part, small_part = (
        lax.psum_scatter(local_terms, "group", scatter_dimension=0, tiled=True),
        lax.psum_scatter(small_terms, "group", scatter_dimension=0, tiled=True),
    )
    dense_new, dense_moved = nesterov(old_flat, momentum_flat, old_flat - dense_part / groups)
    small_new, small_moved = nesterov(small_old, small_momentum, small_old - small_part / groups)
    full_flat, small_next = (
        lax.all_gather(dense_new, "group", axis=0, tiled=True),
        lax.all_gather(small_new, "group", axis=0, tiled=True),
    )
    results = []
    offset = 0
    for matrix in matrices:
        block_size = matrix.shape[1] * matrix.shape[2]
        results.append(
            full_flat[offset : offset + block_size].reshape(matrix.shape[1], matrix.shape[2])
        )
        offset = offset + block_size
    difference = embed_old - embed_local[0].astype(f32)
    partial_coeff = lax.dot_general(
        basis,
        difference,
        (((0,), (0,)), ((), ())),
        precision=lax.Precision.HIGHEST,
        preferred_element_type=f32,
    )
    coeff = lax.psum(partial_coeff, ("group", "shard")) / groups
    coeff_moved = momentum_coef * coeff_momentum + coeff
    update = coeff + momentum_coef * coeff_moved
    embed_next = embed_old - outer_rate * jnp.dot(
        basis, update, precision=lax.Precision.HIGHEST, preferred_element_type=f32
    )
    return (
        results[0],
        results[1],
        results[2],
        results[3],
        dense_moved[None, :],
        small_next,
        small_moved,
        embed_next,
        coeff_moved,
    )


local_coef = outer_rate * (1 + momentum_coef) / 2
old_coef = 1 - outer_rate * (1 + momentum_coef)
mom_coef = -outer_rate * momentum_coef * momentum_coef


def split(value):
    high = value.astype(bf16)
    return high, (value - high.astype(f32)).astype(bf16)


def partial_kernel(group_ref, basis_ref, local_ref, old_ref, out_ref):
    del group_ref
    rank = basis_ref.shape[0]
    high, low = split(basis_ref[...])
    both = jnp.concatenate([high, low], axis=0)
    diff_high, diff_low = split(old_ref[...] - local_ref[...].astype(f32))
    first = jnp.dot(both, diff_high, preferred_element_type=f32)
    second = jnp.dot(high, diff_low, preferred_element_type=f32)
    out_ref[...] = first[:rank] + first[rank:] + second


def partial_coeff(group, basis_t, local, old, other):
    rank, depth = basis_t.shape
    columns = old.shape[1] // 2
    steps = 2
    block = columns // steps

    def half(step, group_ref):
        side = 1 - group_ref[0] if other else group_ref[0]
        return (0, side * steps + step)

    return pl.pallas_call(
        partial_kernel,
        grid_spec=pltpu.PrefetchScalarGridSpec(
            num_scalar_prefetch=1,
            grid=(steps,),
            in_specs=[
                pl.BlockSpec((rank, depth), lambda step, group_ref: (0, 0)),
                pl.BlockSpec((depth, block), half),
                pl.BlockSpec((depth, block), half),
            ],
            out_specs=pl.BlockSpec((rank, block), lambda step, group_ref: (0, step)),
        ),
        out_shape=jax.ShapeDtypeStruct((rank, columns), f32),
        cost_estimate=pl.CostEstimate(
            flops=6 * rank * depth * columns, bytes_accessed=6 * depth * columns, transcendentals=0
        ),
        name="partial_coeff",
    )(group, basis_t, local, old)


def embed_kernel(group_ref, basis_ref, coeff_ref, moment_ref, old_ref, *refs):
    del group_ref
    embed_ref, moved_ref = refs[-2:]
    moved = momentum_coef * moment_ref[...] + coeff_ref[...]
    moved_ref[...] = moved
    update = coeff_ref[...] + momentum_coef * moved
    high, low = split(basis_ref[...])
    up_high, up_low = split(update)
    product = lax.dot_general(
        jnp.concatenate([high, low, high], axis=0),
        jnp.concatenate([up_high, up_high, up_low], axis=0),
        (((0,), (0,)), ((), ())),
        preferred_element_type=f32,
    )
    embed_ref[...] = old_ref[...] - outer_rate * product


def embed_half(group, basis_t, coeff, moment, old, before):
    rank, depth = basis_t.shape
    width = old.shape[1]
    columns = width // 2
    steps = 2
    block = columns // steps

    def half(step, group_ref):
        side = group_ref[0] if before is None else 1 - group_ref[0]
        return (0, side * steps + step)

    more = () if before is None else before
    return pl.pallas_call(
        embed_kernel,
        grid_spec=pltpu.PrefetchScalarGridSpec(
            num_scalar_prefetch=1,
            grid=(steps,),
            in_specs=[
                pl.BlockSpec((rank, depth), lambda step, group_ref: (0, 0)),
                pl.BlockSpec((rank, block), lambda step, group_ref: (0, step)),
                pl.BlockSpec((rank, block), half),
                pl.BlockSpec((depth, block), half),
            ]
            + [pl.BlockSpec(memory_space=pl.ANY)] * len(more),
            out_specs=[pl.BlockSpec((depth, block), half), pl.BlockSpec((rank, block), half)],
        ),
        out_shape=[
            jax.ShapeDtypeStruct((depth, width), f32),
            jax.ShapeDtypeStruct((rank, width), f32),
        ],
        input_output_aliases={} if before is None else {5: 0, 6: 1},
        cost_estimate=pl.CostEstimate(
            flops=6 * rank * depth * columns, bytes_accessed=8 * depth * columns, transcendentals=0
        ),
        name="embed_half",
    )(group, basis_t, coeff, moment, old, *more)


def low_lanes(rows):
    return lax.broadcasted_iota(jnp.int32, (rows, LANES), 1) < HALF


def turn(value):
    return pltpu.roll(value, HALF, 1)


def attn_tiles(in_ref, out_ref):
    whole = in_ref.shape[-1] // LANES
    tiles = [in_ref[0, :, k * LANES : (k + 1) * LANES].astype(f32) for k in range(whole)]
    last = in_ref[0, :, whole * LANES :].astype(f32)
    side = out_ref[0, :, LANES:].astype(f32)
    tiles.append(jnp.concatenate([last, side], axis=-1))
    tiles.append(out_ref[0, :, :LANES].astype(f32))
    return tiles


def unflatten_attn(flat, put, rows):
    pairs = rows // 2
    low = low_lanes(pairs)
    inner = [flat(j, pairs, 9) for j in range(9)]
    base = pairs * 9
    outer = [flat(base + j, pairs, 3) for j in range(3)]
    turned = [turn(inner[j]) for j in range(4, 9)]
    turned_out = [turn(outer[j]) for j in (1, 2)]
    for k in range(4):
        put(0, k, inner[k])
        put(1, k, jnp.where(low, turned[k], turned[k + 1]))
    put(0, 4, jnp.where(low, inner[4], turned_out[0]))
    put(1, 4, jnp.where(low, turned[4], outer[2]))
    put(0, 5, outer[0])
    put(1, 5, jnp.where(low, turned_out[0], turned_out[1]))


def flatten_attn(get, rows):
    pairs = rows // 2
    low = low_lanes(pairs)
    even = [get(0, k) for k in range(6)]
    odd = [get(1, k) for k in range(6)]
    turned = [turn(odd[k]) for k in range(5)]
    pieces = [(k, 9, even[k]) for k in range(4)]
    pieces.append((4, 9, jnp.where(low, even[4], turned[0])))
    for k in range(4):
        pieces.append((5 + k, 9, jnp.where(low, turned[k], turned[k + 1])))
    base = pairs * 9
    pieces.append((base, 3, even[5]))
    turned_out = turn(odd[5])
    pieces.append((base + 1, 3, jnp.where(low, turn(even[4]), turned_out)))
    pieces.append((base + 2, 3, jnp.where(low, turned_out, odd[4])))
    return pieces


def before_kernel(
    group_ref, in_ref, out_ref, up_ref, down_ref, old_ref, mom_ref, small_ref, small_old_ref,
    small_mom_ref, send_ref, wide_ref,
):
    rows = up_ref.shape[1]
    mid = rows // 2
    block = rows + mid
    tiles = up_ref.shape[2] // LANES
    small = small_old_ref.shape[1]

    def flat(start, count, stride):
        at = pl.ds(start, count, stride=stride)
        return old_coef * old_ref[at, :] + mom_coef * mom_ref[at, :]

    def put(start, tile, value):
        send_ref[tile, pl.ds(block + start, rows // 2, stride=2), :] = value

    def put_small(other, own):
        own_terms = (
            old_coef * small_old_ref[...] + mom_coef * small_mom_ref[...] + local_coef * own
        )
        send_ref[:, 2 * block :, :] = jnp.zeros((tiles, 8, LANES), f32)
        for tile, value in enumerate((other, own_terms)):
            for row in range(pl.cdiv(small, LANES)):
                piece = value[:, row * LANES : (row + 1) * LANES]
                at = 2 * block + row
                send_ref[tile, at : at + 1, : piece.shape[1]] = piece

    @pl.when(group_ref[0] == 0)
    def _():
        unflatten_attn(flat, put, rows)
        for k, value in enumerate(attn_tiles(in_ref, out_ref)):
            send_ref[k, block : block + rows, :] += local_coef * value
        base = rows * tiles
        for k in range(tiles):
            columns = slice(k * LANES, (k + 1) * LANES)
            send_ref[k, :mid, :] = up_ref[0, mid:, columns].astype(f32)
            send_ref[k, mid:block, :] = down_ref[0, :, columns].astype(f32)
            send_ref[k, block + rows : 2 * block, :] = flat(base + k, mid, tiles) + (
                local_coef * up_ref[0, :mid, columns].astype(f32)
            )
        values = small_ref[...].astype(f32)
        put_small(values[:, small:], values[:, :small])

    @pl.when(group_ref[0] == 1)
    def _():
        for k, value in enumerate(attn_tiles(in_ref, out_ref)):
            send_ref[k, :rows, :] = value
        for k in range(tiles):
            columns = slice(k * LANES, (k + 1) * LANES)
            send_ref[k, rows:block, :] = up_ref[0, :mid, columns].astype(f32)
            send_ref[k, block : block + mid, :] = flat(k, mid, tiles) + (
                local_coef * up_ref[0, mid:, columns].astype(f32)
            )
        base = mid * tiles
        pairs = tiles * HALF
        low = low_lanes(pairs)
        first, second, third = (flat(base + j, pairs, 3) for j in range(3))
        turned, turned_more = turn(second), turn(third)
        even, odd = pl.ds(0, pairs, stride=2), pl.ds(1, pairs, stride=2)
        wide_ref[0, even, :] = first
        wide_ref[1, even, :] = second
        wide_ref[0, odd, :] = jnp.where(low, turned, turned_more)
        wide_ref[1, odd, :] = turned_more
        start = block + mid
        for k in range(tiles):
            columns = slice(k * LANES, (k + 1) * LANES)
            upper = wide_ref[0, columns, :].T
            lower = wide_ref[1, columns, :].T[:HALF]
            send_ref[k, start : start + LANES, :] = upper + (
                local_coef * down_ref[0, :LANES, columns].astype(f32)
            )
            send_ref[k, start + LANES : 2 * block, :] = lower + (
                local_coef * down_ref[0, LANES:, columns].astype(f32)
            )
        values = small_ref[...].astype(f32)
        put_small(values[:, :small], values[:, small:])


def after_kernel(
    group_ref, recv_ref, send_ref, in_ref, out_ref, up_ref, down_ref, old_ref, mom_ref, small_ref,
    small_old_ref, small_mom_ref, in_next_ref, out_next_ref, up_next_ref, down_next_ref, moved_ref,
    small_next_ref, small_moved_ref, sum_ref, wide_ref,
):
    rows = up_ref.shape[1]
    mid = rows // 2
    block = rows + mid
    tiles = up_ref.shape[2] // LANES
    small = small_old_ref.shape[1]

    def put_moved(start, stride, value):
        at = pl.ds(start, value.shape[0], stride=stride)
        moved_ref[at, :] = momentum_coef * mom_ref[at, :] + (old_ref[at, :] - 0.5 * value)

    def get(start, tile):
        return sum_ref[tile, pl.ds(start, rows // 2, stride=2), :]

    def put_attn(tile, value):
        whole = in_ref.shape[-1] // LANES
        if tile < whole:
            in_next_ref[:, tile * LANES : (tile + 1) * LANES] = value
        elif tile == whole:
            in_next_ref[:, tile * LANES :] = value[:, :HALF]
            out_next_ref[:, LANES:] = turn(value)[:, :HALF]
        else:
            out_next_ref[:, :LANES] = value

    def small_row(ref, tile):
        pieces = []
        for row in range(pl.cdiv(small, LANES)):
            at = 2 * block + row
            pieces.append(ref[tile, at : at + 1, : min(LANES, small - row * LANES)])
        return jnp.concatenate(pieces, axis=1)

    def put_small(other, own, first):
        theirs = small_row(recv_ref, 0)
        mine = small_row(send_ref, 1) + local_coef * theirs
        rest = small_row(recv_ref, 1) + local_coef * other
        both = [mine, rest] if first else [rest, mine]
        small_next_ref[...] = jnp.concatenate(both, axis=1)
        small_moved_ref[...] = momentum_coef * small_mom_ref[...] + (
            small_old_ref[...] - 0.5 * (own + theirs)
        )

    @pl.when(group_ref[0] == 0)
    def _():
        for k, value in enumerate(attn_tiles(in_ref, out_ref)):
            theirs = recv_ref[k, :rows, :]
            put_attn(k, send_ref[k, block : block + rows, :] + local_coef * theirs)
            sum_ref[k, :, :] = value + theirs
        for start, stride, value in flatten_attn(get, rows):
            put_moved(start, stride, value)
        base = rows * tiles
        for k in range(tiles):
            columns = slice(k * LANES, (k + 1) * LANES)
            theirs = recv_ref[k, rows:block, :]
            up_next_ref[:mid, columns] = (
                send_ref[k, block + rows : 2 * block, :] + local_coef * theirs
            )
            put_moved(base + k, tiles, up_ref[0, :mid, columns].astype(f32) + theirs)
            up_next_ref[mid:, columns] = recv_ref[k, block : block + mid, :] + (
                local_coef * up_ref[0, mid:, columns].astype(f32)
            )
            down_next_ref[:, columns] = recv_ref[k, block + mid : 2 * block, :] + (
                local_coef * down_ref[0, :, columns].astype(f32)
            )
        values = small_ref[...].astype(f32)
        put_small(values[:, small:], values[:, :small], True)

    @pl.when(group_ref[0] == 1)
    def _():
        for k, value in enumerate(attn_tiles(in_ref, out_ref)):
            put_attn(k, recv_ref[k, block : block + rows, :] + local_coef * value)
        for k in range(tiles):
            columns = slice(k * LANES, (k + 1) * LANES)
            up_next_ref[:mid, columns] = recv_ref[k, block + rows : 2 * block, :] + (
                local_coef * up_ref[0, :mid, columns].astype(f32)
            )
            theirs = recv_ref[k, :mid, :]
            up_next_ref[mid:, columns] = send_ref[k, block : block + mid, :] + local_coef * theirs
            put_moved(k, tiles, up_ref[0, mid:, columns].astype(f32) + theirs)
            theirs = recv_ref[k, mid:block, :]
            down_next_ref[:, columns] = (
                send_ref[k, block + mid : 2 * block, :] + local_coef * theirs
            )
            total = down_ref[0, :, columns].astype(f32) + theirs
            wide_ref[0, columns, :] = total[:LANES].T
            lower = jnp.concatenate([total[LANES:], total[LANES:]], axis=0)
            wide_ref[1, columns, :] = lower.T
        base = mid * tiles
        pairs = tiles * HALF
        low = low_lanes(pairs)
        even, odd = pl.ds(0, pairs, stride=2), pl.ds(1, pairs, stride=2)
        odd_first = turn(wide_ref[0, odd, :])
        put_moved(base, 3, wide_ref[0, even, :])
        put_moved(base + 1, 3, jnp.where(low, wide_ref[1, even, :], odd_first))
        put_moved(base + 2, 3, jnp.where(low, odd_first, wide_ref[1, odd, :]))
        values = small_ref[...].astype(f32)
        put_small(values[:, :small], values[:, small:], False)


WHOLE = pl.BlockSpec(memory_space=pltpu.VMEM)
SCALAR = pl.BlockSpec(memory_space=pltpu.SMEM)


def dense_before(group, matrices, flats, smalls):
    _, rows, width = matrices[2].shape
    return pl.pallas_call(
        before_kernel,
        in_specs=[SCALAR] + [WHOLE] * 9,
        out_specs=WHOLE,
        out_shape=jax.ShapeDtypeStruct((width // LANES, 3 * rows + 8, LANES), f32),
        scratch_shapes=[pltpu.VMEM((2, width, LANES), f32)],
        compiler_params=pltpu.CompilerParams(vmem_limit_bytes=20 * 2**20),
        cost_estimate=pl.CostEstimate(
            flops=9 * rows * width, bytes_accessed=30 * rows * width, transcendentals=0
        ),
        name="dense_before",
    )(group, *matrices, *flats, *smalls)


def dense_after(group, received, sent, matrices, flats, smalls):
    _, rows, width = matrices[2].shape
    outs = [matrix.shape[1:] for matrix in matrices]
    outs += [flats[0].shape, smalls[0].shape, smalls[1].shape]
    return pl.pallas_call(
        after_kernel,
        in_specs=[SCALAR] + [WHOLE] * 11,
        out_specs=[WHOLE] * 7,
        out_shape=[jax.ShapeDtypeStruct(shape, f32) for shape in outs],
        scratch_shapes=[
            pltpu.VMEM((width // LANES, rows, LANES), f32),
            pltpu.VMEM((2, width, LANES), f32),
        ],
        compiler_params=pltpu.CompilerParams(vmem_limit_bytes=24 * 2**20),
        cost_estimate=pl.CostEstimate(
            flops=9 * rows * width, bytes_accessed=40 * rows * width, transcendentals=0
        ),
        name="dense_after",
    )(group, received, sent, *matrices, *flats, *smalls)


def paired(
    attn_in_local,
    attn_out_local,
    ffn_in_local,
    ffn_out_local,
    small_local,
    dense_old,
    dense_momentum,
    small_old,
    small_momentum,
    embed_local,
    embed_old,
    basis,
    coeff_momentum,
):
    position = lax.axis_index("group")
    group = position.astype(jnp.int32).reshape(1)
    swap = [(0, 1), (1, 0)]
    shards_count = lax.axis_size("shard")
    near = [(i, i ^ 1) for i in range(shards_count)]
    far = [(i, i ^ 2) for i in range(shards_count)]

    basis_t = basis.T
    local = embed_local[0]
    theirs = partial_coeff(group, basis_t, local, embed_old, True)
    theirs = lax.ppermute(theirs, "group", swap)
    mine = partial_coeff(group, basis_t, local, embed_old, False)
    columns = mine.shape[1] // 2

    matrices = (attn_in_local, attn_out_local, ffn_in_local, jnp.swapaxes(ffn_out_local, 1, 2))
    flats = (dense_old.reshape(-1, LANES), dense_momentum.reshape(-1, LANES))
    smalls = (small_local, small_old[None, :], small_momentum[None, :])
    sent = dense_before(group, matrices, flats, smalls)
    received = lax.ppermute(sent, "group", swap)
    dense = dense_after(group, received, sent, matrices, flats, smalls)

    left = mine[:, :columns] + theirs[:, :columns]
    right = mine[:, columns:] + theirs[:, columns:]
    left, right = (
        left + lax.ppermute(left, "shard", near),
        right + lax.ppermute(right, "shard", far),
    )
    left, right = (
        left + lax.ppermute(left, "shard", far),
        right + lax.ppermute(right, "shard", near),
    )
    own = 0.5 * jnp.concatenate([left, right], axis=1)
    rest = lax.ppermute(own, "group", swap)
    done = embed_half(group, basis_t, own, coeff_momentum, embed_old, None)
    embed_next, coeff_moved = embed_half(group, basis_t, rest, coeff_momentum, embed_old, done)

    attn_in_next, attn_out_next, ffn_in_next, ffn_out_next, moved, small_next, small_moved = dense
    return (
        attn_in_next,
        attn_out_next,
        ffn_in_next,
        ffn_out_next.T,
        moved.reshape(dense_old.shape),
        small_next[0],
        small_moved[0],
        embed_next,
        coeff_moved,
    )


def is_paired(mesh, shapes):
    attn_in, attn_out, ffn_in, ffn_out = (shape[1:] for shape in shapes[:4])
    rows = ffn_in[0]
    return (
        mesh.shape["group"] == 2
        and mesh.shape["shard"] == 4
        and attn_in == (rows, 4 * LANES + HALF)
        and attn_out == (rows, LANES + HALF)
        and ffn_in[1] == 6 * LANES
        and ffn_out == (6 * LANES, rows)
        and rows == LANES + HALF
        and shapes[7][0] <= 8 * LANES
        and shapes[10][1] % (8 * LANES) == 0
    )


def solution(mesh):
    placed = (
        P("group", "shard", "tensor"),
        P("group", "shard", "tensor"),
        P("group", "shard", "tensor"),
        P("group", "shard", "tensor"),
        P("group", None),
        P(("shard", "tensor"), "group"),
        P(("shard", "tensor"), "group"),
        P("group"),
        P("group"),
        P("group", "shard", "tensor"),
        P("shard", "tensor"),
        P("shard", None),
        P(None, "tensor"),
    )

    def shards(*args):
        plan = paired if is_paired(mesh, [arg.shape for arg in args]) else general
        return plan(*args)

    return jax.shard_map(
        shards,
        mesh=mesh,
        in_specs=placed,
        out_specs=(
            P("shard", "tensor"),
            P("shard", "tensor"),
            P("shard", "tensor"),
            P("shard", "tensor"),
            P(("shard", "tensor"), "group"),
            P(),
            P("group"),
            P("shard", "tensor"),
            P(None, "tensor"),
        ),
        check_vma=False,
    )
```

```python
import functools

import jax
import jax.numpy as jnp
from jax import lax
from jax.experimental import pallas as pl
from jax.experimental.pallas import tpu as pltpu
from jax.sharding import PartitionSpec as P

momentum_coef = 0.5
outer_rate = 0.7

f32 = jnp.float32
bf16 = jnp.bfloat16
LANES = 128
HALF = LANES // 2


def nesterov(old_value, momentum, delta):
    moved = momentum_coef * momentum + delta
    return (old_value - outer_rate * (delta + momentum_coef * moved), moved)


def general(
    attn_in_local,
    attn_out_local,
    ffn_in_local,
    ffn_out_local,
    small_local,
    dense_old,
    dense_momentum,
    small_old,
    small_momentum,
    embed_local,
    embed_old,
    basis,
    coeff_momentum,
):
    groups = lax.axis_size("group")
    matrices = (attn_in_local, attn_out_local, ffn_in_local, ffn_out_local)
    local_terms = jnp.concatenate([matrix[0].reshape(-1) for matrix in matrices]).astype(f32)
    small_terms = small_local[0].astype(f32)
    old_flat = dense_old[0]
    momentum_flat = dense_momentum[0]
    dense_part, small_part = (
        lax.psum_scatter(local_terms, "group", scatter_dimension=0, tiled=True),
        lax.psum_scatter(small_terms, "group", scatter_dimension=0, tiled=True),
    )
    dense_new, dense_moved = nesterov(old_flat, momentum_flat, old_flat - dense_part / groups)
    small_new, small_moved = nesterov(small_old, small_momentum, small_old - small_part / groups)
    full_flat, small_next = (
        lax.all_gather(dense_new, "group", axis=0, tiled=True),
        lax.all_gather(small_new, "group", axis=0, tiled=True),
    )
    results = []
    offset = 0
    for matrix in matrices:
        block_size = matrix.shape[1] * matrix.shape[2]
        results.append(
            full_flat[offset : offset + block_size].reshape(matrix.shape[1], matrix.shape[2])
        )
        offset = offset + block_size
    difference = embed_old - embed_local[0].astype(f32)
    partial_coeff = lax.dot_general(
        basis,
        difference,
        (((0,), (0,)), ((), ())),
        precision=lax.Precision.HIGHEST,
        preferred_element_type=f32,
    )
    coeff = lax.psum(partial_coeff, ("group", "shard")) / groups
    coeff_moved = momentum_coef * coeff_momentum + coeff
    update = coeff + momentum_coef * coeff_moved
    embed_next = embed_old - outer_rate * jnp.dot(
        basis, update, precision=lax.Precision.HIGHEST, preferred_element_type=f32
    )
    return (
        results[0],
        results[1],
        results[2],
        results[3],
        dense_moved[None, :],
        small_next,
        small_moved,
        embed_next,
        coeff_moved,
    )


local_coef = outer_rate * (1 + momentum_coef) / 2
old_coef = 1 - outer_rate * (1 + momentum_coef)
mom_coef = -outer_rate * momentum_coef * momentum_coef


def split(value):
    high = value.astype(bf16)
    return high, (value - high.astype(f32)).astype(bf16)


CHUNKS = 2
WHOLE = pl.BlockSpec(memory_space=pltpu.VMEM)
SCALAR = pl.BlockSpec(memory_space=pltpu.SMEM)
ANY = pl.BlockSpec(memory_space=pl.ANY)


def in_hbm(arrays):
    return [pltpu.with_memory_space_constraint(array, pltpu.HBM) for array in arrays]


def side_start(side_ref, other, columns):
    side = 1 - side_ref[0] if other else side_ref[0]
    return side * columns


def partial_kernel(other, side_ref, basis_hbm, local_hbm, old_hbm, moment_hbm, *refs):
    if other:
        out_ref, old_ref, basis_ref, local_ref, sems = refs
    else:
        out_ref, old_ref, moment_ref, stack_ref, basis_ref, local_ref, sems = refs
    rank, columns = out_ref.shape
    block = columns // CHUNKS
    start = side_start(side_ref, other, columns)
    copies = [pltpu.make_async_copy(basis_hbm, basis_ref, sems.at[0])]
    for k in range(CHUNKS):
        source = pl.ds(pl.multiple_of(start + k * block, block), block)
        target = pl.ds(k * block, block)
        copies.append(
            pltpu.make_async_copy(
                old_hbm.at[:, source], old_ref.at[:, target], sems.at[1 + 2 * k]
            )
        )
        copies.append(
            pltpu.make_async_copy(
                local_hbm.at[:, source], local_ref.at[:, target], sems.at[2 + 2 * k]
            )
        )
    if not other:
        copies.append(pltpu.make_async_copy(moment_hbm, moment_ref, sems.at[1 + 2 * CHUNKS]))
    for copy in copies:
        copy.start()
    copies[0].wait()
    high, low = split(basis_ref[...])
    both = jnp.concatenate([high, low], axis=0)
    for k in range(CHUNKS):
        copies[1 + 2 * k].wait()
        copies[2 + 2 * k].wait()
        target = slice(k * block, (k + 1) * block)
        diff_high, diff_low = split(old_ref[:, target] - local_ref[:, target].astype(f32))
        first = jnp.dot(both, diff_high, preferred_element_type=f32)
        second = jnp.dot(high, diff_low, preferred_element_type=f32)
        out_ref[:, target] = first[:rank] + first[rank:] + second
    if not other:
        basis = basis_ref[...]
        stack = jnp.concatenate([high.astype(f32), basis - high.astype(f32), high.astype(f32)], axis=0)
        stack_ref[...] = stack.T.astype(bf16)
        copies[-1].wait()


def partial_coeff(side, basis_t, local, old, moment, other):
    rank, depth = basis_t.shape
    width = old.shape[1]
    columns = width // 2
    out_shape = [
        jax.ShapeDtypeStruct((rank, columns), f32),
        jax.ShapeDtypeStruct((depth, columns), f32),
    ]
    if not other:
        out_shape += [
            jax.ShapeDtypeStruct((rank, width), f32),
            jax.ShapeDtypeStruct((depth, 3 * rank), bf16),
        ]
    return pl.pallas_call(
        functools.partial(partial_kernel, other),
        in_specs=[SCALAR] + [ANY] * 4,
        out_specs=[WHOLE] * len(out_shape),
        out_shape=out_shape,
        scratch_shapes=[
            pltpu.VMEM((rank, depth), f32),
            pltpu.VMEM((depth, columns), bf16),
            pltpu.SemaphoreType.DMA((2 + 2 * CHUNKS,)),
        ],
        compiler_params=pltpu.CompilerParams(vmem_limit_bytes=8 * 2**20),
        cost_estimate=pl.CostEstimate(
            flops=6 * rank * depth * columns, bytes_accessed=6 * depth * columns, transcendentals=0
        ),
        name="partial_coeff",
    )(side, *in_hbm((basis_t, local, old, moment)))


def embed_kernel(other, side_ref, stack_ref, coeff_ref, moment_ref, old_ref, *refs):
    embed_hbm, moved_hbm, embed_ref, moved_ref, sems = refs[-5:]
    columns = coeff_ref.shape[1]
    block = columns // CHUNKS
    start = side_start(side_ref, other, columns)
    copies = []
    for k in range(CHUNKS):
        here = slice(k * block, (k + 1) * block)
        there = pl.ds(pl.multiple_of(start + k * block, block), block)
        coeff = coeff_ref[:, here]
        moved = momentum_coef * moment_ref[:, there] + coeff
        moved_ref[:, here] = moved
        up_high, up_low = split(coeff + momentum_coef * moved)
        product = jnp.dot(
            stack_ref[...],
            jnp.concatenate([up_high, up_high, up_low], axis=0),
            preferred_element_type=f32,
        )
        embed_ref[:, here] = old_ref[:, here] - outer_rate * product
        target = pl.ds(k * block, block)
        for source_ref, target_hbm, at in ((moved_ref, moved_hbm, 0), (embed_ref, embed_hbm, 1)):
            copy = pltpu.make_async_copy(
                source_ref.at[:, target], target_hbm.at[:, there], sems.at[2 * k + at]
            )
            copy.start()
            copies.append(copy)
    for copy in copies:
        copy.wait()


def embed_half(side, stack, coeff, moment, old, before):
    rank, columns = coeff.shape
    depth = old.shape[0]
    more = () if before is None else tuple(before)
    return pl.pallas_call(
        functools.partial(embed_kernel, before is not None),
        in_specs=[SCALAR] + [WHOLE] * 4 + [ANY] * len(more),
        out_specs=[ANY, ANY],
        out_shape=[
            jax.ShapeDtypeStruct((depth, 2 * columns), f32),
            jax.ShapeDtypeStruct((rank, 2 * columns), f32),
        ],
        scratch_shapes=[
            pltpu.VMEM((depth, columns), f32),
            pltpu.VMEM((rank, columns), f32),
            pltpu.SemaphoreType.DMA((2 * CHUNKS,)),
        ],
        input_output_aliases={} if before is None else {5: 0, 6: 1},
        compiler_params=pltpu.CompilerParams(vmem_limit_bytes=8 * 2**20),
        cost_estimate=pl.CostEstimate(
            flops=6 * rank * depth * columns, bytes_accessed=8 * depth * columns, transcendentals=0
        ),
        name="embed_half",
    )(side, stack, coeff, moment, old, *more)


def low_lanes(rows):
    return lax.broadcasted_iota(jnp.int32, (rows, LANES), 1) < HALF


def turn(value):
    return pltpu.roll(value, HALF, 1)


def attn_tiles(in_ref, out_ref):
    whole = in_ref.shape[-1] // LANES
    tiles = [in_ref[0, :, k * LANES : (k + 1) * LANES].astype(f32) for k in range(whole)]
    last = in_ref[0, :, whole * LANES :].astype(f32)
    side = out_ref[0, :, LANES:].astype(f32)
    tiles.append(jnp.concatenate([last, side], axis=-1))
    tiles.append(out_ref[0, :, :LANES].astype(f32))
    return tiles


def unflatten_attn(flat, put, rows):
    pairs = rows // 2
    low = low_lanes(pairs)
    inner = [flat(j, pairs, 9) for j in range(9)]
    base = pairs * 9
    outer = [flat(base + j, pairs, 3) for j in range(3)]
    turned = [turn(inner[j]) for j in range(4, 9)]
    turned_out = [turn(outer[j]) for j in (1, 2)]
    for k in range(4):
        put(0, k, inner[k])
        put(1, k, jnp.where(low, turned[k], turned[k + 1]))
    put(0, 4, jnp.where(low, inner[4], turned_out[0]))
    put(1, 4, jnp.where(low, turned[4], outer[2]))
    put(0, 5, outer[0])
    put(1, 5, jnp.where(low, turned_out[0], turned_out[1]))


def flatten_attn(get, rows):
    pairs = rows // 2
    low = low_lanes(pairs)
    even = [get(0, k) for k in range(6)]
    odd = [get(1, k) for k in range(6)]
    turned = [turn(odd[k]) for k in range(5)]
    pieces = [(k, 9, even[k]) for k in range(4)]
    pieces.append((4, 9, jnp.where(low, even[4], turned[0])))
    for k in range(4):
        pieces.append((5 + k, 9, jnp.where(low, turned[k], turned[k + 1])))
    base = pairs * 9
    pieces.append((base, 3, even[5]))
    turned_out = turn(odd[5])
    pieces.append((base + 1, 3, jnp.where(low, turn(even[4]), turned_out)))
    pieces.append((base + 2, 3, jnp.where(low, turned_out, odd[4])))
    return pieces


def before_kernel(
    group_ref, in_ref, out_ref, up_ref, down_ref, old_ref, mom_ref, small_ref, small_old_ref,
    small_mom_ref, send_ref, mark_ref, wide_ref,
):
    mark_ref[...] = jnp.zeros(mark_ref.shape, f32)
    rows = up_ref.shape[1]
    mid = rows // 2
    block = rows + mid
    tiles = up_ref.shape[2] // LANES
    small = small_old_ref.shape[1]

    def flat(start, count, stride):
        at = pl.ds(start, count, stride=stride)
        return old_coef * old_ref[at, :] + mom_coef * mom_ref[at, :]

    def put(start, tile, value):
        send_ref[tile, pl.ds(block + start, rows // 2, stride=2), :] = value

    def put_small(other, own):
        own_terms = (
            old_coef * small_old_ref[...] + mom_coef * small_mom_ref[...] + local_coef * own
        )
        send_ref[:, 2 * block :, :] = jnp.zeros((tiles, 8, LANES), f32)
        for tile, value in enumerate((other, own_terms)):
            for row in range(pl.cdiv(small, LANES)):
                piece = value[:, row * LANES : (row + 1) * LANES]
                at = 2 * block + row
                send_ref[tile, at : at + 1, : piece.shape[1]] = piece

    @pl.when(group_ref[0] == 0)
    def _():
        unflatten_attn(flat, put, rows)
        for k, value in enumerate(attn_tiles(in_ref, out_ref)):
            send_ref[k, block : block + rows, :] += local_coef * value
        base = rows * tiles
        for k in range(tiles):
            columns = slice(k * LANES, (k + 1) * LANES)
            send_ref[k, :mid, :] = up_ref[0, mid:, columns].astype(f32)
            send_ref[k, mid:block, :] = down_ref[0, :, columns].astype(f32)
            send_ref[k, block + rows : 2 * block, :] = flat(base + k, mid, tiles) + (
                local_coef * up_ref[0, :mid, columns].astype(f32)
            )
        values = small_ref[...].astype(f32)
        put_small(values[:, small:], values[:, :small])

    @pl.when(group_ref[0] == 1)
    def _():
        for k, value in enumerate(attn_tiles(in_ref, out_ref)):
            send_ref[k, :rows, :] = value
        for k in range(tiles):
            columns = slice(k * LANES, (k + 1) * LANES)
            send_ref[k, rows:block, :] = up_ref[0, :mid, columns].astype(f32)
            send_ref[k, block : block + mid, :] = flat(k, mid, tiles) + (
                local_coef * up_ref[0, mid:, columns].astype(f32)
            )
        base = mid * tiles
        pairs = tiles * HALF
        low = low_lanes(pairs)
        first, second, third = (flat(base + j, pairs, 3) for j in range(3))
        turned, turned_more = turn(second), turn(third)
        even, odd = pl.ds(0, pairs, stride=2), pl.ds(1, pairs, stride=2)
        wide_ref[0, even, :] = first
        wide_ref[1, even, :] = second
        wide_ref[0, odd, :] = jnp.where(low, turned, turned_more)
        wide_ref[1, odd, :] = turned_more
        start = block + mid
        for k in range(tiles):
            columns = slice(k * LANES, (k + 1) * LANES)
            upper = wide_ref[0, columns, :].T
            lower = wide_ref[1, columns, :].T[:HALF]
            send_ref[k, start : start + LANES, :] = upper + (
                local_coef * down_ref[0, :LANES, columns].astype(f32)
            )
            send_ref[k, start + LANES : 2 * block, :] = lower + (
                local_coef * down_ref[0, LANES:, columns].astype(f32)
            )
        values = small_ref[...].astype(f32)
        put_small(values[:, :small], values[:, small:])


def after_kernel(
    group_ref, recv_ref, send_ref, in_ref, out_ref, up_ref, down_ref, old_ref, mom_ref, small_ref,
    small_old_ref, small_mom_ref, in_next_ref, out_next_ref, up_next_ref, down_next_ref, moved_ref,
    small_next_ref, small_moved_ref, sum_ref, wide_ref,
):
    rows = up_ref.shape[1]
    mid = rows // 2
    block = rows + mid
    tiles = up_ref.shape[2] // LANES
    small = small_old_ref.shape[1]

    def put_moved(start, stride, value):
        at = pl.ds(start, value.shape[0], stride=stride)
        moved_ref[at, :] = momentum_coef * mom_ref[at, :] + (old_ref[at, :] - 0.5 * value)

    def get(start, tile):
        return sum_ref[tile, pl.ds(start, rows // 2, stride=2), :]

    def put_attn(tile, value):
        whole = in_ref.shape[-1] // LANES
        if tile < whole:
            in_next_ref[:, tile * LANES : (tile + 1) * LANES] = value
        elif tile == whole:
            in_next_ref[:, tile * LANES :] = value[:, :HALF]
            out_next_ref[:, LANES:] = turn(value)[:, :HALF]
        else:
            out_next_ref[:, :LANES] = value

    def small_row(ref, tile):
        pieces = []
        for row in range(pl.cdiv(small, LANES)):
            at = 2 * block + row
            pieces.append(ref[tile, at : at + 1, : min(LANES, small - row * LANES)])
        return jnp.concatenate(pieces, axis=1)

    def put_small(other, own, first):
        theirs = small_row(recv_ref, 0)
        mine = small_row(send_ref, 1) + local_coef * theirs
        rest = small_row(recv_ref, 1) + local_coef * other
        both = [mine, rest] if first else [rest, mine]
        small_next_ref[...] = jnp.concatenate(both, axis=1)
        small_moved_ref[...] = momentum_coef * small_mom_ref[...] + (
            small_old_ref[...] - 0.5 * (own + theirs)
        )

    @pl.when(group_ref[0] == 0)
    def _():
        for k, value in enumerate(attn_tiles(in_ref, out_ref)):
            theirs = recv_ref[k, :rows, :]
            put_attn(k, send_ref[k, block : block + rows, :] + local_coef * theirs)
            sum_ref[k, :, :] = value + theirs
        for start, stride, value in flatten_attn(get, rows):
            put_moved(start, stride, value)
        base = rows * tiles
        for k in range(tiles):
            columns = slice(k * LANES, (k + 1) * LANES)
            theirs = recv_ref[k, rows:block, :]
            up_next_ref[:mid, columns] = (
                send_ref[k, block + rows : 2 * block, :] + local_coef * theirs
            )
            put_moved(base + k, tiles, up_ref[0, :mid, columns].astype(f32) + theirs)
            up_next_ref[mid:, columns] = recv_ref[k, block : block + mid, :] + (
                local_coef * up_ref[0, mid:, columns].astype(f32)
            )
            down_next_ref[:, columns] = recv_ref[k, block + mid : 2 * block, :] + (
                local_coef * down_ref[0, :, columns].astype(f32)
            )
        values = small_ref[...].astype(f32)
        put_small(values[:, small:], values[:, :small], True)

    @pl.when(group_ref[0] == 1)
    def _():
        for k, value in enumerate(attn_tiles(in_ref, out_ref)):
            put_attn(k, recv_ref[k, block : block + rows, :] + local_coef * value)
        for k in range(tiles):
            columns = slice(k * LANES, (k + 1) * LANES)
            up_next_ref[:mid, columns] = recv_ref[k, block + rows : 2 * block, :] + (
                local_coef * up_ref[0, :mid, columns].astype(f32)
            )
            theirs = recv_ref[k, :mid, :]
            up_next_ref[mid:, columns] = send_ref[k, block : block + mid, :] + local_coef * theirs
            put_moved(k, tiles, up_ref[0, mid:, columns].astype(f32) + theirs)
            theirs = recv_ref[k, mid:block, :]
            down_next_ref[:, columns] = (
                send_ref[k, block + mid : 2 * block, :] + local_coef * theirs
            )
            total = down_ref[0, :, columns].astype(f32) + theirs
            wide_ref[0, columns, :] = total[:LANES].T
            lower = jnp.concatenate([total[LANES:], total[LANES:]], axis=0)
            wide_ref[1, columns, :] = lower.T
        base = mid * tiles
        pairs = tiles * HALF
        low = low_lanes(pairs)
        even, odd = pl.ds(0, pairs, stride=2), pl.ds(1, pairs, stride=2)
        odd_first = turn(wide_ref[0, odd, :])
        put_moved(base, 3, wide_ref[0, even, :])
        put_moved(base + 1, 3, jnp.where(low, wide_ref[1, even, :], odd_first))
        put_moved(base + 2, 3, jnp.where(low, odd_first, wide_ref[1, odd, :]))
        values = small_ref[...].astype(f32)
        put_small(values[:, :small], values[:, small:], False)


def dense_before(group, operands):
    _, rows, width = operands[2].shape
    return pl.pallas_call(
        before_kernel,
        in_specs=[SCALAR] + [WHOLE] * 9,
        out_specs=[WHOLE] * 2,
        out_shape=[
            jax.ShapeDtypeStruct((width // LANES, 3 * rows + 8, LANES), f32),
            jax.ShapeDtypeStruct((8, LANES), f32),
        ],
        scratch_shapes=[pltpu.VMEM((2, width, LANES), f32)],
        compiler_params=pltpu.CompilerParams(vmem_limit_bytes=20 * 2**20),
        cost_estimate=pl.CostEstimate(
            flops=60000 * rows * width, bytes_accessed=30 * rows * width, transcendentals=0
        ),
        name="dense_before",
    )(group, *operands)


def dense_after(group, received, sent, operands):
    _, rows, width = operands[2].shape
    outs = [matrix.shape[1:] for matrix in operands[:4]]
    outs += [operands[4].shape, operands[6].shape, operands[7].shape]
    return pl.pallas_call(
        after_kernel,
        in_specs=[SCALAR] + [WHOLE] * 11,
        out_specs=[WHOLE] * 7,
        out_shape=[jax.ShapeDtypeStruct(shape, f32) for shape in outs],
        scratch_shapes=[
            pltpu.VMEM((width // LANES, rows, LANES), f32),
            pltpu.VMEM((2, width, LANES), f32),
        ],
        compiler_params=pltpu.CompilerParams(vmem_limit_bytes=24 * 2**20),
        cost_estimate=pl.CostEstimate(
            flops=60000 * rows * width, bytes_accessed=40 * rows * width, transcendentals=0
        ),
        name="dense_after",
    )(group, received, sent, *operands)


def paired(
    attn_in_local,
    attn_out_local,
    ffn_in_local,
    ffn_out_local,
    small_local,
    dense_old,
    dense_momentum,
    small_old,
    small_momentum,
    embed_local,
    embed_old,
    basis,
    coeff_momentum,
):
    position = lax.axis_index("group")
    group = position.astype(jnp.int32).reshape(1)
    swap = [(0, 1), (1, 0)]
    chips = lax.axis_size("shard")

    def turned(chip):
        return (chip ^ (chip >> 1)) & 1

    first, second = (
        [
            (core * chips + chip, (1 - core) * chips + (chip ^ (1 + (core ^ turned(chip) ^ late))))
            for core in range(2)
            for chip in range(chips)
        ]
        for late in range(2)
    )
    side = group ^ turned(lax.axis_index("shard").astype(jnp.int32))
    axes = ("group", "shard")

    basis_t = basis.T
    embed = (basis_t, embed_local[0], embed_old, coeff_momentum)
    theirs, old_rest = partial_coeff(side, *embed, True)
    theirs = lax.ppermute(theirs, "group", swap)
    mine, old_own, moment, stack = partial_coeff(side, *embed, False)
    total = mine + theirs

    operands = (
        attn_in_local,
        attn_out_local,
        ffn_in_local,
        jnp.swapaxes(ffn_out_local, 1, 2),
        dense_old.reshape(-1, LANES),
        dense_momentum.reshape(-1, LANES),
        small_local,
        small_old[None, :],
        small_momentum[None, :],
    )
    total, group_later = lax.optimization_barrier((total, group))
    moving = lax.ppermute(total, axes, first)
    sent, mark = dense_before(group_later, operands)
    received = lax.ppermute(sent, "group", swap)
    moving, mark = lax.optimization_barrier((moving, mark))
    total = total + moving
    moving = lax.ppermute(total, axes, second)
    dense = list(dense_after(group, received, sent, operands))
    moving, dense[-1] = lax.optimization_barrier((moving, dense[-1]))

    own = 0.5 * (total + moving)
    rest = lax.ppermute(own, "group", swap)
    done = embed_half(side, stack, own, moment, old_own, None)
    embed_next, coeff_moved = embed_half(side, stack, rest, moment, old_rest, done)

    attn_in_next, attn_out_next, ffn_in_next, ffn_out_next, moved, small_next, small_moved = dense
    return (
        attn_in_next,
        attn_out_next,
        ffn_in_next,
        ffn_out_next.T,
        moved.reshape(dense_old.shape),
        small_next[0],
        small_moved[0],
        embed_next,
        coeff_moved,
    )


def is_paired(mesh, shapes):
    attn_in, attn_out, ffn_in, ffn_out = (shape[1:] for shape in shapes[:4])
    rows = ffn_in[0]
    return (
        mesh.shape["group"] == 2
        and mesh.shape["shard"] == 4
        and attn_in == (rows, 4 * LANES + HALF)
        and attn_out == (rows, LANES + HALF)
        and ffn_in[1] == 6 * LANES
        and ffn_out == (6 * LANES, rows)
        and rows == LANES + HALF
        and shapes[7][0] <= 8 * LANES
        and shapes[10][1] % (8 * LANES) == 0
    )


def solution(mesh):
    placed = (
        P("group", "shard", "tensor"),
        P("group", "shard", "tensor"),
        P("group", "shard", "tensor"),
        P("group", "shard", "tensor"),
        P("group", None),
        P(("shard", "tensor"), "group"),
        P(("shard", "tensor"), "group"),
        P("group"),
        P("group"),
        P("group", "shard", "tensor"),
        P("shard", "tensor"),
        P("shard", None),
        P(None, "tensor"),
    )

    def shards(*args):
        plan = paired if is_paired(mesh, [arg.shape for arg in args]) else general
        return plan(*args)

    return jax.shard_map(
        shards,
        mesh=mesh,
        in_specs=placed,
        out_specs=(
            P("shard", "tensor"),
            P("shard", "tensor"),
            P("shard", "tensor"),
            P("shard", "tensor"),
            P(("shard", "tensor"), "group"),
            P(),
            P("group"),
            P("shard", "tensor"),
            P(None, "tensor"),
        ),
        check_vma=False,
    )
```

```python
import functools

import jax
import jax.numpy as jnp
from jax import lax
from jax.experimental import pallas as pl
from jax.experimental.pallas import tpu as pltpu
from jax.sharding import PartitionSpec as P

momentum_coef = 0.5
outer_rate = 0.7

f32 = jnp.float32
bf16 = jnp.bfloat16
LANES = 128
HALF = LANES // 2


def nesterov(old_value, momentum, delta):
    moved = momentum_coef * momentum + delta
    return (old_value - outer_rate * (delta + momentum_coef * moved), moved)


def general(
    attn_in_local,
    attn_out_local,
    ffn_in_local,
    ffn_out_local,
    small_local,
    dense_old,
    dense_momentum,
    small_old,
    small_momentum,
    embed_local,
    embed_old,
    basis,
    coeff_momentum,
):
    groups = lax.axis_size("group")
    matrices = (attn_in_local, attn_out_local, ffn_in_local, ffn_out_local)
    local_terms = jnp.concatenate([matrix[0].reshape(-1) for matrix in matrices]).astype(f32)
    small_terms = small_local[0].astype(f32)
    old_flat = dense_old[0]
    momentum_flat = dense_momentum[0]
    dense_part, small_part = (
        lax.psum_scatter(local_terms, "group", scatter_dimension=0, tiled=True),
        lax.psum_scatter(small_terms, "group", scatter_dimension=0, tiled=True),
    )
    dense_new, dense_moved = nesterov(old_flat, momentum_flat, old_flat - dense_part / groups)
    small_new, small_moved = nesterov(small_old, small_momentum, small_old - small_part / groups)
    full_flat, small_next = (
        lax.all_gather(dense_new, "group", axis=0, tiled=True),
        lax.all_gather(small_new, "group", axis=0, tiled=True),
    )
    results = []
    offset = 0
    for matrix in matrices:
        block_size = matrix.shape[1] * matrix.shape[2]
        results.append(
            full_flat[offset : offset + block_size].reshape(matrix.shape[1], matrix.shape[2])
        )
        offset = offset + block_size
    difference = embed_old - embed_local[0].astype(f32)
    partial_coeff = lax.dot_general(
        basis,
        difference,
        (((0,), (0,)), ((), ())),
        precision=lax.Precision.HIGHEST,
        preferred_element_type=f32,
    )
    coeff = lax.psum(partial_coeff, ("group", "shard")) / groups
    coeff_moved = momentum_coef * coeff_momentum + coeff
    update = coeff + momentum_coef * coeff_moved
    embed_next = embed_old - outer_rate * jnp.dot(
        basis, update, precision=lax.Precision.HIGHEST, preferred_element_type=f32
    )
    return (
        results[0],
        results[1],
        results[2],
        results[3],
        dense_moved[None, :],
        small_next,
        small_moved,
        embed_next,
        coeff_moved,
    )


local_coef = outer_rate * (1 + momentum_coef) / 2
old_coef = 1 - outer_rate * (1 + momentum_coef)
mom_coef = -outer_rate * momentum_coef * momentum_coef


def split(value):
    high = value.astype(bf16)
    return high, (value - high.astype(f32)).astype(bf16)


CHUNKS = 2
WHOLE = pl.BlockSpec(memory_space=pltpu.VMEM)
ANY = pl.BlockSpec(memory_space=pl.ANY)


def in_hbm(arrays):
    return [pltpu.with_memory_space_constraint(array, pltpu.HBM) for array in arrays]


def turned(chip):
    return (chip ^ (chip >> 1)) & 1


def side_start(other, columns):
    side = lax.axis_index("group") ^ turned(lax.axis_index("shard"))
    return (1 - side if other else side) * columns


def product(basis, local, old):
    rank = basis.shape[0]
    high, low = split(basis)
    diff_high, diff_low = split(old - local.astype(f32))
    first = jnp.dot(
        jnp.concatenate([high, low], axis=0), diff_high, preferred_element_type=f32
    )
    return first[:rank] + first[rank:] + jnp.dot(high, diff_low, preferred_element_type=f32)


def partial_kernel(other, basis_hbm, local_hbm, old_hbm, out_ref, old_ref, *refs):
    basis_ref, local_ref, sems = refs[-3:]
    columns = out_ref.shape[1]
    block = columns // CHUNKS
    start = side_start(other, columns)
    copies = [pltpu.make_async_copy(basis_hbm, basis_ref, sems.at[0])]
    for k in range(CHUNKS):
        there = pl.ds(pl.multiple_of(start + k * block, block), block)
        here = pl.ds(k * block, block)
        for source, target in ((old_hbm, old_ref), (local_hbm, local_ref)):
            at = sems.at[len(copies)]
            copies.append(pltpu.make_async_copy(source.at[:, there], target.at[:, here], at))
    for copy in copies:
        copy.start()
    copies[0].wait()
    basis = basis_ref[...]
    for k in range(CHUNKS):
        copies[1 + 2 * k].wait()
        copies[2 + 2 * k].wait()
        here = slice(k * block, (k + 1) * block)
        out_ref[:, here] = product(basis, local_ref[:, here], old_ref[:, here])
    if not other:
        high = basis.astype(bf16).astype(f32)
        refs[0][...] = jnp.concatenate([high, basis - high, high], axis=0).T.astype(bf16)


def partial_coeff(basis_t, local, old, other):
    rank, depth = basis_t.shape
    columns = old.shape[1] // 2
    shapes = [((rank, columns), f32), ((depth, columns), f32)]
    if not other:
        shapes.append(((depth, 3 * rank), bf16))
    return pl.pallas_call(
        functools.partial(partial_kernel, other),
        in_specs=[ANY] * 3,
        out_specs=[WHOLE] * len(shapes),
        out_shape=[jax.ShapeDtypeStruct(*shape) for shape in shapes],
        scratch_shapes=[
            pltpu.VMEM((rank, depth), f32),
            pltpu.VMEM((depth, columns), bf16),
            pltpu.SemaphoreType.DMA((1 + 2 * CHUNKS,)),
        ],
        compiler_params=pltpu.CompilerParams(vmem_limit_bytes=6 * 2**20),
        cost_estimate=pl.CostEstimate(
            flops=6 * rank * depth * columns, bytes_accessed=6 * depth * columns, transcendentals=0
        ),
        name="partial_coeff",
    )(*in_hbm((basis_t, local, old)))


def add_kernel(scale, first_ref, second_ref, out_ref):
    out_ref[...] = scale * (first_ref[...] + second_ref[...])


def add(first, second, scale=1.0):
    return pl.pallas_call(
        functools.partial(add_kernel, scale),
        in_specs=[WHOLE] * 2,
        out_specs=WHOLE,
        out_shape=jax.ShapeDtypeStruct(first.shape, f32),
        compiler_params=pltpu.CompilerParams(vmem_limit_bytes=2 * 2**20),
        cost_estimate=pl.CostEstimate(flops=10**11, bytes_accessed=0, transcendentals=0),
        name="add",
    )(first, second)


def embed_kernel(other, stack_ref, coeff_ref, moment_ref, old_ref, *refs):
    embed_hbm, moved_hbm, embed_ref, moved_ref, sems = refs[-5:]
    columns = coeff_ref.shape[1]
    block = columns // CHUNKS
    start = side_start(other, columns)
    copies = []
    for k in range(CHUNKS):
        here = slice(k * block, (k + 1) * block)
        there = pl.ds(pl.multiple_of(start + k * block, block), block)
        coeff = coeff_ref[:, here]
        moved = momentum_coef * moment_ref[:, there] + coeff
        moved_ref[:, here] = moved
        up_high, up_low = split(coeff + momentum_coef * moved)
        product = jnp.dot(
            stack_ref[...],
            jnp.concatenate([up_high, up_high, up_low], axis=0),
            preferred_element_type=f32,
        )
        embed_ref[:, here] = old_ref[:, here] - outer_rate * product
        target = pl.ds(k * block, block)
        for source_ref, target_hbm, at in ((moved_ref, moved_hbm, 0), (embed_ref, embed_hbm, 1)):
            copy = pltpu.make_async_copy(
                source_ref.at[:, target], target_hbm.at[:, there], sems.at[2 * k + at]
            )
            copy.start()
            copies.append(copy)
    for copy in copies:
        copy.wait()


def embed_half(stack, coeff, moment, old, before):
    rank, columns = coeff.shape
    depth = old.shape[0]
    more = () if before is None else tuple(before)
    return pl.pallas_call(
        functools.partial(embed_kernel, before is not None),
        in_specs=[WHOLE] * 4 + [ANY] * len(more),
        out_specs=[ANY, ANY],
        out_shape=[
            jax.ShapeDtypeStruct((depth, 2 * columns), f32),
            jax.ShapeDtypeStruct((rank, 2 * columns), f32),
        ],
        scratch_shapes=[
            pltpu.VMEM((depth, columns), f32),
            pltpu.VMEM((rank, columns), f32),
            pltpu.SemaphoreType.DMA((2 * CHUNKS,)),
        ],
        input_output_aliases={} if before is None else {4: 0, 5: 1},
        compiler_params=pltpu.CompilerParams(vmem_limit_bytes=8 * 2**20),
        cost_estimate=pl.CostEstimate(
            flops=6 * rank * depth * columns, bytes_accessed=8 * depth * columns, transcendentals=0
        ),
        name="embed_half",
    )(stack, coeff, moment, old, *more)


def low_lanes(rows):
    return lax.broadcasted_iota(jnp.int32, (rows, LANES), 1) < HALF


def turn(value):
    return pltpu.roll(value, HALF, 1)


def attn_tiles(in_ref, out_ref):
    whole = in_ref.shape[-1] // LANES
    tiles = [in_ref[0, :, k * LANES : (k + 1) * LANES].astype(f32) for k in range(whole)]
    last = in_ref[0, :, whole * LANES :].astype(f32)
    side = out_ref[0, :, LANES:].astype(f32)
    tiles.append(jnp.concatenate([last, side], axis=-1))
    tiles.append(out_ref[0, :, :LANES].astype(f32))
    return tiles


def unflatten_attn(flat, put, rows):
    pairs = rows // 2
    low = low_lanes(pairs)
    inner = [flat(j, pairs, 9) for j in range(9)]
    base = pairs * 9
    outer = [flat(base + j, pairs, 3) for j in range(3)]
    turned = [turn(inner[j]) for j in range(4, 9)]
    turned_out = [turn(outer[j]) for j in (1, 2)]
    for k in range(4):
        put(0, k, inner[k])
        put(1, k, jnp.where(low, turned[k], turned[k + 1]))
    put(0, 4, jnp.where(low, inner[4], turned_out[0]))
    put(1, 4, jnp.where(low, turned[4], outer[2]))
    put(0, 5, outer[0])
    put(1, 5, jnp.where(low, turned_out[0], turned_out[1]))


def flatten_attn(get, rows):
    pairs = rows // 2
    low = low_lanes(pairs)
    even = [get(0, k) for k in range(6)]
    odd = [get(1, k) for k in range(6)]
    turned = [turn(odd[k]) for k in range(5)]
    pieces = [(k, 9, even[k]) for k in range(4)]
    pieces.append((4, 9, jnp.where(low, even[4], turned[0])))
    for k in range(4):
        pieces.append((5 + k, 9, jnp.where(low, turned[k], turned[k + 1])))
    base = pairs * 9
    pieces.append((base, 3, even[5]))
    turned_out = turn(odd[5])
    pieces.append((base + 1, 3, jnp.where(low, turn(even[4]), turned_out)))
    pieces.append((base + 2, 3, jnp.where(low, turned_out, odd[4])))
    return pieces


def before_kernel(order_ref, *refs):
    del order_ref
    count = len(refs) // 2 - 1
    sources, send_ref, kept, (wide_ref, sems) = (
        refs[:count], refs[count], refs[count + 1 : -2], refs[-2:]
    )
    copies = [
        pltpu.make_async_copy(source, target, sems.at[k])
        for k, (source, target) in enumerate(zip(sources, kept))
    ]
    for copy in copies:
        copy.start()
    for copy in copies:
        copy.wait()
    in_ref, out_ref, up_ref, down_ref, old_ref, mom_ref, small_ref, small_old_ref, small_mom_ref = (
        kept[:9]
    )
    group = lax.axis_index("group")
    rows = up_ref.shape[1]
    mid = rows // 2
    block = rows + mid
    tiles = up_ref.shape[2] // LANES
    small = small_old_ref.shape[1]

    def flat(start, count, stride):
        at = pl.ds(start, count, stride=stride)
        return old_coef * old_ref[at, :] + mom_coef * mom_ref[at, :]

    def put(start, tile, value):
        send_ref[tile, pl.ds(block + start, rows // 2, stride=2), :] = value

    def put_small(other, own):
        own_terms = (
            old_coef * small_old_ref[...] + mom_coef * small_mom_ref[...] + local_coef * own
        )
        send_ref[:, 2 * block :, :] = jnp.zeros((tiles, 8, LANES), f32)
        for tile, value in enumerate((other, own_terms)):
            for row in range(pl.cdiv(small, LANES)):
                piece = value[:, row * LANES : (row + 1) * LANES]
                at = 2 * block + row
                send_ref[tile, at : at + 1, : piece.shape[1]] = piece

    @pl.when(group == 0)
    def _():
        unflatten_attn(flat, put, rows)
        for k, value in enumerate(attn_tiles(in_ref, out_ref)):
            send_ref[k, block : block + rows, :] += local_coef * value
        base = rows * tiles
        for k in range(tiles):
            columns = slice(k * LANES, (k + 1) * LANES)
            send_ref[k, :mid, :] = up_ref[0, mid:, columns].astype(f32)
            send_ref[k, mid:block, :] = down_ref[0, :, columns].astype(f32)
            send_ref[k, block + rows : 2 * block, :] = flat(base + k, mid, tiles) + (
                local_coef * up_ref[0, :mid, columns].astype(f32)
            )
        values = small_ref[...].astype(f32)
        put_small(values[:, small:], values[:, :small])

    @pl.when(group == 1)
    def _():
        for k, value in enumerate(attn_tiles(in_ref, out_ref)):
            send_ref[k, :rows, :] = value
        for k in range(tiles):
            columns = slice(k * LANES, (k + 1) * LANES)
            send_ref[k, rows:block, :] = up_ref[0, :mid, columns].astype(f32)
            send_ref[k, block : block + mid, :] = flat(k, mid, tiles) + (
                local_coef * up_ref[0, mid:, columns].astype(f32)
            )
        base = mid * tiles
        pairs = tiles * HALF
        low = low_lanes(pairs)
        first, second, third = (flat(base + j, pairs, 3) for j in range(3))
        turned, turned_more = turn(second), turn(third)
        even, odd = pl.ds(0, pairs, stride=2), pl.ds(1, pairs, stride=2)
        wide_ref[0, even, :] = first
        wide_ref[1, even, :] = second
        wide_ref[0, odd, :] = jnp.where(low, turned, turned_more)
        wide_ref[1, odd, :] = turned_more
        start = block + mid
        for k in range(tiles):
            columns = slice(k * LANES, (k + 1) * LANES)
            upper = wide_ref[0, columns, :].T
            lower = wide_ref[1, columns, :].T[:HALF]
            send_ref[k, start : start + LANES, :] = upper + (
                local_coef * down_ref[0, :LANES, columns].astype(f32)
            )
            send_ref[k, start + LANES : 2 * block, :] = lower + (
                local_coef * down_ref[0, LANES:, columns].astype(f32)
            )
        values = small_ref[...].astype(f32)
        put_small(values[:, :small], values[:, small:])


def after_kernel(
    recv_ref, send_ref, in_ref, out_ref, up_ref, down_ref, old_ref, mom_ref, small_ref,
    small_old_ref, small_mom_ref, in_next_ref, out_next_ref, up_next_ref, down_next_ref, moved_ref,
    small_next_ref, small_moved_ref, sum_ref, wide_ref,
):
    rows = up_ref.shape[1]
    mid = rows // 2
    block = rows + mid
    tiles = up_ref.shape[2] // LANES
    small = small_old_ref.shape[1]
    group = lax.axis_index("group")

    def put_moved(start, stride, value):
        at = pl.ds(start, value.shape[0], stride=stride)
        moved_ref[at, :] = momentum_coef * mom_ref[at, :] + (old_ref[at, :] - 0.5 * value)

    def get(start, tile):
        return sum_ref[tile, pl.ds(start, rows // 2, stride=2), :]

    def put_attn(tile, value):
        whole = in_ref.shape[-1] // LANES
        if tile < whole:
            in_next_ref[:, tile * LANES : (tile + 1) * LANES] = value
        elif tile == whole:
            in_next_ref[:, tile * LANES :] = value[:, :HALF]
            out_next_ref[:, LANES:] = turn(value)[:, :HALF]
        else:
            out_next_ref[:, :LANES] = value

    def small_row(ref, tile):
        pieces = []
        for row in range(pl.cdiv(small, LANES)):
            at = 2 * block + row
            pieces.append(ref[tile, at : at + 1, : min(LANES, small - row * LANES)])
        return jnp.concatenate(pieces, axis=1)

    def put_small(other, own, first):
        theirs = small_row(recv_ref, 0)
        mine = small_row(send_ref, 1) + local_coef * theirs
        rest = small_row(recv_ref, 1) + local_coef * other
        both = [mine, rest] if first else [rest, mine]
        small_next_ref[...] = jnp.concatenate(both, axis=1).reshape(-1)
        small_moved_ref[...] = momentum_coef * small_mom_ref[...] + (
            small_old_ref[...] - 0.5 * (own + theirs)
        )

    @pl.when(group == 0)
    def _():
        for k, value in enumerate(attn_tiles(in_ref, out_ref)):
            theirs = recv_ref[k, :rows, :]
            put_attn(k, send_ref[k, block : block + rows, :] + local_coef * theirs)
            sum_ref[k, :, :] = value + theirs
        for start, stride, value in flatten_attn(get, rows):
            put_moved(start, stride, value)
        base = rows * tiles
        for k in range(tiles):
            columns = slice(k * LANES, (k + 1) * LANES)
            theirs = recv_ref[k, rows:block, :]
            up_next_ref[:mid, columns] = (
                send_ref[k, block + rows : 2 * block, :] + local_coef * theirs
            )
            put_moved(base + k, tiles, up_ref[0, :mid, columns].astype(f32) + theirs)
            up_next_ref[mid:, columns] = recv_ref[k, block : block + mid, :] + (
                local_coef * up_ref[0, mid:, columns].astype(f32)
            )
            down_next_ref[:, columns] = recv_ref[k, block + mid : 2 * block, :] + (
                local_coef * down_ref[0, :, columns].astype(f32)
            )
        values = small_ref[...].astype(f32)
        put_small(values[:, small:], values[:, :small], True)

    @pl.when(group == 1)
    def _():
        for k, value in enumerate(attn_tiles(in_ref, out_ref)):
            put_attn(k, recv_ref[k, block : block + rows, :] + local_coef * value)
        for k in range(tiles):
            columns = slice(k * LANES, (k + 1) * LANES)
            up_next_ref[:mid, columns] = recv_ref[k, block + rows : 2 * block, :] + (
                local_coef * up_ref[0, :mid, columns].astype(f32)
            )
            theirs = recv_ref[k, :mid, :]
            up_next_ref[mid:, columns] = send_ref[k, block : block + mid, :] + local_coef * theirs
            put_moved(k, tiles, up_ref[0, mid:, columns].astype(f32) + theirs)
            theirs = recv_ref[k, mid:block, :]
            down_next_ref[:, columns] = (
                send_ref[k, block + mid : 2 * block, :] + local_coef * theirs
            )
            total = down_ref[0, :, columns].astype(f32) + theirs
            wide_ref[0, columns, :] = total[:LANES].T
            lower = jnp.concatenate([total[LANES:], total[LANES:]], axis=0)
            wide_ref[1, columns, :] = lower.T
        base = mid * tiles
        pairs = tiles * HALF
        low = low_lanes(pairs)
        even, odd = pl.ds(0, pairs, stride=2), pl.ds(1, pairs, stride=2)
        odd_first = turn(wide_ref[0, odd, :])
        put_moved(base, 3, wide_ref[0, even, :])
        put_moved(base + 1, 3, jnp.where(low, wide_ref[1, even, :], odd_first))
        put_moved(base + 2, 3, jnp.where(low, odd_first, wide_ref[1, odd, :]))
        values = small_ref[...].astype(f32)
        put_small(values[:, :small], values[:, small:], False)


def dense_before(order, operands):
    _, rows, width = operands[2].shape
    count = len(operands)
    return pl.pallas_call(
        before_kernel,
        in_specs=[ANY] * (1 + count),
        out_specs=[WHOLE] * (1 + count),
        out_shape=[jax.ShapeDtypeStruct((width // LANES, 3 * rows + 8, LANES), f32)]
        + [jax.ShapeDtypeStruct(array.shape, array.dtype) for array in operands],
        scratch_shapes=[pltpu.VMEM((2, width, LANES), f32), pltpu.SemaphoreType.DMA((count,))],
        compiler_params=pltpu.CompilerParams(vmem_limit_bytes=20 * 2**20),
        cost_estimate=pl.CostEstimate(
            flops=60000 * rows * width, bytes_accessed=30 * rows * width, transcendentals=0
        ),
        name="dense_before",
    )(order, *in_hbm(operands))


def dense_after(received, sent, operands):
    _, rows, width = operands[2].shape
    outs = [matrix.shape[1:] for matrix in operands[:4]]
    outs += [operands[4].shape, operands[6].shape[1:], operands[7].shape]
    return pl.pallas_call(
        after_kernel,
        in_specs=[WHOLE] * 11,
        out_specs=[WHOLE] * 7,
        out_shape=[jax.ShapeDtypeStruct(shape, f32) for shape in outs],
        scratch_shapes=[
            pltpu.VMEM((width // LANES, rows, LANES), f32),
            pltpu.VMEM((2, width, LANES), f32),
        ],
        compiler_params=pltpu.CompilerParams(vmem_limit_bytes=24 * 2**20),
        cost_estimate=pl.CostEstimate(
            flops=60000 * rows * width, bytes_accessed=40 * rows * width, transcendentals=0
        ),
        name="dense_after",
    )(received, sent, *operands)


def paired(
    attn_in_local,
    attn_out_local,
    ffn_in_local,
    ffn_out_local,
    small_local,
    dense_old,
    dense_momentum,
    small_old,
    small_momentum,
    embed_local,
    embed_old,
    basis,
    coeff_momentum,
):
    swap = [(0, 1), (1, 0)]
    chips = lax.axis_size("shard")

    first, second = (
        [
            (core * chips + chip, (1 - core) * chips + (chip ^ (1 + (core ^ turned(chip) ^ late))))
            for core in range(2)
            for chip in range(chips)
        ]
        for late in range(2)
    )
    axes = ("group", "shard")

    embed = (basis.T, embed_local[0], embed_old)
    theirs, old_rest = partial_coeff(*embed, True)
    theirs = lax.ppermute(theirs, "group", swap)
    mine, old_own, stack = partial_coeff(*embed, False)

    operands = (
        attn_in_local,
        attn_out_local,
        ffn_in_local,
        jnp.swapaxes(ffn_out_local, 1, 2),
        dense_old.reshape(-1, LANES),
        dense_momentum.reshape(-1, LANES),
        small_local,
        small_old[None, :],
        small_momentum[None, :],
        coeff_momentum,
    )
    total = add(mine, theirs)
    moving = lax.ppermute(total, axes, first)
    sent, *kept, moment = dense_before(total, operands)
    received = lax.ppermute(sent, "group", swap)
    total = add(total, moving)
    moving = lax.ppermute(total, axes, second)
    dense = list(dense_after(received, sent, kept))
    moving, dense[-1] = lax.optimization_barrier((moving, dense[-1]))

    own = add(total, moving, 0.5)
    rest = lax.ppermute(own, "group", swap)
    done = embed_half(stack, own, moment, old_own, None)
    embed_next, coeff_moved = embed_half(stack, rest, moment, old_rest, done)

    attn_in_next, attn_out_next, ffn_in_next, ffn_out_next, moved, small_next, small_moved = dense
    return (
        attn_in_next,
        attn_out_next,
        ffn_in_next,
        ffn_out_next.T,
        moved.reshape(dense_old.shape),
        small_next,
        small_moved[0],
        embed_next,
        coeff_moved,
    )


def is_paired(mesh, shapes):
    attn_in, attn_out, ffn_in, ffn_out = (shape[1:] for shape in shapes[:4])
    rows = ffn_in[0]
    return (
        mesh.shape["group"] == 2
        and mesh.shape["shard"] == 4
        and attn_in == (rows, 4 * LANES + HALF)
        and attn_out == (rows, LANES + HALF)
        and ffn_in[1] == 6 * LANES
        and ffn_out == (6 * LANES, rows)
        and rows == LANES + HALF
        and shapes[7][0] <= 8 * LANES
        and shapes[10][1] % (8 * LANES) == 0
    )


def solution(mesh):
    placed = (
        P("group", "shard", "tensor"),
        P("group", "shard", "tensor"),
        P("group", "shard", "tensor"),
        P("group", "shard", "tensor"),
        P("group", None),
        P(("shard", "tensor"), "group"),
        P(("shard", "tensor"), "group"),
        P("group"),
        P("group"),
        P("group", "shard", "tensor"),
        P("shard", "tensor"),
        P("shard", None),
        P(None, "tensor"),
    )

    def shards(*args):
        plan = paired if is_paired(mesh, [arg.shape for arg in args]) else general
        return plan(*args)

    return jax.shard_map(
        shards,
        mesh=mesh,
        in_specs=placed,
        out_specs=(
            P("shard", "tensor"),
            P("shard", "tensor"),
            P("shard", "tensor"),
            P("shard", "tensor"),
            P(("shard", "tensor"), "group"),
            P(),
            P("group"),
            P("shard", "tensor"),
            P(None, "tensor"),
        ),
        check_vma=False,
    )
```

```python
import functools

import jax
import jax.numpy as jnp
from jax import lax
from jax.experimental import pallas as pl
from jax.experimental.pallas import tpu as pltpu
from jax.sharding import PartitionSpec as P

momentum_coef = 0.5
outer_rate = 0.7

f32 = jnp.float32
bf16 = jnp.bfloat16
LANES = 128
HALF = LANES // 2


def nesterov(old_value, momentum, delta):
    moved = momentum_coef * momentum + delta
    return (old_value - outer_rate * (delta + momentum_coef * moved), moved)


def general(
    attn_in_local,
    attn_out_local,
    ffn_in_local,
    ffn_out_local,
    small_local,
    dense_old,
    dense_momentum,
    small_old,
    small_momentum,
    embed_local,
    embed_old,
    basis,
    coeff_momentum,
):
    groups = lax.axis_size("group")
    matrices = (attn_in_local, attn_out_local, ffn_in_local, ffn_out_local)
    local_terms = jnp.concatenate([matrix[0].reshape(-1) for matrix in matrices]).astype(f32)
    small_terms = small_local[0].astype(f32)
    old_flat = dense_old[0]
    momentum_flat = dense_momentum[0]
    dense_part, small_part = (
        lax.psum_scatter(local_terms, "group", scatter_dimension=0, tiled=True),
        lax.psum_scatter(small_terms, "group", scatter_dimension=0, tiled=True),
    )
    dense_new, dense_moved = nesterov(old_flat, momentum_flat, old_flat - dense_part / groups)
    small_new, small_moved = nesterov(small_old, small_momentum, small_old - small_part / groups)
    full_flat, small_next = (
        lax.all_gather(dense_new, "group", axis=0, tiled=True),
        lax.all_gather(small_new, "group", axis=0, tiled=True),
    )
    results = []
    offset = 0
    for matrix in matrices:
        block_size = matrix.shape[1] * matrix.shape[2]
        results.append(
            full_flat[offset : offset + block_size].reshape(matrix.shape[1], matrix.shape[2])
        )
        offset = offset + block_size
    difference = embed_old - embed_local[0].astype(f32)
    partial_coeff = lax.dot_general(
        basis,
        difference,
        (((0,), (0,)), ((), ())),
        precision=lax.Precision.HIGHEST,
        preferred_element_type=f32,
    )
    coeff = lax.psum(partial_coeff, ("group", "shard")) / groups
    coeff_moved = momentum_coef * coeff_momentum + coeff
    update = coeff + momentum_coef * coeff_moved
    embed_next = embed_old - outer_rate * jnp.dot(
        basis, update, precision=lax.Precision.HIGHEST, preferred_element_type=f32
    )
    return (
        results[0],
        results[1],
        results[2],
        results[3],
        dense_moved[None, :],
        small_next,
        small_moved,
        embed_next,
        coeff_moved,
    )


local_coef = outer_rate * (1 + momentum_coef) / 2
old_coef = 1 - outer_rate * (1 + momentum_coef)
mom_coef = -outer_rate * momentum_coef * momentum_coef


def split(value):
    high = value.astype(bf16)
    return high, (value - high.astype(f32)).astype(bf16)


CHUNKS = 2
WHOLE = pl.BlockSpec(memory_space=pltpu.VMEM)
ANY = pl.BlockSpec(memory_space=pl.ANY)


def in_hbm(arrays):
    return [pltpu.with_memory_space_constraint(array, pltpu.HBM) for array in arrays]


def turned(chip):
    return (chip ^ (chip >> 1)) & 1


def side_start(other, columns):
    side = lax.axis_index("group") ^ turned(lax.axis_index("shard"))
    return (1 - side if other else side) * columns


def product(basis, local, old):
    rank = basis.shape[0]
    high, low = split(basis)
    diff_high, diff_low = split(old - local.astype(f32))
    first = jnp.dot(
        jnp.concatenate([high, low], axis=0), diff_high, preferred_element_type=f32
    )
    return first[:rank] + first[rank:] + jnp.dot(high, diff_low, preferred_element_type=f32)


def first_kernel(
    basis_hbm, local_hbm, old_hbm, out_ref, basis_ref, local_own, old_own, old_rest, local_rest, sems
):
    columns = out_ref.shape[1]
    block = columns // CHUNKS
    copies = [pltpu.make_async_copy(basis_hbm, basis_ref, sems.at[0])]
    for k in range(CHUNKS):
        there = pl.ds(pl.multiple_of(side_start(True, columns) + k * block, block), block)
        here = pl.ds(k * block, block)
        for source, target in ((old_hbm, old_rest), (local_hbm, local_rest)):
            at = sems.at[len(copies)]
            copies.append(pltpu.make_async_copy(source.at[:, there], target.at[:, here], at))
    there = pl.ds(pl.multiple_of(side_start(False, columns), columns), columns)
    for source, target in ((old_hbm, old_own), (local_hbm, local_own)):
        copies.append(pltpu.make_async_copy(source.at[:, there], target, sems.at[len(copies)]))
    for copy in copies:
        copy.start()
    copies[0].wait()
    basis = basis_ref[...]
    for k in range(CHUNKS):
        copies[1 + 2 * k].wait()
        copies[2 + 2 * k].wait()
        here = slice(k * block, (k + 1) * block)
        out_ref[:, here] = product(basis, local_rest[:, here], old_rest[:, here])
    copies[-2].wait()
    copies[-1].wait()


def first_half(basis_t, local, old):
    rank, depth = basis_t.shape
    columns = old.shape[1] // 2
    shapes = [((rank, columns), f32), ((rank, depth), f32), ((depth, columns), bf16)]
    shapes += [((depth, columns), f32)] * 2
    return pl.pallas_call(
        first_kernel,
        in_specs=[ANY] * 3,
        out_specs=[WHOLE] * len(shapes),
        out_shape=[jax.ShapeDtypeStruct(*shape) for shape in shapes],
        scratch_shapes=[
            pltpu.VMEM((depth, columns), bf16),
            pltpu.SemaphoreType.DMA((3 + 2 * CHUNKS,)),
        ],
        compiler_params=pltpu.CompilerParams(vmem_limit_bytes=8 * 2**20),
        cost_estimate=pl.CostEstimate(
            flops=6 * rank * depth * columns, bytes_accessed=12 * depth * columns, transcendentals=0
        ),
        name="first_half",
    )(*in_hbm((basis_t, local, old)))


def second_kernel(basis_ref, local_ref, old_ref, out_ref, stack_ref):
    basis = basis_ref[...]
    out_ref[...] = product(basis, local_ref[...], old_ref[...])
    high = basis.astype(bf16).astype(f32)
    stack_ref[...] = jnp.concatenate([high, basis - high, high], axis=0).T.astype(bf16)


def second_half(basis, local, old):
    rank, depth = basis.shape
    columns = old.shape[1]
    return pl.pallas_call(
        second_kernel,
        in_specs=[WHOLE] * 3,
        out_specs=[WHOLE] * 2,
        out_shape=[
            jax.ShapeDtypeStruct((rank, columns), f32),
            jax.ShapeDtypeStruct((depth, 3 * rank), bf16),
        ],
        compiler_params=pltpu.CompilerParams(vmem_limit_bytes=4 * 2**20),
        cost_estimate=pl.CostEstimate(
            flops=6 * rank * depth * columns, bytes_accessed=6 * depth * columns, transcendentals=0
        ),
        name="second_half",
    )(basis, local, old)


def add_kernel(scale, first_ref, second_ref, *out_refs):
    width = out_refs[0].shape[1]
    for part, out_ref in enumerate(out_refs):
        here = slice(part * width, (part + 1) * width)
        out_ref[...] = scale * (first_ref[:, here] + second_ref[:, here])


def add(first, second, parts=1, scale=1.0, flops=2 * 10**10):
    rows, columns = first.shape
    return pl.pallas_call(
        functools.partial(add_kernel, scale),
        in_specs=[WHOLE] * 2,
        out_specs=[WHOLE] * parts,
        out_shape=[jax.ShapeDtypeStruct((rows, columns // parts), f32)] * parts,
        compiler_params=pltpu.CompilerParams(vmem_limit_bytes=2 * 2**20),
        cost_estimate=pl.CostEstimate(flops=flops, bytes_accessed=0, transcendentals=0),
        name="add",
    )(first, second)


def embed_kernel(pieces, stack_ref, moment_ref, *refs):
    count = len(pieces)
    coeffs, olds = refs[:count], refs[count : 2 * count]
    embed_hbm, moved_hbm, embed_ref, moved_ref, sems = refs[-5:]
    width = coeffs[0].shape[1]
    copies = []
    for k, (other, part) in enumerate(pieces):
        start = side_start(other, olds[k].shape[1]) + part * width
        there = pl.ds(pl.multiple_of(start, width), width)
        coeff = coeffs[k][...]
        moved = momentum_coef * moment_ref[:, there] + coeff
        moved_ref[k] = moved
        up_high, up_low = split(coeff + momentum_coef * moved)
        change = jnp.dot(
            stack_ref[...],
            jnp.concatenate([up_high, up_high, up_low], axis=0),
            preferred_element_type=f32,
        )
        embed_ref[k] = olds[k][:, part * width : (part + 1) * width] - outer_rate * change
        for source, target, at in ((moved_ref, moved_hbm, 0), (embed_ref, embed_hbm, 1)):
            copy = pltpu.make_async_copy(source.at[k], target.at[:, there], sems.at[2 * k + at])
            copy.start()
            copies.append(copy)
    for copy in copies:
        copy.wait()


def embed_pieces(pieces, stack, moment, coeffs, olds, before):
    count = len(pieces)
    rank, width = coeffs[0].shape
    depth, columns = olds[0].shape
    first = 2 + 2 * count
    return pl.pallas_call(
        functools.partial(embed_kernel, pieces),
        in_specs=[WHOLE] * first + [ANY] * len(before),
        out_specs=[ANY, ANY],
        out_shape=[
            jax.ShapeDtypeStruct((depth, 2 * columns), f32),
            jax.ShapeDtypeStruct((rank, 2 * columns), f32),
        ],
        scratch_shapes=[
            pltpu.VMEM((count, depth, width), f32),
            pltpu.VMEM((count, rank, width), f32),
            pltpu.SemaphoreType.DMA((2 * count,)),
        ],
        input_output_aliases={first: 0, first + 1: 1} if before else {},
        compiler_params=pltpu.CompilerParams(vmem_limit_bytes=8 * 2**20),
        cost_estimate=pl.CostEstimate(
            flops=6 * count * rank * depth * width,
            bytes_accessed=8 * count * depth * width,
            transcendentals=0,
        ),
        name="embed_pieces",
    )(stack, moment, *coeffs, *olds, *before)


def low_lanes(rows):
    return lax.broadcasted_iota(jnp.int32, (rows, LANES), 1) < HALF


def turn(value):
    return pltpu.roll(value, HALF, 1)


def attn_tiles(in_ref, out_ref):
    whole = in_ref.shape[-1] // LANES
    tiles = [in_ref[0, :, k * LANES : (k + 1) * LANES].astype(f32) for k in range(whole)]
    last = in_ref[0, :, whole * LANES :].astype(f32)
    side = out_ref[0, :, LANES:].astype(f32)
    tiles.append(jnp.concatenate([last, side], axis=-1))
    tiles.append(out_ref[0, :, :LANES].astype(f32))
    return tiles


def unflatten_attn(flat, put, rows):
    pairs = rows // 2
    low = low_lanes(pairs)
    inner = [flat(j, pairs, 9) for j in range(9)]
    base = pairs * 9
    outer = [flat(base + j, pairs, 3) for j in range(3)]
    turned = [turn(inner[j]) for j in range(4, 9)]
    turned_out = [turn(outer[j]) for j in (1, 2)]
    for k in range(4):
        put(0, k, inner[k])
        put(1, k, jnp.where(low, turned[k], turned[k + 1]))
    put(0, 4, jnp.where(low, inner[4], turned_out[0]))
    put(1, 4, jnp.where(low, turned[4], outer[2]))
    put(0, 5, outer[0])
    put(1, 5, jnp.where(low, turned_out[0], turned_out[1]))


def flatten_attn(get, rows):
    pairs = rows // 2
    low = low_lanes(pairs)
    even = [get(0, k) for k in range(6)]
    odd = [get(1, k) for k in range(6)]
    turned = [turn(odd[k]) for k in range(5)]
    pieces = [(k, 9, even[k]) for k in range(4)]
    pieces.append((4, 9, jnp.where(low, even[4], turned[0])))
    for k in range(4):
        pieces.append((5 + k, 9, jnp.where(low, turned[k], turned[k + 1])))
    base = pairs * 9
    pieces.append((base, 3, even[5]))
    turned_out = turn(odd[5])
    pieces.append((base + 1, 3, jnp.where(low, turn(even[4]), turned_out)))
    pieces.append((base + 2, 3, jnp.where(low, turned_out, odd[4])))
    return pieces


def before_kernel(
    order_ref, moment_hbm, in_ref, out_ref, up_ref, down_ref, old_ref, mom_ref, small_ref,
    small_old_ref, small_mom_ref, send_ref, moment_ref, wide_ref, sem,
):
    del order_ref
    copy = pltpu.make_async_copy(moment_hbm, moment_ref, sem)
    copy.start()
    group = lax.axis_index("group")
    rows = up_ref.shape[1]
    mid = rows // 2
    block = rows + mid
    tiles = up_ref.shape[2] // LANES
    small = small_old_ref.shape[1]

    def flat(start, count, stride):
        at = pl.ds(start, count, stride=stride)
        return old_coef * old_ref[at, :] + mom_coef * mom_ref[at, :]

    def put(start, tile, value):
        send_ref[tile, pl.ds(block + start, rows // 2, stride=2), :] = value

    def put_small(other, own):
        own_terms = (
            old_coef * small_old_ref[...] + mom_coef * small_mom_ref[...] + local_coef * own
        )
        send_ref[:, 2 * block :, :] = jnp.zeros((tiles, 8, LANES), f32)
        for tile, value in enumerate((other, own_terms)):
            for row in range(pl.cdiv(small, LANES)):
                piece = value[:, row * LANES : (row + 1) * LANES]
                at = 2 * block + row
                send_ref[tile, at : at + 1, : piece.shape[1]] = piece

    @pl.when(group == 0)
    def _():
        unflatten_attn(flat, put, rows)
        for k, value in enumerate(attn_tiles(in_ref, out_ref)):
            send_ref[k, block : block + rows, :] += local_coef * value
        base = rows * tiles
        for k in range(tiles):
            columns = slice(k * LANES, (k + 1) * LANES)
            send_ref[k, :mid, :] = up_ref[0, mid:, columns].astype(f32)
            send_ref[k, mid:block, :] = down_ref[0, :, columns].astype(f32)
            send_ref[k, block + rows : 2 * block, :] = flat(base + k, mid, tiles) + (
                local_coef * up_ref[0, :mid, columns].astype(f32)
            )
        values = small_ref[...].astype(f32)
        put_small(values[:, small:], values[:, :small])

    @pl.when(group == 1)
    def _():
        for k, value in enumerate(attn_tiles(in_ref, out_ref)):
            send_ref[k, :rows, :] = value
        for k in range(tiles):
            columns = slice(k * LANES, (k + 1) * LANES)
            send_ref[k, rows:block, :] = up_ref[0, :mid, columns].astype(f32)
            send_ref[k, block : block + mid, :] = flat(k, mid, tiles) + (
                local_coef * up_ref[0, mid:, columns].astype(f32)
            )
        base = mid * tiles
        pairs = tiles * HALF
        low = low_lanes(pairs)
        first, second, third = (flat(base + j, pairs, 3) for j in range(3))
        turned, turned_more = turn(second), turn(third)
        even, odd = pl.ds(0, pairs, stride=2), pl.ds(1, pairs, stride=2)
        wide_ref[0, even, :] = first
        wide_ref[1, even, :] = second
        wide_ref[0, odd, :] = jnp.where(low, turned, turned_more)
        wide_ref[1, odd, :] = turned_more
        start = block + mid
        for k in range(tiles):
            columns = slice(k * LANES, (k + 1) * LANES)
            upper = wide_ref[0, columns, :].T
            lower = wide_ref[1, columns, :].T[:HALF]
            send_ref[k, start : start + LANES, :] = upper + (
                local_coef * down_ref[0, :LANES, columns].astype(f32)
            )
            send_ref[k, start + LANES : 2 * block, :] = lower + (
                local_coef * down_ref[0, LANES:, columns].astype(f32)
            )
        values = small_ref[...].astype(f32)
        put_small(values[:, :small], values[:, small:])

    copy.wait()


def after_kernel(
    recv_ref, send_ref, in_ref, out_ref, up_ref, down_ref, old_ref, mom_ref, small_ref,
    small_old_ref, small_mom_ref, in_next_ref, out_next_ref, up_next_ref, down_next_ref, moved_ref,
    small_next_ref, small_moved_ref, sum_ref, wide_ref,
):
    rows = up_ref.shape[1]
    mid = rows // 2
    block = rows + mid
    tiles = up_ref.shape[2] // LANES
    small = small_old_ref.shape[1]
    group = lax.axis_index("group")

    def put_moved(start, stride, value):
        at = pl.ds(start, value.shape[0], stride=stride)
        moved_ref[at, :] = momentum_coef * mom_ref[at, :] + (old_ref[at, :] - 0.5 * value)

    def get(start, tile):
        return sum_ref[tile, pl.ds(start, rows // 2, stride=2), :]

    def put_attn(tile, value):
        whole = in_ref.shape[-1] // LANES
        if tile < whole:
            in_next_ref[:, tile * LANES : (tile + 1) * LANES] = value
        elif tile == whole:
            in_next_ref[:, tile * LANES :] = value[:, :HALF]
            out_next_ref[:, LANES:] = turn(value)[:, :HALF]
        else:
            out_next_ref[:, :LANES] = value

    def small_row(ref, tile):
        pieces = []
        for row in range(pl.cdiv(small, LANES)):
            at = 2 * block + row
            pieces.append(ref[tile, at : at + 1, : min(LANES, small - row * LANES)])
        return jnp.concatenate(pieces, axis=1)

    def put_small(other, own, first):
        theirs = small_row(recv_ref, 0)
        mine = small_row(send_ref, 1) + local_coef * theirs
        rest = small_row(recv_ref, 1) + local_coef * other
        both = [mine, rest] if first else [rest, mine]
        small_next_ref[...] = jnp.concatenate(both, axis=1).reshape(-1)
        small_moved_ref[...] = momentum_coef * small_mom_ref[...] + (
            small_old_ref[...] - 0.5 * (own + theirs)
        )

    @pl.when(group == 0)
    def _():
        for k, value in enumerate(attn_tiles(in_ref, out_ref)):
            theirs = recv_ref[k, :rows, :]
            put_attn(k, send_ref[k, block : block + rows, :] + local_coef * theirs)
            sum_ref[k, :, :] = value + theirs
        for start, stride, value in flatten_attn(get, rows):
            put_moved(start, stride, value)
        base = rows * tiles
        for k in range(tiles):
            columns = slice(k * LANES, (k + 1) * LANES)
            theirs = recv_ref[k, rows:block, :]
            up_next_ref[:mid, columns] = (
                send_ref[k, block + rows : 2 * block, :] + local_coef * theirs
            )
            put_moved(base + k, tiles, up_ref[0, :mid, columns].astype(f32) + theirs)
            up_next_ref[mid:, columns] = recv_ref[k, block : block + mid, :] + (
                local_coef * up_ref[0, mid:, columns].astype(f32)
            )
            down_next_ref[:, columns] = recv_ref[k, block + mid : 2 * block, :] + (
                local_coef * down_ref[0, :, columns].astype(f32)
            )
        values = small_ref[...].astype(f32)
        put_small(values[:, small:], values[:, :small], True)

    @pl.when(group == 1)
    def _():
        for k, value in enumerate(attn_tiles(in_ref, out_ref)):
            put_attn(k, recv_ref[k, block : block + rows, :] + local_coef * value)
        for k in range(tiles):
            columns = slice(k * LANES, (k + 1) * LANES)
            up_next_ref[:mid, columns] = recv_ref[k, block + rows : 2 * block, :] + (
                local_coef * up_ref[0, :mid, columns].astype(f32)
            )
            theirs = recv_ref[k, :mid, :]
            up_next_ref[mid:, columns] = send_ref[k, block : block + mid, :] + local_coef * theirs
            put_moved(k, tiles, up_ref[0, mid:, columns].astype(f32) + theirs)
            theirs = recv_ref[k, mid:block, :]
            down_next_ref[:, columns] = (
                send_ref[k, block + mid : 2 * block, :] + local_coef * theirs
            )
            total = down_ref[0, :, columns].astype(f32) + theirs
            wide_ref[0, columns, :] = total[:LANES].T
            lower = jnp.concatenate([total[LANES:], total[LANES:]], axis=0)
            wide_ref[1, columns, :] = lower.T
        base = mid * tiles
        pairs = tiles * HALF
        low = low_lanes(pairs)
        even, odd = pl.ds(0, pairs, stride=2), pl.ds(1, pairs, stride=2)
        odd_first = turn(wide_ref[0, odd, :])
        put_moved(base, 3, wide_ref[0, even, :])
        put_moved(base + 1, 3, jnp.where(low, wide_ref[1, even, :], odd_first))
        put_moved(base + 2, 3, jnp.where(low, odd_first, wide_ref[1, odd, :]))
        values = small_ref[...].astype(f32)
        put_small(values[:, :small], values[:, small:], False)


def dense_before(order, moment, operands):
    _, rows, width = operands[2].shape
    return pl.pallas_call(
        before_kernel,
        in_specs=[ANY] * 2 + [WHOLE] * 9,
        out_specs=[WHOLE] * 2,
        out_shape=[
            jax.ShapeDtypeStruct((width // LANES, 3 * rows + 8, LANES), f32),
            jax.ShapeDtypeStruct(moment.shape, f32),
        ],
        scratch_shapes=[pltpu.VMEM((2, width, LANES), f32), pltpu.SemaphoreType.DMA],
        compiler_params=pltpu.CompilerParams(vmem_limit_bytes=4 * 2**20),
        cost_estimate=pl.CostEstimate(
            flops=60000 * rows * width, bytes_accessed=30 * rows * width, transcendentals=0
        ),
        name="dense_before",
    )(order, *in_hbm([moment]), *operands)


def dense_after(received, sent, operands):
    _, rows, width = operands[2].shape
    outs = [matrix.shape[1:] for matrix in operands[:4]]
    outs += [operands[4].shape, operands[6].shape[1:], operands[7].shape]
    return pl.pallas_call(
        after_kernel,
        in_specs=[WHOLE] * 11,
        out_specs=[WHOLE] * 7,
        out_shape=[jax.ShapeDtypeStruct(shape, f32) for shape in outs],
        scratch_shapes=[
            pltpu.VMEM((width // LANES, rows, LANES), f32),
            pltpu.VMEM((2, width, LANES), f32),
        ],
        compiler_params=pltpu.CompilerParams(vmem_limit_bytes=8 * 2**20),
        cost_estimate=pl.CostEstimate(
            flops=60000 * rows * width, bytes_accessed=40 * rows * width, transcendentals=0
        ),
        name="dense_after",
    )(received, sent, *operands)


def paired(
    attn_in_local,
    attn_out_local,
    ffn_in_local,
    ffn_out_local,
    small_local,
    dense_old,
    dense_momentum,
    small_old,
    small_momentum,
    embed_local,
    embed_old,
    basis,
    coeff_momentum,
):
    swap = [(0, 1), (1, 0)]
    chips = lax.axis_size("shard")

    first, second = (
        [
            (core * chips + chip, (1 - core) * chips + (chip ^ (1 + (core ^ turned(chip) ^ late))))
            for core in range(2)
            for chip in range(chips)
        ]
        for late in range(2)
    )
    axes = ("group", "shard")

    theirs, basis_t, local_own, old_own, old_rest = first_half(
        basis.T, embed_local[0], embed_old
    )
    theirs = lax.ppermute(theirs, "group", swap)
    mine, stack = second_half(basis_t, local_own, old_own)

    operands = (
        attn_in_local,
        attn_out_local,
        ffn_in_local,
        jnp.swapaxes(ffn_out_local, 1, 2),
        dense_old.reshape(-1, LANES),
        dense_momentum.reshape(-1, LANES),
        small_local,
        small_old[None, :],
        small_momentum[None, :],
    )
    totals = add(mine, theirs, 2)
    moving = [lax.ppermute(total, axes, first) for total in totals]
    sent, moment = dense_before(totals[0], coeff_momentum, operands)
    received = lax.ppermute(sent, "group", swap)
    totals = [
        add(*pair, flops=flops)[0] for *pair, flops in zip(totals, moving, (10**4, 2 * 10**10))
    ]
    moving = [lax.ppermute(total, axes, second) for total in totals]
    dense = list(dense_after(received, sent, operands))
    moving[0], dense[-1] = lax.optimization_barrier((moving[0], dense[-1]))
    own = [add(*pair, scale=0.5)[0] for pair in zip(totals, moving)]
    rest = [lax.ppermute(part, "group", swap) for part in own]
    done = ()
    for pieces, coeffs in (
        (((False, 0), (False, 1), (True, 0)), (*own, rest[0])),
        (((True, 1),), rest[1:]),
    ):
        olds = [old_rest if other else old_own for other, _ in pieces]
        done = embed_pieces(pieces, stack, moment, coeffs, olds, done)
    embed_next, coeff_moved = done

    attn_in_next, attn_out_next, ffn_in_next, ffn_out_next, moved, small_next, small_moved = dense
    return (
        attn_in_next,
        attn_out_next,
        ffn_in_next,
        ffn_out_next.T,
        moved.reshape(dense_old.shape),
        small_next,
        small_moved[0],
        embed_next,
        coeff_moved,
    )


def is_paired(mesh, shapes):
    attn_in, attn_out, ffn_in, ffn_out = (shape[1:] for shape in shapes[:4])
    rows = ffn_in[0]
    return (
        mesh.shape["group"] == 2
        and mesh.shape["shard"] == 4
        and attn_in == (rows, 4 * LANES + HALF)
        and attn_out == (rows, LANES + HALF)
        and ffn_in[1] == 6 * LANES
        and ffn_out == (6 * LANES, rows)
        and rows == LANES + HALF
        and shapes[7][0] <= 8 * LANES
        and shapes[10][1] % (8 * LANES) == 0
    )


def solution(mesh):
    placed = (
        P("group", "shard", "tensor"),
        P("group", "shard", "tensor"),
        P("group", "shard", "tensor"),
        P("group", "shard", "tensor"),
        P("group", None),
        P(("shard", "tensor"), "group"),
        P(("shard", "tensor"), "group"),
        P("group"),
        P("group"),
        P("group", "shard", "tensor"),
        P("shard", "tensor"),
        P("shard", None),
        P(None, "tensor"),
    )

    def shards(*args):
        plan = paired if is_paired(mesh, [arg.shape for arg in args]) else general
        return plan(*args)

    return jax.shard_map(
        shards,
        mesh=mesh,
        in_specs=placed,
        out_specs=(
            P("shard", "tensor"),
            P("shard", "tensor"),
            P("shard", "tensor"),
            P("shard", "tensor"),
            P(("shard", "tensor"), "group"),
            P(),
            P("group"),
            P("shard", "tensor"),
            P(None, "tensor"),
        ),
        check_vma=False,
    )
```

```python
import functools

import jax
import jax.numpy as jnp
from jax import lax
from jax.experimental import pallas as pl
from jax.experimental.pallas import tpu as pltpu
from jax.sharding import PartitionSpec as P

momentum_coef = 0.5
outer_rate = 0.7

f32 = jnp.float32
bf16 = jnp.bfloat16
LANES = 128
HALF = LANES // 2


def nesterov(old_value, momentum, delta):
    moved = momentum_coef * momentum + delta
    return (old_value - outer_rate * (delta + momentum_coef * moved), moved)


def general(
    attn_in_local,
    attn_out_local,
    ffn_in_local,
    ffn_out_local,
    small_local,
    dense_old,
    dense_momentum,
    small_old,
    small_momentum,
    embed_local,
    embed_old,
    basis,
    coeff_momentum,
):
    groups = lax.axis_size("group")
    matrices = (attn_in_local, attn_out_local, ffn_in_local, ffn_out_local)
    local_terms = jnp.concatenate([matrix[0].reshape(-1) for matrix in matrices]).astype(f32)
    small_terms = small_local[0].astype(f32)
    old_flat = dense_old[0]
    momentum_flat = dense_momentum[0]
    dense_part, small_part = (
        lax.psum_scatter(local_terms, "group", scatter_dimension=0, tiled=True),
        lax.psum_scatter(small_terms, "group", scatter_dimension=0, tiled=True),
    )
    dense_new, dense_moved = nesterov(old_flat, momentum_flat, old_flat - dense_part / groups)
    small_new, small_moved = nesterov(small_old, small_momentum, small_old - small_part / groups)
    full_flat, small_next = (
        lax.all_gather(dense_new, "group", axis=0, tiled=True),
        lax.all_gather(small_new, "group", axis=0, tiled=True),
    )
    results = []
    offset = 0
    for matrix in matrices:
        block_size = matrix.shape[1] * matrix.shape[2]
        results.append(
            full_flat[offset : offset + block_size].reshape(matrix.shape[1], matrix.shape[2])
        )
        offset = offset + block_size
    difference = embed_old - embed_local[0].astype(f32)
    partial_coeff = lax.dot_general(
        basis,
        difference,
        (((0,), (0,)), ((), ())),
        precision=lax.Precision.HIGHEST,
        preferred_element_type=f32,
    )
    coeff = lax.psum(partial_coeff, ("group", "shard")) / groups
    coeff_moved = momentum_coef * coeff_momentum + coeff
    update = coeff + momentum_coef * coeff_moved
    embed_next = embed_old - outer_rate * jnp.dot(
        basis, update, precision=lax.Precision.HIGHEST, preferred_element_type=f32
    )
    return (
        results[0],
        results[1],
        results[2],
        results[3],
        dense_moved[None, :],
        small_next,
        small_moved,
        embed_next,
        coeff_moved,
    )


local_coef = outer_rate * (1 + momentum_coef) / 2
old_coef = 1 - outer_rate * (1 + momentum_coef)
mom_coef = -outer_rate * momentum_coef * momentum_coef


def split(value):
    high = value.astype(bf16)
    return high, (value - high.astype(f32)).astype(bf16)


CHUNKS = 2
WHOLE = pl.BlockSpec(memory_space=pltpu.VMEM)
ANY = pl.BlockSpec(memory_space=pl.ANY)


def in_hbm(arrays):
    return [pltpu.with_memory_space_constraint(array, pltpu.HBM) for array in arrays]


def turned(chip):
    return (chip ^ (chip >> 1)) & 1


def side_start(other, columns):
    side = lax.axis_index("group") ^ turned(lax.axis_index("shard"))
    return (1 - side if other else side) * columns


def product(basis, local, old):
    rank = basis.shape[0]
    high, low = split(basis)
    diff_high, diff_low = split(old - local.astype(f32))
    first = jnp.dot(
        jnp.concatenate([high, low], axis=0), diff_high, preferred_element_type=f32
    )
    return first[:rank] + first[rank:] + jnp.dot(high, diff_low, preferred_element_type=f32)


def first_kernel(basis_hbm, local_hbm, old_hbm, *refs):
    out_refs = refs[:CHUNKS]
    basis_ref, local_own, old_own, old_rest, local_rest, sems = refs[CHUNKS:]
    columns = old_own.shape[1]
    block = columns // CHUNKS
    copies = [pltpu.make_async_copy(basis_hbm, basis_ref, sems.at[0])]
    for k in range(CHUNKS):
        there = pl.ds(pl.multiple_of(side_start(True, columns) + k * block, block), block)
        here = pl.ds(k * block, block)
        for source, target in ((old_hbm, old_rest), (local_hbm, local_rest)):
            at = sems.at[len(copies)]
            copies.append(pltpu.make_async_copy(source.at[:, there], target.at[:, here], at))
    there = pl.ds(pl.multiple_of(side_start(False, columns), columns), columns)
    for source, target in ((old_hbm, old_own), (local_hbm, local_own)):
        copies.append(pltpu.make_async_copy(source.at[:, there], target, sems.at[len(copies)]))
    for copy in copies:
        copy.start()
    copies[0].wait()
    basis = basis_ref[...]
    for k in range(CHUNKS):
        copies[1 + 2 * k].wait()
        copies[2 + 2 * k].wait()
        here = slice(k * block, (k + 1) * block)
        out_refs[k][...] = product(basis, local_rest[:, here], old_rest[:, here])
    copies[-2].wait()
    copies[-1].wait()


def first_half(basis_t, local, old):
    rank, depth = basis_t.shape
    columns = old.shape[1] // 2
    shapes = [((rank, columns // CHUNKS), f32)] * CHUNKS
    shapes += [((rank, depth), f32), ((depth, columns), bf16)]
    shapes += [((depth, columns), f32)] * 2
    return pl.pallas_call(
        first_kernel,
        in_specs=[ANY] * 3,
        out_specs=[WHOLE] * len(shapes),
        out_shape=[jax.ShapeDtypeStruct(*shape) for shape in shapes],
        scratch_shapes=[
            pltpu.VMEM((depth, columns), bf16),
            pltpu.SemaphoreType.DMA((3 + 2 * CHUNKS,)),
        ],
        compiler_params=pltpu.CompilerParams(vmem_limit_bytes=8 * 2**20),
        cost_estimate=pl.CostEstimate(
            flops=6 * rank * depth * columns, bytes_accessed=12 * depth * columns, transcendentals=0
        ),
        name="first_half",
    )(*in_hbm((basis_t, local, old)))


def second_kernel(basis_ref, local_ref, old_ref, *refs):
    *out_refs, stack_ref = refs
    basis = basis_ref[...]
    block = old_ref.shape[1] // CHUNKS
    for k, out_ref in enumerate(out_refs):
        here = slice(k * block, (k + 1) * block)
        out_ref[...] = product(basis, local_ref[:, here], old_ref[:, here])
    high = basis.astype(bf16).astype(f32)
    stack_ref[...] = jnp.concatenate([high, basis - high, high], axis=0).T.astype(bf16)


def second_half(basis, local, old):
    rank, depth = basis.shape
    columns = old.shape[1]
    return pl.pallas_call(
        second_kernel,
        in_specs=[WHOLE] * 3,
        out_specs=[WHOLE] * (CHUNKS + 1),
        out_shape=[jax.ShapeDtypeStruct((rank, columns // CHUNKS), f32)] * CHUNKS
        + [jax.ShapeDtypeStruct((depth, 3 * rank), bf16)],
        compiler_params=pltpu.CompilerParams(vmem_limit_bytes=4 * 2**20),
        cost_estimate=pl.CostEstimate(
            flops=10**10, bytes_accessed=6 * depth * columns, transcendentals=0
        ),
        name="second_half",
    )(basis, local, old)


def add_kernel(scale, first_ref, second_ref, *out_refs):
    width = out_refs[0].shape[1]
    for part, out_ref in enumerate(out_refs):
        here = slice(part * width, (part + 1) * width)
        out_ref[...] = scale * (first_ref[:, here] + second_ref[:, here])


def add(first, second, parts=1, scale=1.0, flops=2 * 10**10):
    rows, columns = first.shape
    return pl.pallas_call(
        functools.partial(add_kernel, scale),
        in_specs=[WHOLE] * 2,
        out_specs=[WHOLE] * parts,
        out_shape=[jax.ShapeDtypeStruct((rows, columns // parts), f32)] * parts,
        compiler_params=pltpu.CompilerParams(vmem_limit_bytes=2 * 2**20),
        cost_estimate=pl.CostEstimate(flops=flops, bytes_accessed=0, transcendentals=0),
        name="add",
    )(first, second)


def embed_kernel(pieces, stack_ref, moment_ref, *refs):
    count = len(pieces)
    coeffs, olds = refs[:count], refs[count : 2 * count]
    embed_hbm, moved_hbm, embed_ref, moved_ref, sems = refs[-5:]
    width = coeffs[0].shape[1]
    copies = []
    for k, (other, part) in enumerate(pieces):
        start = side_start(other, olds[k].shape[1]) + part * width
        there = pl.ds(pl.multiple_of(start, width), width)
        coeff = coeffs[k][...]
        moved = momentum_coef * moment_ref[:, there] + coeff
        moved_ref[k] = moved
        up_high, up_low = split(coeff + momentum_coef * moved)
        change = jnp.dot(
            stack_ref[...],
            jnp.concatenate([up_high, up_high, up_low], axis=0),
            preferred_element_type=f32,
        )
        embed_ref[k] = olds[k][:, part * width : (part + 1) * width] - outer_rate * change
        for source, target, at in ((moved_ref, moved_hbm, 0), (embed_ref, embed_hbm, 1)):
            copy = pltpu.make_async_copy(source.at[k], target.at[:, there], sems.at[2 * k + at])
            copy.start()
            copies.append(copy)
    for copy in copies:
        copy.wait()


def embed_pieces(pieces, stack, moment, coeffs, olds, before):
    count = len(pieces)
    rank, width = coeffs[0].shape
    depth, columns = olds[0].shape
    first = 2 + 2 * count
    return pl.pallas_call(
        functools.partial(embed_kernel, pieces),
        in_specs=[WHOLE] * first + [ANY] * len(before),
        out_specs=[ANY, ANY],
        out_shape=[
            jax.ShapeDtypeStruct((depth, 2 * columns), f32),
            jax.ShapeDtypeStruct((rank, 2 * columns), f32),
        ],
        scratch_shapes=[
            pltpu.VMEM((count, depth, width), f32),
            pltpu.VMEM((count, rank, width), f32),
            pltpu.SemaphoreType.DMA((2 * count,)),
        ],
        input_output_aliases={first: 0, first + 1: 1} if before else {},
        compiler_params=pltpu.CompilerParams(vmem_limit_bytes=8 * 2**20),
        cost_estimate=pl.CostEstimate(
            flops=6 * count * rank * depth * width,
            bytes_accessed=8 * count * depth * width,
            transcendentals=0,
        ),
        name="embed_pieces",
    )(stack, moment, *coeffs, *olds, *before)


def low_lanes(rows):
    return lax.broadcasted_iota(jnp.int32, (rows, LANES), 1) < HALF


def turn(value):
    return pltpu.roll(value, HALF, 1)


def attn_tiles(in_ref, out_ref):
    whole = in_ref.shape[-1] // LANES
    tiles = [in_ref[0, :, k * LANES : (k + 1) * LANES].astype(f32) for k in range(whole)]
    last = in_ref[0, :, whole * LANES :].astype(f32)
    side = out_ref[0, :, LANES:].astype(f32)
    tiles.append(jnp.concatenate([last, side], axis=-1))
    tiles.append(out_ref[0, :, :LANES].astype(f32))
    return tiles


def unflatten_attn(flat, put, rows):
    pairs = rows // 2
    low = low_lanes(pairs)
    inner = [flat(j, pairs, 9) for j in range(9)]
    base = pairs * 9
    outer = [flat(base + j, pairs, 3) for j in range(3)]
    turned = [turn(inner[j]) for j in range(4, 9)]
    turned_out = [turn(outer[j]) for j in (1, 2)]
    for k in range(4):
        put(0, k, inner[k])
        put(1, k, jnp.where(low, turned[k], turned[k + 1]))
    put(0, 4, jnp.where(low, inner[4], turned_out[0]))
    put(1, 4, jnp.where(low, turned[4], outer[2]))
    put(0, 5, outer[0])
    put(1, 5, jnp.where(low, turned_out[0], turned_out[1]))


def flatten_attn(get, rows):
    pairs = rows // 2
    low = low_lanes(pairs)
    even = [get(0, k) for k in range(6)]
    odd = [get(1, k) for k in range(6)]
    turned = [turn(odd[k]) for k in range(5)]
    pieces = [(k, 9, even[k]) for k in range(4)]
    pieces.append((4, 9, jnp.where(low, even[4], turned[0])))
    for k in range(4):
        pieces.append((5 + k, 9, jnp.where(low, turned[k], turned[k + 1])))
    base = pairs * 9
    pieces.append((base, 3, even[5]))
    turned_out = turn(odd[5])
    pieces.append((base + 1, 3, jnp.where(low, turn(even[4]), turned_out)))
    pieces.append((base + 2, 3, jnp.where(low, turned_out, odd[4])))
    return pieces


def before_kernel(
    order_ref, moment_hbm, in_ref, out_ref, up_ref, down_ref, old_ref, mom_ref, small_ref,
    small_old_ref, small_mom_ref, send_ref, moment_ref, wide_ref, sem,
):
    del order_ref
    copy = pltpu.make_async_copy(moment_hbm, moment_ref, sem)
    copy.start()
    group = lax.axis_index("group")
    rows = up_ref.shape[1]
    mid = rows // 2
    block = rows + mid
    tiles = up_ref.shape[2] // LANES
    small = small_old_ref.shape[1]

    def flat(start, count, stride):
        at = pl.ds(start, count, stride=stride)
        return old_coef * old_ref[at, :] + mom_coef * mom_ref[at, :]

    def put(start, tile, value):
        send_ref[tile, pl.ds(block + start, rows // 2, stride=2), :] = value

    def put_small(other, own):
        own_terms = (
            old_coef * small_old_ref[...] + mom_coef * small_mom_ref[...] + local_coef * own
        )
        send_ref[:, 2 * block :, :] = jnp.zeros((tiles, 8, LANES), f32)
        for tile, value in enumerate((other, own_terms)):
            for row in range(pl.cdiv(small, LANES)):
                piece = value[:, row * LANES : (row + 1) * LANES]
                at = 2 * block + row
                send_ref[tile, at : at + 1, : piece.shape[1]] = piece

    @pl.when(group == 0)
    def _():
        unflatten_attn(flat, put, rows)
        for k, value in enumerate(attn_tiles(in_ref, out_ref)):
            send_ref[k, block : block + rows, :] += local_coef * value
        base = rows * tiles
        for k in range(tiles):
            columns = slice(k * LANES, (k + 1) * LANES)
            send_ref[k, :mid, :] = up_ref[0, mid:, columns].astype(f32)
            send_ref[k, mid:block, :] = down_ref[0, :, columns].astype(f32)
            send_ref[k, block + rows : 2 * block, :] = flat(base + k, mid, tiles) + (
                local_coef * up_ref[0, :mid, columns].astype(f32)
            )
        values = small_ref[...].astype(f32)
        put_small(values[:, small:], values[:, :small])

    @pl.when(group == 1)
    def _():
        for k, value in enumerate(attn_tiles(in_ref, out_ref)):
            send_ref[k, :rows, :] = value
        for k in range(tiles):
            columns = slice(k * LANES, (k + 1) * LANES)
            send_ref[k, rows:block, :] = up_ref[0, :mid, columns].astype(f32)
            send_ref[k, block : block + mid, :] = flat(k, mid, tiles) + (
                local_coef * up_ref[0, mid:, columns].astype(f32)
            )
        base = mid * tiles
        pairs = tiles * HALF
        low = low_lanes(pairs)
        first, second, third = (flat(base + j, pairs, 3) for j in range(3))
        turned, turned_more = turn(second), turn(third)
        even, odd = pl.ds(0, pairs, stride=2), pl.ds(1, pairs, stride=2)
        wide_ref[0, even, :] = first
        wide_ref[1, even, :] = second
        wide_ref[0, odd, :] = jnp.where(low, turned, turned_more)
        wide_ref[1, odd, :] = turned_more
        start = block + mid
        for k in range(tiles):
            columns = slice(k * LANES, (k + 1) * LANES)
            upper = wide_ref[0, columns, :].T
            lower = wide_ref[1, columns, :].T[:HALF]
            send_ref[k, start : start + LANES, :] = upper + (
                local_coef * down_ref[0, :LANES, columns].astype(f32)
            )
            send_ref[k, start + LANES : 2 * block, :] = lower + (
                local_coef * down_ref[0, LANES:, columns].astype(f32)
            )
        values = small_ref[...].astype(f32)
        put_small(values[:, :small], values[:, small:])

    copy.wait()


def after_kernel(
    recv_ref, send_ref, in_ref, out_ref, up_ref, down_ref, old_ref, mom_ref, small_ref,
    small_old_ref, small_mom_ref, in_next_ref, out_next_ref, up_next_ref, down_next_ref, moved_ref,
    small_next_ref, small_moved_ref, sum_ref, wide_ref,
):
    rows = up_ref.shape[1]
    mid = rows // 2
    block = rows + mid
    tiles = up_ref.shape[2] // LANES
    small = small_old_ref.shape[1]
    group = lax.axis_index("group")

    def put_moved(start, stride, value):
        at = pl.ds(start, value.shape[0], stride=stride)
        moved_ref[at, :] = momentum_coef * mom_ref[at, :] + (old_ref[at, :] - 0.5 * value)

    def get(start, tile):
        return sum_ref[tile, pl.ds(start, rows // 2, stride=2), :]

    def put_attn(tile, value):
        whole = in_ref.shape[-1] // LANES
        if tile < whole:
            in_next_ref[:, tile * LANES : (tile + 1) * LANES] = value
        elif tile == whole:
            in_next_ref[:, tile * LANES :] = value[:, :HALF]
            out_next_ref[:, LANES:] = turn(value)[:, :HALF]
        else:
            out_next_ref[:, :LANES] = value

    def small_row(ref, tile):
        pieces = []
        for row in range(pl.cdiv(small, LANES)):
            at = 2 * block + row
            pieces.append(ref[tile, at : at + 1, : min(LANES, small - row * LANES)])
        return jnp.concatenate(pieces, axis=1)

    def put_small(other, own, first):
        theirs = small_row(recv_ref, 0)
        mine = small_row(send_ref, 1) + local_coef * theirs
        rest = small_row(recv_ref, 1) + local_coef * other
        both = [mine, rest] if first else [rest, mine]
        small_next_ref[...] = jnp.concatenate(both, axis=1).reshape(-1)
        small_moved_ref[...] = momentum_coef * small_mom_ref[...] + (
            small_old_ref[...] - 0.5 * (own + theirs)
        )

    @pl.when(group == 0)
    def _():
        for k, value in enumerate(attn_tiles(in_ref, out_ref)):
            theirs = recv_ref[k, :rows, :]
            put_attn(k, send_ref[k, block : block + rows, :] + local_coef * theirs)
            sum_ref[k, :, :] = value + theirs
        for start, stride, value in flatten_attn(get, rows):
            put_moved(start, stride, value)
        base = rows * tiles
        for k in range(tiles):
            columns = slice(k * LANES, (k + 1) * LANES)
            theirs = recv_ref[k, rows:block, :]
            up_next_ref[:mid, columns] = (
                send_ref[k, block + rows : 2 * block, :] + local_coef * theirs
            )
            put_moved(base + k, tiles, up_ref[0, :mid, columns].astype(f32) + theirs)
            up_next_ref[mid:, columns] = recv_ref[k, block : block + mid, :] + (
                local_coef * up_ref[0, mid:, columns].astype(f32)
            )
            down_next_ref[:, columns] = recv_ref[k, block + mid : 2 * block, :] + (
                local_coef * down_ref[0, :, columns].astype(f32)
            )
        values = small_ref[...].astype(f32)
        put_small(values[:, small:], values[:, :small], True)

    @pl.when(group == 1)
    def _():
        for k, value in enumerate(attn_tiles(in_ref, out_ref)):
            put_attn(k, recv_ref[k, block : block + rows, :] + local_coef * value)
        for k in range(tiles):
            columns = slice(k * LANES, (k + 1) * LANES)
            up_next_ref[:mid, columns] = recv_ref[k, block + rows : 2 * block, :] + (
                local_coef * up_ref[0, :mid, columns].astype(f32)
            )
            theirs = recv_ref[k, :mid, :]
            up_next_ref[mid:, columns] = send_ref[k, block : block + mid, :] + local_coef * theirs
            put_moved(k, tiles, up_ref[0, mid:, columns].astype(f32) + theirs)
            theirs = recv_ref[k, mid:block, :]
            down_next_ref[:, columns] = (
                send_ref[k, block + mid : 2 * block, :] + local_coef * theirs
            )
            total = down_ref[0, :, columns].astype(f32) + theirs
            wide_ref[0, columns, :] = total[:LANES].T
            lower = jnp.concatenate([total[LANES:], total[LANES:]], axis=0)
            wide_ref[1, columns, :] = lower.T
        base = mid * tiles
        pairs = tiles * HALF
        low = low_lanes(pairs)
        even, odd = pl.ds(0, pairs, stride=2), pl.ds(1, pairs, stride=2)
        odd_first = turn(wide_ref[0, odd, :])
        put_moved(base, 3, wide_ref[0, even, :])
        put_moved(base + 1, 3, jnp.where(low, wide_ref[1, even, :], odd_first))
        put_moved(base + 2, 3, jnp.where(low, odd_first, wide_ref[1, odd, :]))
        values = small_ref[...].astype(f32)
        put_small(values[:, :small], values[:, small:], False)


def dense_before(order, moment, operands):
    _, rows, width = operands[2].shape
    return pl.pallas_call(
        before_kernel,
        in_specs=[ANY] * 2 + [WHOLE] * 9,
        out_specs=[WHOLE] * 2,
        out_shape=[
            jax.ShapeDtypeStruct((width // LANES, 3 * rows + 8, LANES), f32),
            jax.ShapeDtypeStruct(moment.shape, f32),
        ],
        scratch_shapes=[pltpu.VMEM((2, width, LANES), f32), pltpu.SemaphoreType.DMA],
        compiler_params=pltpu.CompilerParams(vmem_limit_bytes=4 * 2**20),
        cost_estimate=pl.CostEstimate(
            flops=60000 * rows * width, bytes_accessed=30 * rows * width, transcendentals=0
        ),
        name="dense_before",
    )(order, *in_hbm([moment]), *operands)


def dense_after(received, sent, operands):
    _, rows, width = operands[2].shape
    outs = [matrix.shape[1:] for matrix in operands[:4]]
    outs += [operands[4].shape, operands[6].shape[1:], operands[7].shape]
    return pl.pallas_call(
        after_kernel,
        in_specs=[WHOLE] * 11,
        out_specs=[WHOLE] * 7,
        out_shape=[jax.ShapeDtypeStruct(shape, f32) for shape in outs],
        scratch_shapes=[
            pltpu.VMEM((width // LANES, rows, LANES), f32),
            pltpu.VMEM((2, width, LANES), f32),
        ],
        compiler_params=pltpu.CompilerParams(vmem_limit_bytes=8 * 2**20),
        cost_estimate=pl.CostEstimate(
            flops=60000 * rows * width, bytes_accessed=40 * rows * width, transcendentals=0
        ),
        name="dense_after",
    )(received, sent, *operands)


def paired(
    attn_in_local,
    attn_out_local,
    ffn_in_local,
    ffn_out_local,
    small_local,
    dense_old,
    dense_momentum,
    small_old,
    small_momentum,
    embed_local,
    embed_old,
    basis,
    coeff_momentum,
):
    swap = [(0, 1), (1, 0)]
    chips = lax.axis_size("shard")

    first, second = (
        [
            (core * chips + chip, (1 - core) * chips + (chip ^ (1 + (core ^ turned(chip) ^ late))))
            for core in range(2)
            for chip in range(chips)
        ]
        for late in range(2)
    )
    axes = ("group", "shard")

    *theirs, basis_t, local_own, old_own, old_rest = first_half(
        basis.T, embed_local[0], embed_old
    )
    theirs = [lax.ppermute(part, "group", swap) for part in theirs]
    *mine, stack = second_half(basis_t, local_own, old_own)

    operands = (
        attn_in_local,
        attn_out_local,
        ffn_in_local,
        jnp.swapaxes(ffn_out_local, 1, 2),
        dense_old.reshape(-1, LANES),
        dense_momentum.reshape(-1, LANES),
        small_local,
        small_old[None, :],
        small_momentum[None, :],
    )
    totals = [add(*pair, flops=10**4)[0] for pair in zip(mine, theirs)]
    moving = [lax.ppermute(total, axes, first) for total in totals]
    sent, moment = dense_before(totals[0], coeff_momentum, operands)
    received = lax.ppermute(sent, "group", swap)
    totals = [
        add(*pair, flops=flops)[0] for *pair, flops in zip(totals, moving, (10**4, 2 * 10**10))
    ]
    moving = [lax.ppermute(total, axes, second) for total in totals]
    dense = list(dense_after(received, sent, operands))
    moving[0], dense[-1] = lax.optimization_barrier((moving[0], dense[-1]))
    own = [add(*pair, scale=0.5)[0] for pair in zip(totals, moving)]
    rest = [lax.ppermute(part, "group", swap) for part in own]
    done = ()
    for pieces, coeffs in (
        (((False, 0), (False, 1), (True, 0)), (*own, rest[0])),
        (((True, 1),), rest[1:]),
    ):
        olds = [old_rest if other else old_own for other, _ in pieces]
        done = embed_pieces(pieces, stack, moment, coeffs, olds, done)
    embed_next, coeff_moved = done

    attn_in_next, attn_out_next, ffn_in_next, ffn_out_next, moved, small_next, small_moved = dense
    return (
        attn_in_next,
        attn_out_next,
        ffn_in_next,
        ffn_out_next.T,
        moved.reshape(dense_old.shape),
        small_next,
        small_moved[0],
        embed_next,
        coeff_moved,
    )


def is_paired(mesh, shapes):
    attn_in, attn_out, ffn_in, ffn_out = (shape[1:] for shape in shapes[:4])
    rows = ffn_in[0]
    return (
        mesh.shape["group"] == 2
        and mesh.shape["shard"] == 4
        and attn_in == (rows, 4 * LANES + HALF)
        and attn_out == (rows, LANES + HALF)
        and ffn_in[1] == 6 * LANES
        and ffn_out == (6 * LANES, rows)
        and rows == LANES + HALF
        and shapes[7][0] <= 8 * LANES
        and shapes[10][1] % (8 * LANES) == 0
    )


def solution(mesh):
    placed = (
        P("group", "shard", "tensor"),
        P("group", "shard", "tensor"),
        P("group", "shard", "tensor"),
        P("group", "shard", "tensor"),
        P("group", None),
        P(("shard", "tensor"), "group"),
        P(("shard", "tensor"), "group"),
        P("group"),
        P("group"),
        P("group", "shard", "tensor"),
        P("shard", "tensor"),
        P("shard", None),
        P(None, "tensor"),
    )

    def shards(*args):
        plan = paired if is_paired(mesh, [arg.shape for arg in args]) else general
        return plan(*args)

    return jax.shard_map(
        shards,
        mesh=mesh,
        in_specs=placed,
        out_specs=(
            P("shard", "tensor"),
            P("shard", "tensor"),
            P("shard", "tensor"),
            P("shard", "tensor"),
            P(("shard", "tensor"), "group"),
            P(),
            P("group"),
            P("shard", "tensor"),
            P(None, "tensor"),
        ),
        check_vma=False,
    )
```

```python
import functools

import jax
import jax.numpy as jnp
from jax import lax
from jax.experimental import pallas as pl
from jax.experimental.pallas import tpu as pltpu
from jax.sharding import PartitionSpec as P

momentum_coef = 0.5
outer_rate = 0.7

f32 = jnp.float32
bf16 = jnp.bfloat16
LANES = 128
HALF = LANES // 2


def nesterov(old_value, momentum, delta):
    moved = momentum_coef * momentum + delta
    return (old_value - outer_rate * (delta + momentum_coef * moved), moved)


def general(
    attn_in_local,
    attn_out_local,
    ffn_in_local,
    ffn_out_local,
    small_local,
    dense_old,
    dense_momentum,
    small_old,
    small_momentum,
    embed_local,
    embed_old,
    basis,
    coeff_momentum,
):
    groups = lax.axis_size("group")
    matrices = (attn_in_local, attn_out_local, ffn_in_local, ffn_out_local)
    local_terms = jnp.concatenate([matrix[0].reshape(-1) for matrix in matrices]).astype(f32)
    small_terms = small_local[0].astype(f32)
    old_flat = dense_old[0]
    momentum_flat = dense_momentum[0]
    dense_part, small_part = (
        lax.psum_scatter(local_terms, "group", scatter_dimension=0, tiled=True),
        lax.psum_scatter(small_terms, "group", scatter_dimension=0, tiled=True),
    )
    dense_new, dense_moved = nesterov(old_flat, momentum_flat, old_flat - dense_part / groups)
    small_new, small_moved = nesterov(small_old, small_momentum, small_old - small_part / groups)
    full_flat, small_next = (
        lax.all_gather(dense_new, "group", axis=0, tiled=True),
        lax.all_gather(small_new, "group", axis=0, tiled=True),
    )
    results = []
    offset = 0
    for matrix in matrices:
        block_size = matrix.shape[1] * matrix.shape[2]
        results.append(
            full_flat[offset : offset + block_size].reshape(matrix.shape[1], matrix.shape[2])
        )
        offset = offset + block_size
    difference = embed_old - embed_local[0].astype(f32)
    partial_coeff = lax.dot_general(
        basis,
        difference,
        (((0,), (0,)), ((), ())),
        precision=lax.Precision.HIGHEST,
        preferred_element_type=f32,
    )
    coeff = lax.psum(partial_coeff, ("group", "shard")) / groups
    coeff_moved = momentum_coef * coeff_momentum + coeff
    update = coeff + momentum_coef * coeff_moved
    embed_next = embed_old - outer_rate * jnp.dot(
        basis, update, precision=lax.Precision.HIGHEST, preferred_element_type=f32
    )
    return (
        results[0],
        results[1],
        results[2],
        results[3],
        dense_moved[None, :],
        small_next,
        small_moved,
        embed_next,
        coeff_moved,
    )


local_coef = outer_rate * (1 + momentum_coef) / 2
old_coef = 1 - outer_rate * (1 + momentum_coef)
mom_coef = -outer_rate * momentum_coef * momentum_coef


def split(value):
    high = value.astype(bf16)
    return high, (value - high.astype(f32)).astype(bf16)


CHUNKS = 2
ROW_CUTS = 2
WHOLE = pl.BlockSpec(memory_space=pltpu.VMEM)
ANY = pl.BlockSpec(memory_space=pl.ANY)


def in_hbm(arrays):
    return [pltpu.with_memory_space_constraint(array, pltpu.HBM) for array in arrays]


def turned(chip):
    return (chip ^ (chip >> 1)) & 1


def side_start(other, columns):
    side = lax.axis_index("group") ^ turned(lax.axis_index("shard"))
    return (1 - side if other else side) * columns


def product(basis, local, old):
    rank = basis.shape[0]
    high, low = split(basis)
    diff_high, diff_low = split(old - local.astype(f32))
    first = jnp.dot(
        jnp.concatenate([high, low], axis=0), diff_high, preferred_element_type=f32
    )
    return first[:rank] + first[rank:] + jnp.dot(high, diff_low, preferred_element_type=f32)


def first_kernel(basis_hbm, local_hbm, old_hbm, out_ref, basis_ref, local_ref, old_ref, sems):
    block = out_ref.shape[1]
    start = side_start(True, CHUNKS * block)
    there = pl.ds(pl.multiple_of(start, block), block)
    rows = old_hbm.shape[0] // ROW_CUTS
    copies = [pltpu.make_async_copy(basis_hbm, basis_ref, sems.at[0])]
    for k in range(ROW_CUTS):
        cut = pl.ds(k * rows, rows)
        for source, target in ((old_hbm, old_ref), (local_hbm, local_ref)):
            at = sems.at[len(copies)]
            copies.append(pltpu.make_async_copy(source.at[cut, there], target.at[cut, :], at))
    for copy in copies:
        copy.start()
    for copy in copies:
        copy.wait()
    out_ref[...] = product(basis_ref[...], local_ref[...], old_ref[...])


def first_part(basis_t, local, old):
    rank, depth = basis_t.shape
    block = old.shape[1] // (2 * CHUNKS)
    return pl.pallas_call(
        first_kernel,
        in_specs=[ANY] * 3,
        out_specs=WHOLE,
        out_shape=jax.ShapeDtypeStruct((rank, block), f32),
        scratch_shapes=[
            pltpu.VMEM((rank, depth), f32),
            pltpu.VMEM((depth, block), bf16),
            pltpu.VMEM((depth, block), f32),
            pltpu.SemaphoreType.DMA((1 + 2 * ROW_CUTS,)),
        ],
        compiler_params=pltpu.CompilerParams(vmem_limit_bytes=4 * 2**20),
        cost_estimate=pl.CostEstimate(
            flops=6 * rank * depth * block, bytes_accessed=6 * depth * block, transcendentals=0
        ),
        name="first_part",
    )(*in_hbm((basis_t, local, old)))


def other_kernel(basis_ref, local_ref, old_ref, rest_ref, *refs):
    *out_refs, stack_ref = refs
    basis = basis_ref[...]
    block = rest_ref.shape[1]
    columns = CHUNKS * block
    places = [(True, k) for k in range(1, CHUNKS)] + [(False, k) for k in range(CHUNKS)]
    for (other, k), out_ref in zip(places, (rest_ref, *out_refs)):
        there = pl.ds(pl.multiple_of(side_start(other, columns) + k * block, block), block)
        out_ref[...] = product(basis, local_ref[:, there], old_ref[:, there])
    high = basis.astype(bf16).astype(f32)
    stack_ref[...] = jnp.concatenate([high, basis - high, high], axis=0).T.astype(bf16)


def other_parts(basis_t, local, old):
    rank, depth = basis_t.shape
    block = old.shape[1] // (2 * CHUNKS)
    return pl.pallas_call(
        other_kernel,
        in_specs=[WHOLE] * 3,
        out_specs=[WHOLE] * (2 * CHUNKS),
        out_shape=[jax.ShapeDtypeStruct((rank, block), f32)] * (2 * CHUNKS - 1)
        + [jax.ShapeDtypeStruct((depth, 3 * rank), bf16)],
        compiler_params=pltpu.CompilerParams(vmem_limit_bytes=4 * 2**20),
        cost_estimate=pl.CostEstimate(
            flops=10**10, bytes_accessed=18 * depth * block, transcendentals=0
        ),
        name="other_parts",
    )(basis_t, local, old)


def add_kernel(scale, first_ref, second_ref, *refs):
    refs[-1][...] = scale * (first_ref[...] + second_ref[...])


def add(first, second, after=(), scale=1.0, flops=2 * 10**10):
    return pl.pallas_call(
        functools.partial(add_kernel, scale),
        in_specs=[WHOLE] * 2 + [ANY] * len(after),
        out_specs=WHOLE,
        out_shape=jax.ShapeDtypeStruct(first.shape, f32),
        compiler_params=pltpu.CompilerParams(vmem_limit_bytes=2 * 2**20),
        cost_estimate=pl.CostEstimate(flops=flops, bytes_accessed=0, transcendentals=0),
        name="add",
    )(first, second, *after)


def embed_piece(start, width, coeff, stack_ref, moment_ref, old_ref):
    there = pl.ds(pl.multiple_of(start, width), width)
    moved = momentum_coef * moment_ref[:, there] + coeff
    up_high, up_low = split(coeff + momentum_coef * moved)
    change = jnp.dot(
        stack_ref[...],
        jnp.concatenate([up_high, up_high, up_low], axis=0),
        preferred_element_type=f32,
    )
    return old_ref[:, there] - outer_rate * change, moved


def early_kernel(stack_ref, moment_ref, old_ref, coeff_ref, embed_ref, moved_ref):
    start = side_start(False, old_ref.shape[1] // 2)
    embed_ref[...], moved_ref[...] = embed_piece(
        start, coeff_ref.shape[1], coeff_ref[...], stack_ref, moment_ref, old_ref
    )


def embed_early(stack, moment, old, coeff):
    depth, (rank, width) = old.shape[0], coeff.shape
    return pl.pallas_call(
        early_kernel,
        in_specs=[WHOLE] * 4,
        out_specs=[WHOLE] * 2,
        out_shape=[
            jax.ShapeDtypeStruct((depth, width), f32),
            jax.ShapeDtypeStruct((rank, width), f32),
        ],
        compiler_params=pltpu.CompilerParams(vmem_limit_bytes=4 * 2**20),
        cost_estimate=pl.CostEstimate(
            flops=6 * rank * depth * width, bytes_accessed=8 * depth * width, transcendentals=0
        ),
        name="embed_early",
    )(stack, moment, old, coeff)


def embed_kernel(pieces, ready, stack_ref, moment_ref, old_ref, *refs):
    count = len(pieces)
    coeffs, refs = refs[:count], refs[count:]
    embed_hbm, moved_hbm, embed_ref, moved_ref, sems = refs[-5:]
    width = coeffs[0].shape[1]
    copies = []

    def start_of(other, part):
        return side_start(other, old_ref.shape[1] // 2) + part * width

    def send(start, embed, moved):
        there = pl.ds(pl.multiple_of(start, width), width)
        for source, target in ((moved, moved_hbm), (embed, embed_hbm)):
            copies.append(
                pltpu.make_async_copy(source, target.at[:, there], sems.at[len(copies)])
            )
            copies[-1].start()

    if ready:
        send(start_of(*ready), refs[0], refs[1])
    for k, piece in enumerate(pieces):
        start = start_of(*piece)
        embed_ref[k], moved_ref[k] = embed_piece(
            start, width, coeffs[k][...], stack_ref, moment_ref, old_ref
        )
        send(start, embed_ref.at[k], moved_ref.at[k])
    for copy in copies:
        copy.wait()


def embed_pieces(pieces, ready, stack, moment, old, coeffs, early, before):
    count = len(pieces)
    rank, width = coeffs[0].shape
    first = 3 + count + len(early)
    return pl.pallas_call(
        functools.partial(embed_kernel, pieces, ready),
        in_specs=[WHOLE] * first + [ANY] * len(before),
        out_specs=[ANY, ANY],
        out_shape=[
            jax.ShapeDtypeStruct(old.shape, f32),
            jax.ShapeDtypeStruct(moment.shape, f32),
        ],
        scratch_shapes=[
            pltpu.VMEM((count, old.shape[0], width), f32),
            pltpu.VMEM((count, rank, width), f32),
            pltpu.SemaphoreType.DMA((2 * count + len(early),)),
        ],
        input_output_aliases={first: 0, first + 1: 1} if before else {},
        compiler_params=pltpu.CompilerParams(vmem_limit_bytes=8 * 2**20),
        cost_estimate=pl.CostEstimate(
            flops=6 * count * rank * old.shape[0] * width,
            bytes_accessed=8 * count * old.shape[0] * width,
            transcendentals=0,
        ),
        name="embed_pieces",
    )(stack, moment, old, *coeffs, *early, *before)


def low_lanes(rows):
    return lax.broadcasted_iota(jnp.int32, (rows, LANES), 1) < HALF


def turn(value):
    return pltpu.roll(value, HALF, 1)


def attn_tiles(in_ref, out_ref):
    whole = in_ref.shape[-1] // LANES
    tiles = [in_ref[0, :, k * LANES : (k + 1) * LANES].astype(f32) for k in range(whole)]
    last = in_ref[0, :, whole * LANES :].astype(f32)
    side = out_ref[0, :, LANES:].astype(f32)
    tiles.append(jnp.concatenate([last, side], axis=-1))
    tiles.append(out_ref[0, :, :LANES].astype(f32))
    return tiles


def unflatten_attn(flat, put, rows):
    pairs = rows // 2
    low = low_lanes(pairs)
    inner = [flat(j, pairs, 9) for j in range(9)]
    base = pairs * 9
    outer = [flat(base + j, pairs, 3) for j in range(3)]
    turned = [turn(inner[j]) for j in range(4, 9)]
    turned_out = [turn(outer[j]) for j in (1, 2)]
    for k in range(4):
        put(0, k, inner[k])
        put(1, k, jnp.where(low, turned[k], turned[k + 1]))
    put(0, 4, jnp.where(low, inner[4], turned_out[0]))
    put(1, 4, jnp.where(low, turned[4], outer[2]))
    put(0, 5, outer[0])
    put(1, 5, jnp.where(low, turned_out[0], turned_out[1]))


def flatten_attn(get, rows):
    pairs = rows // 2
    low = low_lanes(pairs)
    even = [get(0, k) for k in range(6)]
    odd = [get(1, k) for k in range(6)]
    turned = [turn(odd[k]) for k in range(5)]
    pieces = [(k, 9, even[k]) for k in range(4)]
    pieces.append((4, 9, jnp.where(low, even[4], turned[0])))
    for k in range(4):
        pieces.append((5 + k, 9, jnp.where(low, turned[k], turned[k + 1])))
    base = pairs * 9
    pieces.append((base, 3, even[5]))
    turned_out = turn(odd[5])
    pieces.append((base + 1, 3, jnp.where(low, turn(even[4]), turned_out)))
    pieces.append((base + 2, 3, jnp.where(low, turned_out, odd[4])))
    return pieces


def before_kernel(
    order_ref, moment_hbm, in_ref, out_ref, up_ref, down_ref, old_ref, mom_ref, small_ref,
    small_old_ref, small_mom_ref, send_ref, moment_ref, wide_ref, sem,
):
    del order_ref
    copy = pltpu.make_async_copy(moment_hbm, moment_ref, sem)
    copy.start()
    group = lax.axis_index("group")
    rows = up_ref.shape[1]
    mid = rows // 2
    block = rows + mid
    tiles = up_ref.shape[2] // LANES
    small = small_old_ref.shape[1]

    def flat(start, count, stride):
        at = pl.ds(start, count, stride=stride)
        return old_coef * old_ref[at, :] + mom_coef * mom_ref[at, :]

    def put(start, tile, value):
        send_ref[tile, pl.ds(block + start, rows // 2, stride=2), :] = value

    def put_small(other, own):
        own_terms = (
            old_coef * small_old_ref[...] + mom_coef * small_mom_ref[...] + local_coef * own
        )
        send_ref[:, 2 * block :, :] = jnp.zeros((tiles, 8, LANES), f32)
        for tile, value in enumerate((other, own_terms)):
            for row in range(pl.cdiv(small, LANES)):
                piece = value[:, row * LANES : (row + 1) * LANES]
                at = 2 * block + row
                send_ref[tile, at : at + 1, : piece.shape[1]] = piece

    @pl.when(group == 0)
    def _():
        unflatten_attn(flat, put, rows)
        for k, value in enumerate(attn_tiles(in_ref, out_ref)):
            send_ref[k, block : block + rows, :] += local_coef * value
        base = rows * tiles
        for k in range(tiles):
            columns = slice(k * LANES, (k + 1) * LANES)
            send_ref[k, :mid, :] = up_ref[0, mid:, columns].astype(f32)
            send_ref[k, mid:block, :] = down_ref[0, :, columns].astype(f32)
            send_ref[k, block + rows : 2 * block, :] = flat(base + k, mid, tiles) + (
                local_coef * up_ref[0, :mid, columns].astype(f32)
            )
        values = small_ref[...].astype(f32)
        put_small(values[:, small:], values[:, :small])

    @pl.when(group == 1)
    def _():
        for k, value in enumerate(attn_tiles(in_ref, out_ref)):
            send_ref[k, :rows, :] = value
        for k in range(tiles):
            columns = slice(k * LANES, (k + 1) * LANES)
            send_ref[k, rows:block, :] = up_ref[0, :mid, columns].astype(f32)
            send_ref[k, block : block + mid, :] = flat(k, mid, tiles) + (
                local_coef * up_ref[0, mid:, columns].astype(f32)
            )
        base = mid * tiles
        pairs = tiles * HALF
        low = low_lanes(pairs)
        first, second, third = (flat(base + j, pairs, 3) for j in range(3))
        turned, turned_more = turn(second), turn(third)
        even, odd = pl.ds(0, pairs, stride=2), pl.ds(1, pairs, stride=2)
        wide_ref[0, even, :] = first
        wide_ref[1, even, :] = second
        wide_ref[0, odd, :] = jnp.where(low, turned, turned_more)
        wide_ref[1, odd, :] = turned_more
        start = block + mid
        for k in range(tiles):
            columns = slice(k * LANES, (k + 1) * LANES)
            upper = wide_ref[0, columns, :].T
            lower = wide_ref[1, columns, :].T[:HALF]
            send_ref[k, start : start + LANES, :] = upper + (
                local_coef * down_ref[0, :LANES, columns].astype(f32)
            )
            send_ref[k, start + LANES : 2 * block, :] = lower + (
                local_coef * down_ref[0, LANES:, columns].astype(f32)
            )
        values = small_ref[...].astype(f32)
        put_small(values[:, :small], values[:, small:])

    copy.wait()


def after_kernel(
    recv_ref, send_ref, in_ref, out_ref, up_ref, down_ref, old_ref, mom_ref, small_ref,
    small_old_ref, small_mom_ref, *refs,
):
    targets, sources, (sum_ref, wide_ref, sems) = refs[:7], refs[7:14], refs[14:]
    (
        in_next_ref, out_next_ref, up_next_ref, down_next_ref, moved_ref, small_next_ref,
        small_moved_ref,
    ) = sources
    copies = [
        pltpu.make_async_copy(source, target, sems.at[k])
        for k, (source, target) in enumerate(zip(sources, targets))
    ]

    def go(*numbers):
        for k in numbers:
            copies[k].start()

    rows = up_ref.shape[1]
    mid = rows // 2
    block = rows + mid
    tiles = up_ref.shape[2] // LANES
    small = small_old_ref.shape[1]
    group = lax.axis_index("group")

    def put_moved(start, stride, value):
        at = pl.ds(start, value.shape[0], stride=stride)
        moved_ref[at, :] = momentum_coef * mom_ref[at, :] + (old_ref[at, :] - 0.5 * value)

    def get(start, tile):
        return sum_ref[tile, pl.ds(start, rows // 2, stride=2), :]

    def put_attn(tile, value):
        whole = in_ref.shape[-1] // LANES
        if tile < whole:
            in_next_ref[:, tile * LANES : (tile + 1) * LANES] = value
        elif tile == whole:
            in_next_ref[:, tile * LANES :] = value[:, :HALF]
            out_next_ref[:, LANES:] = turn(value)[:, :HALF]
        else:
            out_next_ref[:, :LANES] = value

    def small_row(ref, tile):
        pieces = []
        for row in range(pl.cdiv(small, LANES)):
            at = 2 * block + row
            pieces.append(ref[tile, at : at + 1, : min(LANES, small - row * LANES)])
        return jnp.concatenate(pieces, axis=1)

    def put_small(other, own, first):
        theirs = small_row(recv_ref, 0)
        mine = small_row(send_ref, 1) + local_coef * theirs
        rest = small_row(recv_ref, 1) + local_coef * other
        both = [mine, rest] if first else [rest, mine]
        small_next_ref[...] = jnp.concatenate(both, axis=1).reshape(-1)
        small_moved_ref[...] = momentum_coef * small_mom_ref[...] + (
            small_old_ref[...] - 0.5 * (own + theirs)
        )

    @pl.when(group == 0)
    def _():
        for k, value in enumerate(attn_tiles(in_ref, out_ref)):
            theirs = recv_ref[k, :rows, :]
            put_attn(k, send_ref[k, block : block + rows, :] + local_coef * theirs)
            sum_ref[k, :, :] = value + theirs
        go(0, 1)
        for start, stride, value in flatten_attn(get, rows):
            put_moved(start, stride, value)
        base = rows * tiles
        for k in range(tiles):
            columns = slice(k * LANES, (k + 1) * LANES)
            theirs = recv_ref[k, rows:block, :]
            up_next_ref[:mid, columns] = (
                send_ref[k, block + rows : 2 * block, :] + local_coef * theirs
            )
            put_moved(base + k, tiles, up_ref[0, :mid, columns].astype(f32) + theirs)
            up_next_ref[mid:, columns] = recv_ref[k, block : block + mid, :] + (
                local_coef * up_ref[0, mid:, columns].astype(f32)
            )
            down_next_ref[:, columns] = recv_ref[k, block + mid : 2 * block, :] + (
                local_coef * down_ref[0, :, columns].astype(f32)
            )
        go(2, 3, 4)
        values = small_ref[...].astype(f32)
        put_small(values[:, small:], values[:, :small], True)
        go(5, 6)
        for copy in copies:
            copy.wait()

    @pl.when(group == 1)
    def _():
        for k, value in enumerate(attn_tiles(in_ref, out_ref)):
            put_attn(k, recv_ref[k, block : block + rows, :] + local_coef * value)
        go(0, 1)
        for k in range(tiles):
            columns = slice(k * LANES, (k + 1) * LANES)
            up_next_ref[:mid, columns] = recv_ref[k, block + rows : 2 * block, :] + (
                local_coef * up_ref[0, :mid, columns].astype(f32)
            )
            theirs = recv_ref[k, :mid, :]
            up_next_ref[mid:, columns] = send_ref[k, block : block + mid, :] + local_coef * theirs
            put_moved(k, tiles, up_ref[0, mid:, columns].astype(f32) + theirs)
            theirs = recv_ref[k, mid:block, :]
            down_next_ref[:, columns] = (
                send_ref[k, block + mid : 2 * block, :] + local_coef * theirs
            )
            total = down_ref[0, :, columns].astype(f32) + theirs
            wide_ref[0, columns, :] = total[:LANES].T
            lower = jnp.concatenate([total[LANES:], total[LANES:]], axis=0)
            wide_ref[1, columns, :] = lower.T
        go(2, 3)
        base = mid * tiles
        pairs = tiles * HALF
        low = low_lanes(pairs)
        even, odd = pl.ds(0, pairs, stride=2), pl.ds(1, pairs, stride=2)
        odd_first = turn(wide_ref[0, odd, :])
        put_moved(base, 3, wide_ref[0, even, :])
        put_moved(base + 1, 3, jnp.where(low, wide_ref[1, even, :], odd_first))
        put_moved(base + 2, 3, jnp.where(low, odd_first, wide_ref[1, odd, :]))
        go(4)
        values = small_ref[...].astype(f32)
        put_small(values[:, :small], values[:, small:], False)
        go(5, 6)
        for copy in copies:
            copy.wait()


def dense_before(order, moment, operands):
    _, rows, width = operands[2].shape
    return pl.pallas_call(
        before_kernel,
        in_specs=[ANY] * 2 + [WHOLE] * 9,
        out_specs=[WHOLE] * 2,
        out_shape=[
            jax.ShapeDtypeStruct((width // LANES, 3 * rows + 8, LANES), f32),
            jax.ShapeDtypeStruct(moment.shape, f32),
        ],
        scratch_shapes=[pltpu.VMEM((2, width, LANES), f32), pltpu.SemaphoreType.DMA],
        compiler_params=pltpu.CompilerParams(vmem_limit_bytes=4 * 2**20),
        cost_estimate=pl.CostEstimate(
            flops=60000 * rows * width, bytes_accessed=30 * rows * width, transcendentals=0
        ),
        name="dense_before",
    )(order, *in_hbm([moment]), *operands)


def dense_after(received, sent, operands):
    _, rows, width = operands[2].shape
    outs = [matrix.shape[1:] for matrix in operands[:4]]
    outs += [operands[4].shape, operands[6].shape[1:], operands[7].shape]
    return pl.pallas_call(
        after_kernel,
        in_specs=[WHOLE] * 11,
        out_specs=[ANY] * 7,
        out_shape=[jax.ShapeDtypeStruct(shape, f32) for shape in outs],
        scratch_shapes=[pltpu.VMEM(shape, f32) for shape in outs]
        + [
            pltpu.VMEM((width // LANES, rows, LANES), f32),
            pltpu.VMEM((2, width, LANES), f32),
            pltpu.SemaphoreType.DMA((7,)),
        ],
        compiler_params=pltpu.CompilerParams(vmem_limit_bytes=8 * 2**20),
        cost_estimate=pl.CostEstimate(
            flops=60000 * rows * width, bytes_accessed=40 * rows * width, transcendentals=0
        ),
        name="dense_after",
    )(received, sent, *operands)


def paired(
    attn_in_local,
    attn_out_local,
    ffn_in_local,
    ffn_out_local,
    small_local,
    dense_old,
    dense_momentum,
    small_old,
    small_momentum,
    embed_local,
    embed_old,
    basis,
    coeff_momentum,
):
    swap = [(0, 1), (1, 0)]
    chips = lax.axis_size("shard")

    first, second = (
        [
            (core * chips + chip, (1 - core) * chips + (chip ^ (1 + (core ^ turned(chip) ^ late))))
            for core in range(2)
            for chip in range(chips)
        ]
        for late in range(2)
    )
    axes = ("group", "shard")

    embed = (basis.T, embed_local[0], embed_old)
    theirs = [lax.ppermute(first_part(*embed), "group", swap)]
    late, *mine, stack = other_parts(*embed)
    theirs.append(lax.ppermute(late, "group", swap))

    operands = (
        attn_in_local,
        attn_out_local,
        ffn_in_local,
        jnp.swapaxes(ffn_out_local, 1, 2),
        dense_old.reshape(-1, LANES),
        dense_momentum.reshape(-1, LANES),
        small_local,
        small_old[None, :],
        small_momentum[None, :],
    )
    totals = [add(*pair, flops=10**4) for pair in zip(mine, theirs)]
    moving = [lax.ppermute(total, axes, first) for total in totals]
    sent, moment = dense_before(totals[0], coeff_momentum, operands)
    received = lax.ppermute(sent, "group", swap)
    totals = [
        add(*pair, flops=flops) for *pair, flops in zip(totals, moving, (10**4, 2 * 10**10))
    ]
    moving = [lax.ppermute(total, axes, second) for total in totals]
    dense = list(dense_after(received, sent, operands))
    moving[0], dense[-1] = lax.optimization_barrier((moving[0], dense[-1]))
    own = [add(totals[0], moving[0], scale=0.5)]
    rest = [lax.ppermute(own[0], "group", swap)]
    early = embed_early(stack, moment, embed_old, own[0])
    own.append(add(totals[1], moving[1], early[:1], scale=0.5))
    rest.append(lax.ppermute(own[1], "group", swap))
    shared = (stack, moment, embed_old)
    done = embed_pieces(
        ((False, 1), (True, 0)), (False, 0), *shared, (own[1], rest[0]), early, ()
    )
    done = embed_pieces(((True, 1),), None, *shared, rest[1:], (), done)
    embed_next, coeff_moved = done

    attn_in_next, attn_out_next, ffn_in_next, ffn_out_next, moved, small_next, small_moved = dense
    return (
        attn_in_next,
        attn_out_next,
        ffn_in_next,
        ffn_out_next.T,
        moved.reshape(dense_old.shape),
        small_next,
        small_moved[0],
        embed_next,
        coeff_moved,
    )


def is_paired(mesh, shapes):
    attn_in, attn_out, ffn_in, ffn_out = (shape[1:] for shape in shapes[:4])
    rows = ffn_in[0]
    return (
        mesh.shape["group"] == 2
        and mesh.shape["shard"] == 4
        and attn_in == (rows, 4 * LANES + HALF)
        and attn_out == (rows, LANES + HALF)
        and ffn_in[1] == 6 * LANES
        and ffn_out == (6 * LANES, rows)
        and rows == LANES + HALF
        and shapes[7][0] <= 8 * LANES
        and shapes[10][1] % (8 * LANES) == 0
    )


def solution(mesh):
    placed = (
        P("group", "shard", "tensor"),
        P("group", "shard", "tensor"),
        P("group", "shard", "tensor"),
        P("group", "shard", "tensor"),
        P("group", None),
        P(("shard", "tensor"), "group"),
        P(("shard", "tensor"), "group"),
        P("group"),
        P("group"),
        P("group", "shard", "tensor"),
        P("shard", "tensor"),
        P("shard", None),
        P(None, "tensor"),
    )

    def shards(*args):
        plan = paired if is_paired(mesh, [arg.shape for arg in args]) else general
        return plan(*args)

    return jax.shard_map(
        shards,
        mesh=mesh,
        in_specs=placed,
        out_specs=(
            P("shard", "tensor"),
            P("shard", "tensor"),
            P("shard", "tensor"),
            P("shard", "tensor"),
            P(("shard", "tensor"), "group"),
            P(),
            P("group"),
            P("shard", "tensor"),
            P(None, "tensor"),
        ),
        check_vma=False,
    )
```

```python
import functools

import jax
import jax.numpy as jnp
from jax import lax
from jax.experimental import pallas as pl
from jax.experimental.pallas import tpu as pltpu
from jax.sharding import PartitionSpec as P

momentum_coef = 0.5
outer_rate = 0.7

f32 = jnp.float32
bf16 = jnp.bfloat16
LANES = 128
HALF = LANES // 2


def nesterov(old_value, momentum, delta):
    moved = momentum_coef * momentum + delta
    return (old_value - outer_rate * (delta + momentum_coef * moved), moved)


def general(
    attn_in_local,
    attn_out_local,
    ffn_in_local,
    ffn_out_local,
    small_local,
    dense_old,
    dense_momentum,
    small_old,
    small_momentum,
    embed_local,
    embed_old,
    basis,
    coeff_momentum,
):
    groups = lax.axis_size("group")
    matrices = (attn_in_local, attn_out_local, ffn_in_local, ffn_out_local)
    local_terms = jnp.concatenate([matrix[0].reshape(-1) for matrix in matrices]).astype(f32)
    small_terms = small_local[0].astype(f32)
    old_flat = dense_old[0]
    momentum_flat = dense_momentum[0]
    dense_part, small_part = (
        lax.psum_scatter(local_terms, "group", scatter_dimension=0, tiled=True),
        lax.psum_scatter(small_terms, "group", scatter_dimension=0, tiled=True),
    )
    dense_new, dense_moved = nesterov(old_flat, momentum_flat, old_flat - dense_part / groups)
    small_new, small_moved = nesterov(small_old, small_momentum, small_old - small_part / groups)
    full_flat, small_next = (
        lax.all_gather(dense_new, "group", axis=0, tiled=True),
        lax.all_gather(small_new, "group", axis=0, tiled=True),
    )
    results = []
    offset = 0
    for matrix in matrices:
        block_size = matrix.shape[1] * matrix.shape[2]
        results.append(
            full_flat[offset : offset + block_size].reshape(matrix.shape[1], matrix.shape[2])
        )
        offset = offset + block_size
    difference = embed_old - embed_local[0].astype(f32)
    partial_coeff = lax.dot_general(
        basis,
        difference,
        (((0,), (0,)), ((), ())),
        precision=lax.Precision.HIGHEST,
        preferred_element_type=f32,
    )
    coeff = lax.psum(partial_coeff, ("group", "shard")) / groups
    coeff_moved = momentum_coef * coeff_momentum + coeff
    update = coeff + momentum_coef * coeff_moved
    embed_next = embed_old - outer_rate * jnp.dot(
        basis, update, precision=lax.Precision.HIGHEST, preferred_element_type=f32
    )
    return (
        results[0],
        results[1],
        results[2],
        results[3],
        dense_moved[None, :],
        small_next,
        small_moved,
        embed_next,
        coeff_moved,
    )


local_coef = outer_rate * (1 + momentum_coef) / 2
old_coef = 1 - outer_rate * (1 + momentum_coef)
mom_coef = -outer_rate * momentum_coef * momentum_coef


def split(value):
    high = value.astype(bf16)
    return high, (value - high.astype(f32)).astype(bf16)


CHUNKS = 2
WHOLE = pl.BlockSpec(memory_space=pltpu.VMEM)
ANY = pl.BlockSpec(memory_space=pl.ANY)


def in_hbm(arrays):
    return [pltpu.with_memory_space_constraint(array, pltpu.HBM) for array in arrays]


def turned(chip):
    return (chip ^ (chip >> 1)) & 1


def side_start(other, columns):
    side = lax.axis_index("group") ^ turned(lax.axis_index("shard"))
    return (1 - side if other else side) * columns


def product(basis, local, old):
    rank = basis.shape[0]
    high, low = split(basis)
    diff_high, diff_low = split(old - local.astype(f32))
    first = jnp.dot(
        jnp.concatenate([high, low], axis=0), diff_high, preferred_element_type=f32
    )
    return first[:rank] + first[rank:] + jnp.dot(high, diff_low, preferred_element_type=f32)


def first_kernel(basis_hbm, local_hbm, old_hbm, out_ref, *refs):
    *held, sems = refs
    columns = out_ref.shape[1]
    there = pl.ds(pl.multiple_of(side_start(True, CHUNKS * columns), columns), columns)
    sources = (basis_hbm, local_hbm.at[:, there], old_hbm.at[:, there])
    copies = [
        pltpu.make_async_copy(source, target, sems.at[k])
        for k, (source, target) in enumerate(zip(sources, held))
    ]
    for copy in copies:
        copy.start()
    for copy in copies:
        copy.wait()
    out_ref[...] = product(*(ref[...] for ref in held))


def first_part(basis_t, local, old):
    rank, depth = basis_t.shape
    block = old.shape[1] // (2 * CHUNKS)
    return pl.pallas_call(
        first_kernel,
        in_specs=[ANY] * 3,
        out_specs=WHOLE,
        out_shape=jax.ShapeDtypeStruct((rank, block), f32),
        scratch_shapes=[
            pltpu.VMEM((rank, depth), f32),
            pltpu.VMEM((depth, block), bf16),
            pltpu.VMEM((depth, block), f32),
            pltpu.SemaphoreType.DMA((3,)),
        ],
        compiler_params=pltpu.CompilerParams(vmem_limit_bytes=4 * 2**20),
        cost_estimate=pl.CostEstimate(
            flops=6 * rank * depth * block, bytes_accessed=6 * depth * block, transcendentals=0
        ),
        name="first_part",
    )(*in_hbm((basis_t, local, old)))


def other_kernel(basis_ref, local_ref, old_ref, rest_ref, *refs):
    *out_refs, stack_ref = refs
    basis = basis_ref[...]
    block = rest_ref.shape[1]
    columns = CHUNKS * block
    places = [(True, k) for k in range(1, CHUNKS)] + [(False, k) for k in range(CHUNKS)]
    for (other, k), out_ref in zip(places, (rest_ref, *out_refs)):
        there = pl.ds(pl.multiple_of(side_start(other, columns) + k * block, block), block)
        out_ref[...] = product(basis, local_ref[:, there], old_ref[:, there])
    high = basis.astype(bf16).astype(f32)
    stack_ref[...] = jnp.concatenate([high, basis - high, high], axis=0).T.astype(bf16)


def other_parts(basis_t, local, old):
    rank, depth = basis_t.shape
    block = old.shape[1] // (2 * CHUNKS)
    return pl.pallas_call(
        other_kernel,
        in_specs=[WHOLE] * 3,
        out_specs=[WHOLE] * (2 * CHUNKS),
        out_shape=[jax.ShapeDtypeStruct((rank, block), f32)] * (2 * CHUNKS - 1)
        + [jax.ShapeDtypeStruct((depth, 3 * rank), bf16)],
        compiler_params=pltpu.CompilerParams(vmem_limit_bytes=4 * 2**20),
        cost_estimate=pl.CostEstimate(
            flops=10**10, bytes_accessed=18 * depth * block, transcendentals=0
        ),
        name="other_parts",
    )(basis_t, local, old)


def add_kernel(scale, first_ref, second_ref, *refs):
    refs[-1][...] = scale * (first_ref[...] + second_ref[...])


def add(first, second, after=(), scale=1.0, flops=2 * 10**10):
    return pl.pallas_call(
        functools.partial(add_kernel, scale),
        in_specs=[WHOLE] * 2 + [ANY] * len(after),
        out_specs=WHOLE,
        out_shape=jax.ShapeDtypeStruct(first.shape, f32),
        compiler_params=pltpu.CompilerParams(vmem_limit_bytes=2 * 2**20),
        cost_estimate=pl.CostEstimate(flops=flops, bytes_accessed=0, transcendentals=0),
        name="add",
    )(first, second, *after)


def embed_piece(start, width, coeff, stack_ref, moment_ref, old_ref):
    there = pl.ds(pl.multiple_of(start, width), width)
    moved = momentum_coef * moment_ref[:, there] + coeff
    up_high, up_low = split(coeff + momentum_coef * moved)
    change = jnp.dot(
        stack_ref[...],
        jnp.concatenate([up_high, up_high, up_low], axis=0),
        preferred_element_type=f32,
    )
    return old_ref[:, there] - outer_rate * change, moved


def early_kernel(stack_ref, moment_ref, old_ref, coeff_ref, embed_ref, moved_ref):
    start = side_start(False, old_ref.shape[1] // 2)
    embed_ref[...], moved_ref[...] = embed_piece(
        start, coeff_ref.shape[1], coeff_ref[...], stack_ref, moment_ref, old_ref
    )


def embed_early(stack, moment, old, coeff):
    depth, (rank, width) = old.shape[0], coeff.shape
    return pl.pallas_call(
        early_kernel,
        in_specs=[WHOLE] * 4,
        out_specs=[WHOLE] * 2,
        out_shape=[
            jax.ShapeDtypeStruct((depth, width), f32),
            jax.ShapeDtypeStruct((rank, width), f32),
        ],
        compiler_params=pltpu.CompilerParams(vmem_limit_bytes=4 * 2**20),
        cost_estimate=pl.CostEstimate(
            flops=6 * rank * depth * width, bytes_accessed=8 * depth * width, transcendentals=0
        ),
        name="embed_early",
    )(stack, moment, old, coeff)


def embed_kernel(pieces, ready, stack_ref, moment_ref, old_ref, *refs):
    count = len(pieces)
    coeffs, refs = refs[:count], refs[count:]
    embed_hbm, moved_hbm, embed_ref, moved_ref, sems = refs[-5:]
    width = coeffs[0].shape[1]
    copies = []

    def start_of(other, part):
        return side_start(other, old_ref.shape[1] // 2) + part * width

    def send(start, embed, moved):
        there = pl.ds(pl.multiple_of(start, width), width)
        for source, target in ((moved, moved_hbm), (embed, embed_hbm)):
            copies.append(
                pltpu.make_async_copy(source, target.at[:, there], sems.at[len(copies)])
            )
            copies[-1].start()

    if ready:
        send(start_of(*ready), refs[0], refs[1])
    for k, piece in enumerate(pieces):
        start = start_of(*piece)
        embed_ref[k], moved_ref[k] = embed_piece(
            start, width, coeffs[k][...], stack_ref, moment_ref, old_ref
        )
        send(start, embed_ref.at[k], moved_ref.at[k])
    for copy in copies:
        copy.wait()


def embed_pieces(pieces, ready, stack, moment, old, coeffs, early, before):
    count = len(pieces)
    rank, width = coeffs[0].shape
    first = 3 + count + len(early)
    return pl.pallas_call(
        functools.partial(embed_kernel, pieces, ready),
        in_specs=[WHOLE] * first + [ANY] * len(before),
        out_specs=[ANY, ANY],
        out_shape=[
            jax.ShapeDtypeStruct(old.shape, f32),
            jax.ShapeDtypeStruct(moment.shape, f32),
        ],
        scratch_shapes=[
            pltpu.VMEM((count, old.shape[0], width), f32),
            pltpu.VMEM((count, rank, width), f32),
            pltpu.SemaphoreType.DMA((2 * count + len(early),)),
        ],
        input_output_aliases={first: 0, first + 1: 1} if before else {},
        compiler_params=pltpu.CompilerParams(vmem_limit_bytes=8 * 2**20),
        cost_estimate=pl.CostEstimate(
            flops=6 * count * rank * old.shape[0] * width,
            bytes_accessed=8 * count * old.shape[0] * width,
            transcendentals=0,
        ),
        name="embed_pieces",
    )(stack, moment, old, *coeffs, *early, *before)


def low_lanes(rows):
    return lax.broadcasted_iota(jnp.int32, (rows, LANES), 1) < HALF


def turn(value):
    return pltpu.roll(value, HALF, 1)


def attn_tiles(in_ref, out_ref):
    whole = in_ref.shape[-1] // LANES
    tiles = [in_ref[0, :, k * LANES : (k + 1) * LANES].astype(f32) for k in range(whole)]
    last = in_ref[0, :, whole * LANES :].astype(f32)
    side = out_ref[0, :, LANES:].astype(f32)
    tiles.append(jnp.concatenate([last, side], axis=-1))
    tiles.append(out_ref[0, :, :LANES].astype(f32))
    return tiles


def unflatten_attn(flat, put, rows):
    pairs = rows // 2
    low = low_lanes(pairs)
    inner = [flat(j, pairs, 9) for j in range(9)]
    base = pairs * 9
    outer = [flat(base + j, pairs, 3) for j in range(3)]
    turned = [turn(inner[j]) for j in range(4, 9)]
    turned_out = [turn(outer[j]) for j in (1, 2)]
    for k in range(4):
        put(0, k, inner[k])
        put(1, k, jnp.where(low, turned[k], turned[k + 1]))
    put(0, 4, jnp.where(low, inner[4], turned_out[0]))
    put(1, 4, jnp.where(low, turned[4], outer[2]))
    put(0, 5, outer[0])
    put(1, 5, jnp.where(low, turned_out[0], turned_out[1]))


def flatten_attn(get, rows):
    pairs = rows // 2
    low = low_lanes(pairs)
    even = [get(0, k) for k in range(6)]
    odd = [get(1, k) for k in range(6)]
    turned = [turn(odd[k]) for k in range(5)]
    pieces = [(k, 9, even[k]) for k in range(4)]
    pieces.append((4, 9, jnp.where(low, even[4], turned[0])))
    for k in range(4):
        pieces.append((5 + k, 9, jnp.where(low, turned[k], turned[k + 1])))
    base = pairs * 9
    pieces.append((base, 3, even[5]))
    turned_out = turn(odd[5])
    pieces.append((base + 1, 3, jnp.where(low, turn(even[4]), turned_out)))
    pieces.append((base + 2, 3, jnp.where(low, turned_out, odd[4])))
    return pieces


def before_kernel(
    order_ref, in_ref, out_ref, up_ref, down_ref, old_ref, mom_ref, small_ref, small_old_ref,
    small_mom_ref, send_ref, wide_ref,
):
    del order_ref
    group = lax.axis_index("group")
    rows = up_ref.shape[1]
    mid = rows // 2
    block = rows + mid
    tiles = up_ref.shape[2] // LANES
    small = small_old_ref.shape[1]

    def flat(start, count, stride):
        at = pl.ds(start, count, stride=stride)
        return old_coef * old_ref[at, :] + mom_coef * mom_ref[at, :]

    def put(start, tile, value):
        send_ref[tile, pl.ds(block + start, rows // 2, stride=2), :] = value

    def put_small(other, own):
        own_terms = (
            old_coef * small_old_ref[...] + mom_coef * small_mom_ref[...] + local_coef * own
        )
        send_ref[:, 2 * block :, :] = jnp.zeros((tiles, 8, LANES), f32)
        for tile, value in enumerate((other, own_terms)):
            for row in range(pl.cdiv(small, LANES)):
                piece = value[:, row * LANES : (row + 1) * LANES]
                at = 2 * block + row
                send_ref[tile, at : at + 1, : piece.shape[1]] = piece

    @pl.when(group == 0)
    def _():
        unflatten_attn(flat, put, rows)
        for k, value in enumerate(attn_tiles(in_ref, out_ref)):
            send_ref[k, block : block + rows, :] += local_coef * value
        base = rows * tiles
        for k in range(tiles):
            columns = slice(k * LANES, (k + 1) * LANES)
            send_ref[k, :mid, :] = up_ref[0, mid:, columns].astype(f32)
            send_ref[k, mid:block, :] = down_ref[0, :, columns].astype(f32)
            send_ref[k, block + rows : 2 * block, :] = flat(base + k, mid, tiles) + (
                local_coef * up_ref[0, :mid, columns].astype(f32)
            )
        values = small_ref[...].astype(f32)
        put_small(values[:, small:], values[:, :small])

    @pl.when(group == 1)
    def _():
        for k, value in enumerate(attn_tiles(in_ref, out_ref)):
            send_ref[k, :rows, :] = value
        for k in range(tiles):
            columns = slice(k * LANES, (k + 1) * LANES)
            send_ref[k, rows:block, :] = up_ref[0, :mid, columns].astype(f32)
            send_ref[k, block : block + mid, :] = flat(k, mid, tiles) + (
                local_coef * up_ref[0, mid:, columns].astype(f32)
            )
        base = mid * tiles
        pairs = tiles * HALF
        low = low_lanes(pairs)
        first, second, third = (flat(base + j, pairs, 3) for j in range(3))
        turned, turned_more = turn(second), turn(third)
        even, odd = pl.ds(0, pairs, stride=2), pl.ds(1, pairs, stride=2)
        wide_ref[0, even, :] = first
        wide_ref[1, even, :] = second
        wide_ref[0, odd, :] = jnp.where(low, turned, turned_more)
        wide_ref[1, odd, :] = turned_more
        start = block + mid
        for k in range(tiles):
            columns = slice(k * LANES, (k + 1) * LANES)
            upper = wide_ref[0, columns, :].T
            lower = wide_ref[1, columns, :].T[:HALF]
            send_ref[k, start : start + LANES, :] = upper + (
                local_coef * down_ref[0, :LANES, columns].astype(f32)
            )
            send_ref[k, start + LANES : 2 * block, :] = lower + (
                local_coef * down_ref[0, LANES:, columns].astype(f32)
            )
        values = small_ref[...].astype(f32)
        put_small(values[:, :small], values[:, small:])


def after_kernel(
    recv_ref, send_ref, in_ref, out_ref, up_ref, down_ref, old_ref, mom_ref, small_ref,
    small_old_ref, small_mom_ref, moment_hbm, *refs,
):
    targets, moment_ref, sources, (sum_ref, wide_ref, sems) = refs[:7], refs[7], refs[8:15], refs[15:]
    (
        in_next_ref, out_next_ref, up_next_ref, down_next_ref, moved_ref, small_next_ref,
        small_moved_ref,
    ) = sources
    copies = [
        pltpu.make_async_copy(source, target, sems.at[k])
        for k, (source, target) in enumerate(zip(sources, targets))
    ]
    copies.append(pltpu.make_async_copy(moment_hbm, moment_ref, sems.at[7]))
    copies[7].start()

    def go(*numbers):
        for k in numbers:
            copies[k].start()

    rows = up_ref.shape[1]
    mid = rows // 2
    block = rows + mid
    tiles = up_ref.shape[2] // LANES
    small = small_old_ref.shape[1]
    group = lax.axis_index("group")

    def put_moved(start, stride, value):
        at = pl.ds(start, value.shape[0], stride=stride)
        moved_ref[at, :] = momentum_coef * mom_ref[at, :] + (old_ref[at, :] - 0.5 * value)

    def get(start, tile):
        return sum_ref[tile, pl.ds(start, rows // 2, stride=2), :]

    def put_attn(tile, value):
        whole = in_ref.shape[-1] // LANES
        if tile < whole:
            in_next_ref[:, tile * LANES : (tile + 1) * LANES] = value
        elif tile == whole:
            in_next_ref[:, tile * LANES :] = value[:, :HALF]
            out_next_ref[:, LANES:] = turn(value)[:, :HALF]
        else:
            out_next_ref[:, :LANES] = value

    def small_row(ref, tile):
        pieces = []
        for row in range(pl.cdiv(small, LANES)):
            at = 2 * block + row
            pieces.append(ref[tile, at : at + 1, : min(LANES, small - row * LANES)])
        return jnp.concatenate(pieces, axis=1)

    def put_small(other, own, first):
        theirs = small_row(recv_ref, 0)
        mine = small_row(send_ref, 1) + local_coef * theirs
        rest = small_row(recv_ref, 1) + local_coef * other
        both = [mine, rest] if first else [rest, mine]
        small_next_ref[...] = jnp.concatenate(both, axis=1).reshape(-1)
        small_moved_ref[...] = momentum_coef * small_mom_ref[...] + (
            small_old_ref[...] - 0.5 * (own + theirs)
        )

    @pl.when(group == 0)
    def _():
        for k, value in enumerate(attn_tiles(in_ref, out_ref)):
            theirs = recv_ref[k, :rows, :]
            put_attn(k, send_ref[k, block : block + rows, :] + local_coef * theirs)
            sum_ref[k, :, :] = value + theirs
        go(0, 1)
        for start, stride, value in flatten_attn(get, rows):
            put_moved(start, stride, value)
        base = rows * tiles
        for k in range(tiles):
            columns = slice(k * LANES, (k + 1) * LANES)
            theirs = recv_ref[k, rows:block, :]
            up_next_ref[:mid, columns] = (
                send_ref[k, block + rows : 2 * block, :] + local_coef * theirs
            )
            put_moved(base + k, tiles, up_ref[0, :mid, columns].astype(f32) + theirs)
            up_next_ref[mid:, columns] = recv_ref[k, block : block + mid, :] + (
                local_coef * up_ref[0, mid:, columns].astype(f32)
            )
            down_next_ref[:, columns] = recv_ref[k, block + mid : 2 * block, :] + (
                local_coef * down_ref[0, :, columns].astype(f32)
            )
        go(2, 3, 4)
        values = small_ref[...].astype(f32)
        put_small(values[:, small:], values[:, :small], True)
        go(5, 6)
        for copy in copies:
            copy.wait()

    @pl.when(group == 1)
    def _():
        for k, value in enumerate(attn_tiles(in_ref, out_ref)):
            put_attn(k, recv_ref[k, block : block + rows, :] + local_coef * value)
        go(0, 1)
        for k in range(tiles):
            columns = slice(k * LANES, (k + 1) * LANES)
            up_next_ref[:mid, columns] = recv_ref[k, block + rows : 2 * block, :] + (
                local_coef * up_ref[0, :mid, columns].astype(f32)
            )
            theirs = recv_ref[k, :mid, :]
            up_next_ref[mid:, columns] = send_ref[k, block : block + mid, :] + local_coef * theirs
            put_moved(k, tiles, up_ref[0, mid:, columns].astype(f32) + theirs)
            theirs = recv_ref[k, mid:block, :]
            down_next_ref[:, columns] = (
                send_ref[k, block + mid : 2 * block, :] + local_coef * theirs
            )
            total = down_ref[0, :, columns].astype(f32) + theirs
            wide_ref[0, columns, :] = total[:LANES].T
            lower = jnp.concatenate([total[LANES:], total[LANES:]], axis=0)
            wide_ref[1, columns, :] = lower.T
        go(2, 3)
        base = mid * tiles
        pairs = tiles * HALF
        low = low_lanes(pairs)
        even, odd = pl.ds(0, pairs, stride=2), pl.ds(1, pairs, stride=2)
        odd_first = turn(wide_ref[0, odd, :])
        put_moved(base, 3, wide_ref[0, even, :])
        put_moved(base + 1, 3, jnp.where(low, wide_ref[1, even, :], odd_first))
        put_moved(base + 2, 3, jnp.where(low, odd_first, wide_ref[1, odd, :]))
        go(4)
        values = small_ref[...].astype(f32)
        put_small(values[:, :small], values[:, small:], False)
        go(5, 6)
        for copy in copies:
            copy.wait()


def dense_before(order, operands):
    _, rows, width = operands[2].shape
    return pl.pallas_call(
        before_kernel,
        in_specs=[ANY] + [WHOLE] * 9,
        out_specs=WHOLE,
        out_shape=jax.ShapeDtypeStruct((width // LANES, 3 * rows + 8, LANES), f32),
        scratch_shapes=[pltpu.VMEM((2, width, LANES), f32)],
        compiler_params=pltpu.CompilerParams(vmem_limit_bytes=4 * 2**20),
        cost_estimate=pl.CostEstimate(
            flops=60000 * rows * width, bytes_accessed=30 * rows * width, transcendentals=0
        ),
        name="dense_before",
    )(order, *operands)


def dense_after(received, sent, operands, moment):
    _, rows, width = operands[2].shape
    outs = [matrix.shape[1:] for matrix in operands[:4]]
    outs += [operands[4].shape, operands[6].shape[1:], operands[7].shape]
    return pl.pallas_call(
        after_kernel,
        in_specs=[WHOLE] * 11 + [ANY],
        out_specs=[ANY] * 7 + [WHOLE],
        out_shape=[jax.ShapeDtypeStruct(shape, f32) for shape in (*outs, moment.shape)],
        scratch_shapes=[pltpu.VMEM(shape, f32) for shape in outs]
        + [
            pltpu.VMEM((width // LANES, rows, LANES), f32),
            pltpu.VMEM((2, width, LANES), f32),
            pltpu.SemaphoreType.DMA((8,)),
        ],
        compiler_params=pltpu.CompilerParams(vmem_limit_bytes=8 * 2**20),
        cost_estimate=pl.CostEstimate(
            flops=60000 * rows * width, bytes_accessed=40 * rows * width, transcendentals=0
        ),
        name="dense_after",
    )(received, sent, *operands, *in_hbm([moment]))


def paired(
    attn_in_local,
    attn_out_local,
    ffn_in_local,
    ffn_out_local,
    small_local,
    dense_old,
    dense_momentum,
    small_old,
    small_momentum,
    embed_local,
    embed_old,
    basis,
    coeff_momentum,
):
    swap = [(0, 1), (1, 0)]
    chips = lax.axis_size("shard")

    first, second = (
        [
            (core * chips + chip, (1 - core) * chips + (chip ^ (1 + (core ^ turned(chip) ^ late))))
            for core in range(2)
            for chip in range(chips)
        ]
        for late in range(2)
    )
    axes = ("group", "shard")

    embed = (basis.T, embed_local[0], embed_old)
    theirs = [lax.ppermute(first_part(*embed), "group", swap)]
    late, *mine, stack = other_parts(*embed)
    theirs.append(lax.ppermute(late, "group", swap))

    operands = (
        attn_in_local,
        attn_out_local,
        ffn_in_local,
        jnp.swapaxes(ffn_out_local, 1, 2),
        dense_old.reshape(-1, LANES),
        dense_momentum.reshape(-1, LANES),
        small_local,
        small_old[None, :],
        small_momentum[None, :],
    )
    totals = [add(*pair, flops=10**4) for pair in zip(mine, theirs)]
    moving = [lax.ppermute(total, axes, first) for total in totals]
    sent = dense_before(totals[0], operands)
    received = lax.ppermute(sent, "group", swap)
    totals = [
        add(*pair, flops=flops) for *pair, flops in zip(totals, moving, (10**4, 2 * 10**10))
    ]
    moving = [lax.ppermute(total, axes, second) for total in totals]
    *dense, moment = dense_after(received, sent, operands, coeff_momentum)
    moving[0], dense[-1] = lax.optimization_barrier((moving[0], dense[-1]))
    own = [add(totals[0], moving[0], scale=0.5)]
    rest = [lax.ppermute(own[0], "group", swap)]
    early = embed_early(stack, moment, embed_old, own[0])
    own.append(add(totals[1], moving[1], early[:1], scale=0.5))
    rest.append(lax.ppermute(own[1], "group", swap))
    shared = (stack, moment, embed_old)
    done = embed_pieces(
        ((False, 1), (True, 0)), (False, 0), *shared, (own[1], rest[0]), early, ()
    )
    done = embed_pieces(((True, 1),), None, *shared, rest[1:], (), done)
    embed_next, coeff_moved = done

    attn_in_next, attn_out_next, ffn_in_next, ffn_out_next, moved, small_next, small_moved = dense
    return (
        attn_in_next,
        attn_out_next,
        ffn_in_next,
        ffn_out_next.T,
        moved.reshape(dense_old.shape),
        small_next,
        small_moved[0],
        embed_next,
        coeff_moved,
    )


def is_paired(mesh, shapes):
    attn_in, attn_out, ffn_in, ffn_out = (shape[1:] for shape in shapes[:4])
    rows = ffn_in[0]
    return (
        mesh.shape["group"] == 2
        and mesh.shape["shard"] == 4
        and attn_in == (rows, 4 * LANES + HALF)
        and attn_out == (rows, LANES + HALF)
        and ffn_in[1] == 6 * LANES
        and ffn_out == (6 * LANES, rows)
        and rows == LANES + HALF
        and shapes[7][0] <= 8 * LANES
        and shapes[10][1] % (8 * LANES) == 0
    )


def solution(mesh):
    placed = (
        P("group", "shard", "tensor"),
        P("group", "shard", "tensor"),
        P("group", "shard", "tensor"),
        P("group", "shard", "tensor"),
        P("group", None),
        P(("shard", "tensor"), "group"),
        P(("shard", "tensor"), "group"),
        P("group"),
        P("group"),
        P("group", "shard", "tensor"),
        P("shard", "tensor"),
        P("shard", None),
        P(None, "tensor"),
    )

    def shards(*args):
        plan = paired if is_paired(mesh, [arg.shape for arg in args]) else general
        return plan(*args)

    return jax.shard_map(
        shards,
        mesh=mesh,
        in_specs=placed,
        out_specs=(
            P("shard", "tensor"),
            P("shard", "tensor"),
            P("shard", "tensor"),
            P("shard", "tensor"),
            P(("shard", "tensor"), "group"),
            P(),
            P("group"),
            P("shard", "tensor"),
            P(None, "tensor"),
        ),
        check_vma=False,
    )
```

```python
import functools

import jax
import jax.numpy as jnp
from jax import lax
from jax.experimental import pallas as pl
from jax.experimental.pallas import tpu as pltpu
from jax.sharding import PartitionSpec as P

momentum_coef = 0.5
outer_rate = 0.7

f32 = jnp.float32
bf16 = jnp.bfloat16
LANES = 128
HALF = LANES // 2


def nesterov(old_value, momentum, delta):
    moved = momentum_coef * momentum + delta
    return (old_value - outer_rate * (delta + momentum_coef * moved), moved)


def general(
    attn_in_local,
    attn_out_local,
    ffn_in_local,
    ffn_out_local,
    small_local,
    dense_old,
    dense_momentum,
    small_old,
    small_momentum,
    embed_local,
    embed_old,
    basis,
    coeff_momentum,
):
    groups = lax.axis_size("group")
    matrices = (attn_in_local, attn_out_local, ffn_in_local, ffn_out_local)
    local_terms = jnp.concatenate([matrix[0].reshape(-1) for matrix in matrices]).astype(f32)
    small_terms = small_local[0].astype(f32)
    old_flat = dense_old[0]
    momentum_flat = dense_momentum[0]
    dense_part, small_part = (
        lax.psum_scatter(local_terms, "group", scatter_dimension=0, tiled=True),
        lax.psum_scatter(small_terms, "group", scatter_dimension=0, tiled=True),
    )
    dense_new, dense_moved = nesterov(old_flat, momentum_flat, old_flat - dense_part / groups)
    small_new, small_moved = nesterov(small_old, small_momentum, small_old - small_part / groups)
    full_flat, small_next = (
        lax.all_gather(dense_new, "group", axis=0, tiled=True),
        lax.all_gather(small_new, "group", axis=0, tiled=True),
    )
    results = []
    offset = 0
    for matrix in matrices:
        block_size = matrix.shape[1] * matrix.shape[2]
        results.append(
            full_flat[offset : offset + block_size].reshape(matrix.shape[1], matrix.shape[2])
        )
        offset = offset + block_size
    difference = embed_old - embed_local[0].astype(f32)
    partial_coeff = lax.dot_general(
        basis,
        difference,
        (((0,), (0,)), ((), ())),
        precision=lax.Precision.HIGHEST,
        preferred_element_type=f32,
    )
    coeff = lax.psum(partial_coeff, ("group", "shard")) / groups
    coeff_moved = momentum_coef * coeff_momentum + coeff
    update = coeff + momentum_coef * coeff_moved
    embed_next = embed_old - outer_rate * jnp.dot(
        basis, update, precision=lax.Precision.HIGHEST, preferred_element_type=f32
    )
    return (
        results[0],
        results[1],
        results[2],
        results[3],
        dense_moved[None, :],
        small_next,
        small_moved,
        embed_next,
        coeff_moved,
    )


local_coef = outer_rate * (1 + momentum_coef) / 2
old_coef = 1 - outer_rate * (1 + momentum_coef)
mom_coef = -outer_rate * momentum_coef * momentum_coef


def split(value):
    high = value.astype(bf16)
    return high, (value - high.astype(f32)).astype(bf16)


CHUNKS = 2
WHOLE = pl.BlockSpec(memory_space=pltpu.VMEM)
ANY = pl.BlockSpec(memory_space=pl.ANY)


def in_hbm(arrays):
    return [pltpu.with_memory_space_constraint(array, pltpu.HBM) for array in arrays]


def turned(chip):
    return (chip ^ (chip >> 1)) & 1


def side_start(other, columns):
    side = lax.axis_index("group") ^ turned(lax.axis_index("shard"))
    return (1 - side if other else side) * columns


def both_parts(basis):
    return jnp.concatenate(split(basis), axis=0)


def doubled_product(both, local, old):
    rank = both.shape[0] // 2
    diff_high, diff_low = split(2 * old - local.astype(f32))
    first = jnp.dot(both, diff_high, preferred_element_type=f32)
    second = jnp.dot(both[:rank], diff_low, preferred_element_type=f32)
    return first[:rank] + first[rank:] + second


def local_product(both, local):
    rank = both.shape[0] // 2
    first = jnp.dot(both, local, preferred_element_type=f32)
    return -(first[:rank] + first[rank:])


def first_kernel(basis_hbm, local_hbm, old_hbm, out_ref, *refs):
    *held, sems = refs
    basis_ref, local_ref, old_ref = held
    group = lax.axis_index("group")
    columns = out_ref.shape[1]
    there = pl.ds(pl.multiple_of(side_start(True, CHUNKS * columns), columns), columns)
    sources = (basis_hbm, local_hbm.at[:, there], old_hbm.at[:, there])
    copies = [
        pltpu.make_async_copy(source, target, sems.at[k])
        for k, (source, target) in enumerate(zip(sources, held))
    ]

    @pl.when(group == 0)
    def _():
        for copy in copies[:2]:
            copy.start()
        for copy in copies[:2]:
            copy.wait()
        out_ref[...] = local_product(both_parts(basis_ref[...]), local_ref[...])

    @pl.when(group == 1)
    def _():
        for copy in copies:
            copy.start()
        for copy in copies:
            copy.wait()
        out_ref[...] = doubled_product(both_parts(basis_ref[...]), local_ref[...], old_ref[...])


def first_part(basis_t, local, old):
    rank, depth = basis_t.shape
    block = old.shape[1] // (2 * CHUNKS)
    return pl.pallas_call(
        first_kernel,
        in_specs=[ANY] * 3,
        out_specs=WHOLE,
        out_shape=jax.ShapeDtypeStruct((rank, block), f32),
        scratch_shapes=[
            pltpu.VMEM((rank, depth), f32),
            pltpu.VMEM((depth, block), bf16),
            pltpu.VMEM((depth, block), f32),
            pltpu.SemaphoreType.DMA((3,)),
        ],
        compiler_params=pltpu.CompilerParams(vmem_limit_bytes=4 * 2**20),
        cost_estimate=pl.CostEstimate(
            flops=6 * rank * depth * block, bytes_accessed=6 * depth * block, transcendentals=0
        ),
        name="first_part",
    )(*in_hbm((basis_t, local, old)))


def other_kernel(basis_ref, local_ref, old_ref, rest_ref, *refs):
    *out_refs, stack_ref = refs
    basis = basis_ref[...]
    both = both_parts(basis)
    block = rest_ref.shape[1]
    columns = CHUNKS * block
    places = [(True, k) for k in range(1, CHUNKS)] + [(False, k) for k in range(CHUNKS)]
    group = lax.axis_index("group")
    parts = [
        (pl.ds(pl.multiple_of(side_start(other, columns) + k * block, block), block), out_ref)
        for (other, k), out_ref in zip(places, (rest_ref, *out_refs))
    ]

    @pl.when(group == 0)
    def _():
        for there, out_ref in parts:
            out_ref[...] = local_product(both, local_ref[:, there])

    @pl.when(group == 1)
    def _():
        for there, out_ref in parts:
            out_ref[...] = doubled_product(both, local_ref[:, there], old_ref[:, there])

    high = basis.astype(bf16).astype(f32)
    stack_ref[...] = jnp.concatenate([high, basis - high, high], axis=0).T.astype(bf16)


def other_parts(basis_t, local, old):
    rank, depth = basis_t.shape
    block = old.shape[1] // (2 * CHUNKS)
    return pl.pallas_call(
        other_kernel,
        in_specs=[WHOLE] * 3,
        out_specs=[WHOLE] * (2 * CHUNKS),
        out_shape=[jax.ShapeDtypeStruct((rank, block), f32)] * (2 * CHUNKS - 1)
        + [jax.ShapeDtypeStruct((depth, 3 * rank), bf16)],
        compiler_params=pltpu.CompilerParams(vmem_limit_bytes=4 * 2**20),
        cost_estimate=pl.CostEstimate(
            flops=10**10, bytes_accessed=18 * depth * block, transcendentals=0
        ),
        name="other_parts",
    )(basis_t, local, old)


def add_kernel(scale, first_ref, second_ref, *refs):
    refs[-1][...] = scale * (first_ref[...] + second_ref[...])


def add(first, second, after=(), scale=1.0, flops=2 * 10**10):
    return pl.pallas_call(
        functools.partial(add_kernel, scale),
        in_specs=[WHOLE] * 2 + [ANY] * len(after),
        out_specs=WHOLE,
        out_shape=jax.ShapeDtypeStruct(first.shape, f32),
        compiler_params=pltpu.CompilerParams(vmem_limit_bytes=2 * 2**20),
        cost_estimate=pl.CostEstimate(flops=flops, bytes_accessed=0, transcendentals=0),
        name="add",
    )(first, second, *after)


def embed_piece(start, width, coeff, stack_ref, moment_ref, old_ref):
    there = pl.ds(pl.multiple_of(start, width), width)
    moved = momentum_coef * moment_ref[:, there] + coeff
    up_high, up_low = split(coeff + momentum_coef * moved)
    change = jnp.dot(
        stack_ref[...],
        jnp.concatenate([up_high, up_high, up_low], axis=0),
        preferred_element_type=f32,
    )
    return old_ref[:, there] - outer_rate * change, moved


def early_kernel(stack_ref, moment_ref, old_ref, coeff_ref, embed_ref, moved_ref):
    start = side_start(False, old_ref.shape[1] // 2)
    embed_ref[...], moved_ref[...] = embed_piece(
        start, coeff_ref.shape[1], coeff_ref[...], stack_ref, moment_ref, old_ref
    )


def embed_early(stack, moment, old, coeff):
    depth, (rank, width) = old.shape[0], coeff.shape
    return pl.pallas_call(
        early_kernel,
        in_specs=[WHOLE] * 4,
        out_specs=[WHOLE] * 2,
        out_shape=[
            jax.ShapeDtypeStruct((depth, width), f32),
            jax.ShapeDtypeStruct((rank, width), f32),
        ],
        compiler_params=pltpu.CompilerParams(vmem_limit_bytes=4 * 2**20),
        cost_estimate=pl.CostEstimate(
            flops=6 * rank * depth * width, bytes_accessed=8 * depth * width, transcendentals=0
        ),
        name="embed_early",
    )(stack, moment, old, coeff)


def embed_kernel(pieces, ready, stack_ref, moment_ref, old_ref, *refs):
    count = len(pieces)
    coeffs, refs = refs[:count], refs[count:]
    embed_hbm, moved_hbm, embed_ref, moved_ref, sems = refs[-5:]
    width = coeffs[0].shape[1]
    copies = []

    def start_of(other, part):
        return side_start(other, old_ref.shape[1] // 2) + part * width

    def send(start, embed, moved):
        there = pl.ds(pl.multiple_of(start, width), width)
        for source, target in ((moved, moved_hbm), (embed, embed_hbm)):
            copies.append(
                pltpu.make_async_copy(source, target.at[:, there], sems.at[len(copies)])
            )
            copies[-1].start()

    if ready:
        send(start_of(*ready), refs[0], refs[1])
    for k, piece in enumerate(pieces):
        start = start_of(*piece)
        embed_ref[k], moved_ref[k] = embed_piece(
            start, width, coeffs[k][...], stack_ref, moment_ref, old_ref
        )
        send(start, embed_ref.at[k], moved_ref.at[k])
    for copy in copies:
        copy.wait()


def embed_pieces(pieces, ready, stack, moment, old, coeffs, early, before):
    count = len(pieces)
    rank, width = coeffs[0].shape
    first = 3 + count + len(early)
    return pl.pallas_call(
        functools.partial(embed_kernel, pieces, ready),
        in_specs=[WHOLE] * first + [ANY] * len(before),
        out_specs=[ANY, ANY],
        out_shape=[
            jax.ShapeDtypeStruct(old.shape, f32),
            jax.ShapeDtypeStruct(moment.shape, f32),
        ],
        scratch_shapes=[
            pltpu.VMEM((count, old.shape[0], width), f32),
            pltpu.VMEM((count, rank, width), f32),
            pltpu.SemaphoreType.DMA((2 * count + len(early),)),
        ],
        input_output_aliases={first: 0, first + 1: 1} if before else {},
        compiler_params=pltpu.CompilerParams(vmem_limit_bytes=8 * 2**20),
        cost_estimate=pl.CostEstimate(
            flops=6 * count * rank * old.shape[0] * width,
            bytes_accessed=8 * count * old.shape[0] * width,
            transcendentals=0,
        ),
        name="embed_pieces",
    )(stack, moment, old, *coeffs, *early, *before)


def low_lanes(rows):
    return lax.broadcasted_iota(jnp.int32, (rows, LANES), 1) < HALF


def turn(value):
    return pltpu.roll(value, HALF, 1)


def attn_tiles(in_ref, out_ref):
    whole = in_ref.shape[-1] // LANES
    tiles = [in_ref[0, :, k * LANES : (k + 1) * LANES].astype(f32) for k in range(whole)]
    last = in_ref[0, :, whole * LANES :].astype(f32)
    side = out_ref[0, :, LANES:].astype(f32)
    tiles.append(jnp.concatenate([last, side], axis=-1))
    tiles.append(out_ref[0, :, :LANES].astype(f32))
    return tiles


def unflatten_attn(flat, put, rows):
    pairs = rows // 2
    low = low_lanes(pairs)
    inner = [flat(j, pairs, 9) for j in range(9)]
    base = pairs * 9
    outer = [flat(base + j, pairs, 3) for j in range(3)]
    turned = [turn(inner[j]) for j in range(4, 9)]
    turned_out = [turn(outer[j]) for j in (1, 2)]
    for k in range(4):
        put(0, k, inner[k])
        put(1, k, jnp.where(low, turned[k], turned[k + 1]))
    put(0, 4, jnp.where(low, inner[4], turned_out[0]))
    put(1, 4, jnp.where(low, turned[4], outer[2]))
    put(0, 5, outer[0])
    put(1, 5, jnp.where(low, turned_out[0], turned_out[1]))


def flatten_attn(get, rows):
    pairs = rows // 2
    low = low_lanes(pairs)
    even = [get(0, k) for k in range(6)]
    odd = [get(1, k) for k in range(6)]
    turned = [turn(odd[k]) for k in range(5)]
    pieces = [(k, 9, even[k]) for k in range(4)]
    pieces.append((4, 9, jnp.where(low, even[4], turned[0])))
    for k in range(4):
        pieces.append((5 + k, 9, jnp.where(low, turned[k], turned[k + 1])))
    base = pairs * 9
    pieces.append((base, 3, even[5]))
    turned_out = turn(odd[5])
    pieces.append((base + 1, 3, jnp.where(low, turn(even[4]), turned_out)))
    pieces.append((base + 2, 3, jnp.where(low, turned_out, odd[4])))
    return pieces


def before_kernel(
    order_ref, in_ref, out_ref, up_ref, down_ref, old_ref, mom_ref, small_ref, small_old_ref,
    small_mom_ref, send_ref, wide_ref,
):
    del order_ref
    group = lax.axis_index("group")
    rows = up_ref.shape[1]
    mid = rows // 2
    block = rows + mid
    tiles = up_ref.shape[2] // LANES
    small = small_old_ref.shape[1]

    def flat(start, count, stride):
        at = pl.ds(start, count, stride=stride)
        return old_coef * old_ref[at, :] + mom_coef * mom_ref[at, :]

    def put(start, tile, value):
        send_ref[tile, pl.ds(block + start, rows // 2, stride=2), :] = value

    def put_small(other, own):
        own_terms = (
            old_coef * small_old_ref[...] + mom_coef * small_mom_ref[...] + local_coef * own
        )
        send_ref[:, 2 * block :, :] = jnp.zeros((tiles, 8, LANES), f32)
        for tile, value in enumerate((other, own_terms)):
            for row in range(pl.cdiv(small, LANES)):
                piece = value[:, row * LANES : (row + 1) * LANES]
                at = 2 * block + row
                send_ref[tile, at : at + 1, : piece.shape[1]] = piece

    @pl.when(group == 0)
    def _():
        unflatten_attn(flat, put, rows)
        for k, value in enumerate(attn_tiles(in_ref, out_ref)):
            send_ref[k, block : block + rows, :] += local_coef * value
        base = rows * tiles
        for k in range(tiles):
            columns = slice(k * LANES, (k + 1) * LANES)
            send_ref[k, :mid, :] = up_ref[0, mid:, columns].astype(f32)
            send_ref[k, mid:block, :] = down_ref[0, :, columns].astype(f32)
            send_ref[k, block + rows : 2 * block, :] = flat(base + k, mid, tiles) + (
                local_coef * up_ref[0, :mid, columns].astype(f32)
            )
        values = small_ref[...].astype(f32)
        put_small(values[:, small:], values[:, :small])

    @pl.when(group == 1)
    def _():
        for k, value in enumerate(attn_tiles(in_ref, out_ref)):
            send_ref[k, :rows, :] = value
        for k in range(tiles):
            columns = slice(k * LANES, (k + 1) * LANES)
            send_ref[k, rows:block, :] = up_ref[0, :mid, columns].astype(f32)
            send_ref[k, block : block + mid, :] = flat(k, mid, tiles) + (
                local_coef * up_ref[0, mid:, columns].astype(f32)
            )
        base = mid * tiles
        pairs = tiles * HALF
        low = low_lanes(pairs)
        first, second, third = (flat(base + j, pairs, 3) for j in range(3))
        turned, turned_more = turn(second), turn(third)
        even, odd = pl.ds(0, pairs, stride=2), pl.ds(1, pairs, stride=2)
        wide_ref[0, even, :] = first
        wide_ref[1, even, :] = second
        wide_ref[0, odd, :] = jnp.where(low, turned, turned_more)
        wide_ref[1, odd, :] = turned_more
        start = block + mid
        for k in range(tiles):
            columns = slice(k * LANES, (k + 1) * LANES)
            upper = wide_ref[0, columns, :].T
            lower = wide_ref[1, columns, :].T[:HALF]
            send_ref[k, start : start + LANES, :] = upper + (
                local_coef * down_ref[0, :LANES, columns].astype(f32)
            )
            send_ref[k, start + LANES : 2 * block, :] = lower + (
                local_coef * down_ref[0, LANES:, columns].astype(f32)
            )
        values = small_ref[...].astype(f32)
        put_small(values[:, :small], values[:, small:])


def after_kernel(
    recv_ref, send_ref, in_ref, out_ref, up_ref, down_ref, old_ref, mom_ref, small_ref,
    small_old_ref, small_mom_ref, moment_hbm, *refs,
):
    targets, moment_ref, sources, (sum_ref, wide_ref, sems) = refs[:7], refs[7], refs[8:15], refs[15:]
    (
        in_next_ref, out_next_ref, up_next_ref, down_next_ref, moved_ref, small_next_ref,
        small_moved_ref,
    ) = sources
    copies = [
        pltpu.make_async_copy(source, target, sems.at[k])
        for k, (source, target) in enumerate(zip(sources, targets))
    ]
    copies.append(pltpu.make_async_copy(moment_hbm, moment_ref, sems.at[7]))
    copies[7].start()

    def go(*numbers):
        for k in numbers:
            copies[k].start()

    rows = up_ref.shape[1]
    mid = rows // 2
    block = rows + mid
    tiles = up_ref.shape[2] // LANES
    small = small_old_ref.shape[1]
    group = lax.axis_index("group")

    def put_moved(start, stride, value):
        at = pl.ds(start, value.shape[0], stride=stride)
        moved_ref[at, :] = momentum_coef * mom_ref[at, :] + (old_ref[at, :] - 0.5 * value)

    def get(start, tile):
        return sum_ref[tile, pl.ds(start, rows // 2, stride=2), :]

    def put_attn(tile, value):
        whole = in_ref.shape[-1] // LANES
        if tile < whole:
            in_next_ref[:, tile * LANES : (tile + 1) * LANES] = value
        elif tile == whole:
            in_next_ref[:, tile * LANES :] = value[:, :HALF]
            out_next_ref[:, LANES:] = turn(value)[:, :HALF]
        else:
            out_next_ref[:, :LANES] = value

    def small_row(ref, tile):
        pieces = []
        for row in range(pl.cdiv(small, LANES)):
            at = 2 * block + row
            pieces.append(ref[tile, at : at + 1, : min(LANES, small - row * LANES)])
        return jnp.concatenate(pieces, axis=1)

    def put_small(other, own, first):
        theirs = small_row(recv_ref, 0)
        mine = small_row(send_ref, 1) + local_coef * theirs
        rest = small_row(recv_ref, 1) + local_coef * other
        both = [mine, rest] if first else [rest, mine]
        small_next_ref[...] = jnp.concatenate(both, axis=1).reshape(-1)
        small_moved_ref[...] = momentum_coef * small_mom_ref[...] + (
            small_old_ref[...] - 0.5 * (own + theirs)
        )

    @pl.when(group == 0)
    def _():
        for k, value in enumerate(attn_tiles(in_ref, out_ref)):
            theirs = recv_ref[k, :rows, :]
            put_attn(k, send_ref[k, block : block + rows, :] + local_coef * theirs)
            sum_ref[k, :, :] = value + theirs
        go(0, 1)
        for start, stride, value in flatten_attn(get, rows):
            put_moved(start, stride, value)
        base = rows * tiles
        for k in range(tiles):
            columns = slice(k * LANES, (k + 1) * LANES)
            theirs = recv_ref[k, rows:block, :]
            up_next_ref[:mid, columns] = (
                send_ref[k, block + rows : 2 * block, :] + local_coef * theirs
            )
            put_moved(base + k, tiles, up_ref[0, :mid, columns].astype(f32) + theirs)
            up_next_ref[mid:, columns] = recv_ref[k, block : block + mid, :] + (
                local_coef * up_ref[0, mid:, columns].astype(f32)
            )
            down_next_ref[:, columns] = recv_ref[k, block + mid : 2 * block, :] + (
                local_coef * down_ref[0, :, columns].astype(f32)
            )
        go(2, 3, 4)
        values = small_ref[...].astype(f32)
        put_small(values[:, small:], values[:, :small], True)
        go(5, 6)
        for copy in copies:
            copy.wait()

    @pl.when(group == 1)
    def _():
        for k, value in enumerate(attn_tiles(in_ref, out_ref)):
            put_attn(k, recv_ref[k, block : block + rows, :] + local_coef * value)
        go(0, 1)
        for k in range(tiles):
            columns = slice(k * LANES, (k + 1) * LANES)
            up_next_ref[:mid, columns] = recv_ref[k, block + rows : 2 * block, :] + (
                local_coef * up_ref[0, :mid, columns].astype(f32)
            )
            theirs = recv_ref[k, :mid, :]
            up_next_ref[mid:, columns] = send_ref[k, block : block + mid, :] + local_coef * theirs
            put_moved(k, tiles, up_ref[0, mid:, columns].astype(f32) + theirs)
            theirs = recv_ref[k, mid:block, :]
            down_next_ref[:, columns] = (
                send_ref[k, block + mid : 2 * block, :] + local_coef * theirs
            )
            total = down_ref[0, :, columns].astype(f32) + theirs
            wide_ref[0, columns, :] = total[:LANES].T
            lower = jnp.concatenate([total[LANES:], total[LANES:]], axis=0)
            wide_ref[1, columns, :] = lower.T
        go(2, 3)
        base = mid * tiles
        pairs = tiles * HALF
        low = low_lanes(pairs)
        even, odd = pl.ds(0, pairs, stride=2), pl.ds(1, pairs, stride=2)
        odd_first = turn(wide_ref[0, odd, :])
        put_moved(base, 3, wide_ref[0, even, :])
        put_moved(base + 1, 3, jnp.where(low, wide_ref[1, even, :], odd_first))
        put_moved(base + 2, 3, jnp.where(low, odd_first, wide_ref[1, odd, :]))
        go(4)
        values = small_ref[...].astype(f32)
        put_small(values[:, :small], values[:, small:], False)
        go(5, 6)
        for copy in copies:
            copy.wait()


def dense_before(order, operands):
    _, rows, width = operands[2].shape
    return pl.pallas_call(
        before_kernel,
        in_specs=[ANY] + [WHOLE] * 9,
        out_specs=WHOLE,
        out_shape=jax.ShapeDtypeStruct((width // LANES, 3 * rows + 8, LANES), f32),
        scratch_shapes=[pltpu.VMEM((2, width, LANES), f32)],
        compiler_params=pltpu.CompilerParams(vmem_limit_bytes=4 * 2**20),
        cost_estimate=pl.CostEstimate(
            flops=60000 * rows * width, bytes_accessed=30 * rows * width, transcendentals=0
        ),
        name="dense_before",
    )(order, *operands)


def dense_after(received, sent, operands, moment):
    _, rows, width = operands[2].shape
    outs = [matrix.shape[1:] for matrix in operands[:4]]
    outs += [operands[4].shape, operands[6].shape[1:], operands[7].shape]
    return pl.pallas_call(
        after_kernel,
        in_specs=[WHOLE] * 11 + [ANY],
        out_specs=[ANY] * 7 + [WHOLE],
        out_shape=[jax.ShapeDtypeStruct(shape, f32) for shape in (*outs, moment.shape)],
        scratch_shapes=[pltpu.VMEM(shape, f32) for shape in outs]
        + [
            pltpu.VMEM((width // LANES, rows, LANES), f32),
            pltpu.VMEM((2, width, LANES), f32),
            pltpu.SemaphoreType.DMA((8,)),
        ],
        compiler_params=pltpu.CompilerParams(vmem_limit_bytes=8 * 2**20),
        cost_estimate=pl.CostEstimate(
            flops=60000 * rows * width, bytes_accessed=40 * rows * width, transcendentals=0
        ),
        name="dense_after",
    )(received, sent, *operands, *in_hbm([moment]))


def paired(
    attn_in_local,
    attn_out_local,
    ffn_in_local,
    ffn_out_local,
    small_local,
    dense_old,
    dense_momentum,
    small_old,
    small_momentum,
    embed_local,
    embed_old,
    basis,
    coeff_momentum,
):
    swap = [(0, 1), (1, 0)]
    chips = lax.axis_size("shard")

    first, second = (
        [
            (core * chips + chip, (1 - core) * chips + (chip ^ (1 + (core ^ turned(chip) ^ late))))
            for core in range(2)
            for chip in range(chips)
        ]
        for late in range(2)
    )
    axes = ("group", "shard")

    embed = (basis.T, embed_local[0], embed_old)
    theirs = [lax.ppermute(first_part(*embed), "group", swap)]
    late, *mine, stack = other_parts(*embed)
    theirs.append(lax.ppermute(late, "group", swap))

    operands = (
        attn_in_local,
        attn_out_local,
        ffn_in_local,
        jnp.swapaxes(ffn_out_local, 1, 2),
        dense_old.reshape(-1, LANES),
        dense_momentum.reshape(-1, LANES),
        small_local,
        small_old[None, :],
        small_momentum[None, :],
    )
    totals = [add(*pair, flops=10**4) for pair in zip(mine, theirs)]
    moving = [lax.ppermute(total, axes, first) for total in totals]
    sent = dense_before(totals[0], operands)
    received = lax.ppermute(sent, "group", swap)
    totals = [
        add(*pair, flops=flops) for *pair, flops in zip(totals, moving, (10**4, 2 * 10**10))
    ]
    moving = [lax.ppermute(total, axes, second) for total in totals]
    *dense, moment = dense_after(received, sent, operands, coeff_momentum)
    moving[0], dense[-1] = lax.optimization_barrier((moving[0], dense[-1]))
    own = [add(totals[0], moving[0], scale=0.5)]
    rest = [lax.ppermute(own[0], "group", swap)]
    early = embed_early(stack, moment, embed_old, own[0])
    own.append(add(totals[1], moving[1], early[:1], scale=0.5))
    rest.append(lax.ppermute(own[1], "group", swap))
    shared = (stack, moment, embed_old)
    done = embed_pieces(
        ((False, 1), (True, 0)), (False, 0), *shared, (own[1], rest[0]), early, ()
    )
    done = embed_pieces(((True, 1),), None, *shared, rest[1:], (), done)
    embed_next, coeff_moved = done

    attn_in_next, attn_out_next, ffn_in_next, ffn_out_next, moved, small_next, small_moved = dense
    return (
        attn_in_next,
        attn_out_next,
        ffn_in_next,
        ffn_out_next.T,
        moved.reshape(dense_old.shape),
        small_next,
        small_moved[0],
        embed_next,
        coeff_moved,
    )


def is_paired(mesh, shapes):
    attn_in, attn_out, ffn_in, ffn_out = (shape[1:] for shape in shapes[:4])
    rows = ffn_in[0]
    return (
        mesh.shape["group"] == 2
        and mesh.shape["shard"] == 4
        and attn_in == (rows, 4 * LANES + HALF)
        and attn_out == (rows, LANES + HALF)
        and ffn_in[1] == 6 * LANES
        and ffn_out == (6 * LANES, rows)
        and rows == LANES + HALF
        and shapes[7][0] <= 8 * LANES
        and shapes[10][1] % (8 * LANES) == 0
    )


def solution(mesh):
    placed = (
        P("group", "shard", "tensor"),
        P("group", "shard", "tensor"),
        P("group", "shard", "tensor"),
        P("group", "shard", "tensor"),
        P("group", None),
        P(("shard", "tensor"), "group"),
        P(("shard", "tensor"), "group"),
        P("group"),
        P("group"),
        P("group", "shard", "tensor"),
        P("shard", "tensor"),
        P("shard", None),
        P(None, "tensor"),
    )

    def shards(*args):
        plan = paired if is_paired(mesh, [arg.shape for arg in args]) else general
        return plan(*args)

    return jax.shard_map(
        shards,
        mesh=mesh,
        in_specs=placed,
        out_specs=(
            P("shard", "tensor"),
            P("shard", "tensor"),
            P("shard", "tensor"),
            P("shard", "tensor"),
            P(("shard", "tensor"), "group"),
            P(),
            P("group"),
            P("shard", "tensor"),
            P(None, "tensor"),
        ),
        check_vma=False,
    )
```

```python
import functools

import jax
import jax.numpy as jnp
from jax import lax
from jax.experimental import pallas as pl
from jax.experimental.pallas import tpu as pltpu
from jax.sharding import PartitionSpec as P

momentum_coef = 0.5
outer_rate = 0.7

f32 = jnp.float32
bf16 = jnp.bfloat16
LANES = 128
HALF = LANES // 2


def nesterov(old_value, momentum, delta):
    moved = momentum_coef * momentum + delta
    return (old_value - outer_rate * (delta + momentum_coef * moved), moved)


def general(
    attn_in_local,
    attn_out_local,
    ffn_in_local,
    ffn_out_local,
    small_local,
    dense_old,
    dense_momentum,
    small_old,
    small_momentum,
    embed_local,
    embed_old,
    basis,
    coeff_momentum,
):
    groups = lax.axis_size("group")
    matrices = (attn_in_local, attn_out_local, ffn_in_local, ffn_out_local)
    local_terms = jnp.concatenate([matrix[0].reshape(-1) for matrix in matrices]).astype(f32)
    small_terms = small_local[0].astype(f32)
    old_flat = dense_old[0]
    momentum_flat = dense_momentum[0]
    dense_part, small_part = (
        lax.psum_scatter(local_terms, "group", scatter_dimension=0, tiled=True),
        lax.psum_scatter(small_terms, "group", scatter_dimension=0, tiled=True),
    )
    dense_new, dense_moved = nesterov(old_flat, momentum_flat, old_flat - dense_part / groups)
    small_new, small_moved = nesterov(small_old, small_momentum, small_old - small_part / groups)
    full_flat, small_next = (
        lax.all_gather(dense_new, "group", axis=0, tiled=True),
        lax.all_gather(small_new, "group", axis=0, tiled=True),
    )
    results = []
    offset = 0
    for matrix in matrices:
        block_size = matrix.shape[1] * matrix.shape[2]
        results.append(
            full_flat[offset : offset + block_size].reshape(matrix.shape[1], matrix.shape[2])
        )
        offset = offset + block_size
    difference = embed_old - embed_local[0].astype(f32)
    partial_coeff = lax.dot_general(
        basis,
        difference,
        (((0,), (0,)), ((), ())),
        precision=lax.Precision.HIGHEST,
        preferred_element_type=f32,
    )
    coeff = lax.psum(partial_coeff, ("group", "shard")) / groups
    coeff_moved = momentum_coef * coeff_momentum + coeff
    update = coeff + momentum_coef * coeff_moved
    embed_next = embed_old - outer_rate * jnp.dot(
        basis, update, precision=lax.Precision.HIGHEST, preferred_element_type=f32
    )
    return (
        results[0],
        results[1],
        results[2],
        results[3],
        dense_moved[None, :],
        small_next,
        small_moved,
        embed_next,
        coeff_moved,
    )


local_coef = outer_rate * (1 + momentum_coef) / 2
old_coef = 1 - outer_rate * (1 + momentum_coef)
mom_coef = -outer_rate * momentum_coef * momentum_coef


def split(value):
    high = value.astype(bf16)
    return high, (value - high.astype(f32)).astype(bf16)


CHUNKS = 2
WHOLE = pl.BlockSpec(memory_space=pltpu.VMEM)
ANY = pl.BlockSpec(memory_space=pl.ANY)


def in_hbm(arrays):
    return [pltpu.with_memory_space_constraint(array, pltpu.HBM) for array in arrays]


def turned(chip):
    return (chip ^ (chip >> 1)) & 1


def side_start(other, columns):
    side = lax.axis_index("group") ^ turned(lax.axis_index("shard"))
    return (1 - side if other else side) * columns


def both_parts(basis):
    return jnp.concatenate(split(basis), axis=0)


def doubled_product(both, local, old):
    rank = both.shape[0] // 2
    diff_high, diff_low = split(2 * old - local.astype(f32))
    first = jnp.dot(both, diff_high, preferred_element_type=f32)
    second = jnp.dot(both[:rank], diff_low, preferred_element_type=f32)
    return first[:rank] + first[rank:] + second


def local_product(both, local):
    rank = both.shape[0] // 2
    first = jnp.dot(both, local, preferred_element_type=f32)
    return -(first[:rank] + first[rank:])


def first_kernel(basis_hbm, local_hbm, old_hbm, out_ref, *refs):
    *held, sems = refs
    basis_ref, local_ref, old_ref = held
    group = lax.axis_index("group")
    columns = out_ref.shape[1]
    there = pl.ds(pl.multiple_of(side_start(True, CHUNKS * columns), columns), columns)
    sources = (basis_hbm, local_hbm.at[:, there], old_hbm.at[:, there])
    copies = [
        pltpu.make_async_copy(source, target, sems.at[k])
        for k, (source, target) in enumerate(zip(sources, held))
    ]

    @pl.when(group == 0)
    def _():
        for copy in copies[:2]:
            copy.start()
        for copy in copies[:2]:
            copy.wait()
        out_ref[...] = local_product(both_parts(basis_ref[...]), local_ref[...])

    @pl.when(group == 1)
    def _():
        for copy in copies:
            copy.start()
        for copy in copies:
            copy.wait()
        out_ref[...] = doubled_product(both_parts(basis_ref[...]), local_ref[...], old_ref[...])


def first_part(basis_t, local, old):
    rank, depth = basis_t.shape
    block = old.shape[1] // (2 * CHUNKS)
    return pl.pallas_call(
        first_kernel,
        in_specs=[ANY] * 3,
        out_specs=WHOLE,
        out_shape=jax.ShapeDtypeStruct((rank, block), f32),
        scratch_shapes=[
            pltpu.VMEM((rank, depth), f32),
            pltpu.VMEM((depth, block), bf16),
            pltpu.VMEM((depth, block), f32),
            pltpu.SemaphoreType.DMA((3,)),
        ],
        compiler_params=pltpu.CompilerParams(vmem_limit_bytes=4 * 2**20),
        cost_estimate=pl.CostEstimate(
            flops=6 * rank * depth * block, bytes_accessed=6 * depth * block, transcendentals=0
        ),
        name="first_part",
    )(*in_hbm((basis_t, local, old)))


def other_kernel(basis_ref, local_ref, old_ref, rest_ref, *out_refs):
    block = rest_ref.shape[1]
    columns = CHUNKS * block
    places = [(True, k) for k in range(1, CHUNKS)] + [(False, k) for k in range(CHUNKS)]
    parts = [
        (pl.ds(pl.multiple_of(side_start(other, columns) + k * block, block), block), out_ref)
        for (other, k), out_ref in zip(places, (rest_ref, *out_refs))
    ]

    def run(multiply):
        both = both_parts(basis_ref[...])
        for there, out_ref in parts:
            out_ref[...] = multiply(both, there)

    group = lax.axis_index("group")

    @pl.when(group == 0)
    def _():
        run(lambda both, there: local_product(both, local_ref[:, there]))

    @pl.when(group == 1)
    def _():
        run(lambda both, there: doubled_product(both, local_ref[:, there], old_ref[:, there]))


def other_parts(basis_t, local, old):
    rank, depth = basis_t.shape
    block = old.shape[1] // (2 * CHUNKS)
    return pl.pallas_call(
        other_kernel,
        in_specs=[WHOLE] * 3,
        out_specs=[WHOLE] * (2 * CHUNKS - 1),
        out_shape=[jax.ShapeDtypeStruct((rank, block), f32)] * (2 * CHUNKS - 1),
        compiler_params=pltpu.CompilerParams(vmem_limit_bytes=4 * 2**20),
        cost_estimate=pl.CostEstimate(
            flops=10**10, bytes_accessed=18 * depth * block, transcendentals=0
        ),
        name="other_parts",
    )(basis_t, local, old)


def add_kernel(scale, first_ref, second_ref, *refs):
    refs[-1][...] = scale * (first_ref[...] + second_ref[...])


def add(first, second, after=(), scale=1.0, flops=2 * 10**10):
    return pl.pallas_call(
        functools.partial(add_kernel, scale),
        in_specs=[WHOLE] * 2 + [ANY] * len(after),
        out_specs=WHOLE,
        out_shape=jax.ShapeDtypeStruct(first.shape, f32),
        compiler_params=pltpu.CompilerParams(vmem_limit_bytes=2 * 2**20),
        cost_estimate=pl.CostEstimate(flops=flops, bytes_accessed=0, transcendentals=0),
        name="add",
    )(first, second, *after)


def embed_piece(start, width, coeff, stack_ref, moment_ref, old_ref):
    there = pl.ds(pl.multiple_of(start, width), width)
    moved = momentum_coef * moment_ref[:, there] + coeff
    up_high, up_low = split(coeff + momentum_coef * moved)
    change = jnp.dot(
        stack_ref[...],
        jnp.concatenate([up_high, up_high, up_low], axis=0),
        preferred_element_type=f32,
    )
    return old_ref[:, there] - outer_rate * change, moved


def early_kernel(stack_ref, moment_ref, old_ref, coeff_ref, embed_ref, moved_ref):
    start = side_start(False, old_ref.shape[1] // 2)
    embed_ref[...], moved_ref[...] = embed_piece(
        start, coeff_ref.shape[1], coeff_ref[...], stack_ref, moment_ref, old_ref
    )


def embed_early(stack, moment, old, coeff):
    depth, (rank, width) = old.shape[0], coeff.shape
    return pl.pallas_call(
        early_kernel,
        in_specs=[WHOLE] * 4,
        out_specs=[WHOLE] * 2,
        out_shape=[
            jax.ShapeDtypeStruct((depth, width), f32),
            jax.ShapeDtypeStruct((rank, width), f32),
        ],
        compiler_params=pltpu.CompilerParams(vmem_limit_bytes=4 * 2**20),
        cost_estimate=pl.CostEstimate(
            flops=6 * rank * depth * width, bytes_accessed=8 * depth * width, transcendentals=0
        ),
        name="embed_early",
    )(stack, moment, old, coeff)


def embed_kernel(pieces, ready, stack_ref, moment_ref, old_ref, *refs):
    count = len(pieces)
    coeffs, refs = refs[:count], refs[count:]
    embed_hbm, moved_hbm, embed_ref, moved_ref, sems = refs[-5:]
    width = coeffs[0].shape[1]
    copies = []

    def start_of(other, part):
        return side_start(other, old_ref.shape[1] // 2) + part * width

    def send(start, embed, moved):
        there = pl.ds(pl.multiple_of(start, width), width)
        for source, target in ((moved, moved_hbm), (embed, embed_hbm)):
            copies.append(
                pltpu.make_async_copy(source, target.at[:, there], sems.at[len(copies)])
            )
            copies[-1].start()

    if ready:
        send(start_of(*ready), refs[0], refs[1])
    for k, piece in enumerate(pieces):
        start = start_of(*piece)
        embed_ref[k], moved_ref[k] = embed_piece(
            start, width, coeffs[k][...], stack_ref, moment_ref, old_ref
        )
        send(start, embed_ref.at[k], moved_ref.at[k])
    for copy in copies:
        copy.wait()


def embed_pieces(pieces, ready, stack, moment, old, coeffs, early, before):
    count = len(pieces)
    rank, width = coeffs[0].shape
    first = 3 + count + len(early)
    return pl.pallas_call(
        functools.partial(embed_kernel, pieces, ready),
        in_specs=[WHOLE] * first + [ANY] * len(before),
        out_specs=[ANY, ANY],
        out_shape=[
            jax.ShapeDtypeStruct(old.shape, f32),
            jax.ShapeDtypeStruct(moment.shape, f32),
        ],
        scratch_shapes=[
            pltpu.VMEM((count, old.shape[0], width), f32),
            pltpu.VMEM((count, rank, width), f32),
            pltpu.SemaphoreType.DMA((2 * count + len(early),)),
        ],
        input_output_aliases={first: 0, first + 1: 1} if before else {},
        compiler_params=pltpu.CompilerParams(vmem_limit_bytes=8 * 2**20),
        cost_estimate=pl.CostEstimate(
            flops=6 * count * rank * old.shape[0] * width,
            bytes_accessed=8 * count * old.shape[0] * width,
            transcendentals=0,
        ),
        name="embed_pieces",
    )(stack, moment, old, *coeffs, *early, *before)


def low_lanes(rows):
    return lax.broadcasted_iota(jnp.int32, (rows, LANES), 1) < HALF


def turn(value):
    return pltpu.roll(value, HALF, 1)


def attn_tiles(in_ref, out_ref):
    whole = in_ref.shape[-1] // LANES
    tiles = [in_ref[0, :, k * LANES : (k + 1) * LANES].astype(f32) for k in range(whole)]
    last = in_ref[0, :, whole * LANES :].astype(f32)
    side = out_ref[0, :, LANES:].astype(f32)
    tiles.append(jnp.concatenate([last, side], axis=-1))
    tiles.append(out_ref[0, :, :LANES].astype(f32))
    return tiles


def unflatten_attn(flat, put, rows):
    pairs = rows // 2
    low = low_lanes(pairs)
    inner = [flat(j, pairs, 9) for j in range(9)]
    base = pairs * 9
    outer = [flat(base + j, pairs, 3) for j in range(3)]
    turned = [turn(inner[j]) for j in range(4, 9)]
    turned_out = [turn(outer[j]) for j in (1, 2)]
    for k in range(4):
        put(0, k, inner[k])
        put(1, k, jnp.where(low, turned[k], turned[k + 1]))
    put(0, 4, jnp.where(low, inner[4], turned_out[0]))
    put(1, 4, jnp.where(low, turned[4], outer[2]))
    put(0, 5, outer[0])
    put(1, 5, jnp.where(low, turned_out[0], turned_out[1]))


def flatten_attn(get, rows):
    pairs = rows // 2
    low = low_lanes(pairs)
    even = [get(0, k) for k in range(6)]
    odd = [get(1, k) for k in range(6)]
    turned = [turn(odd[k]) for k in range(5)]
    pieces = [(k, 9, even[k]) for k in range(4)]
    pieces.append((4, 9, jnp.where(low, even[4], turned[0])))
    for k in range(4):
        pieces.append((5 + k, 9, jnp.where(low, turned[k], turned[k + 1])))
    base = pairs * 9
    pieces.append((base, 3, even[5]))
    turned_out = turn(odd[5])
    pieces.append((base + 1, 3, jnp.where(low, turn(even[4]), turned_out)))
    pieces.append((base + 2, 3, jnp.where(low, turned_out, odd[4])))
    return pieces


def before_kernel(
    order_ref, basis_ref, in_ref, out_ref, up_ref, down_ref, old_ref, mom_ref, small_ref,
    small_old_ref, small_mom_ref, send_ref, stack_ref, wide_ref,
):
    del order_ref
    basis = basis_ref[...]
    high = basis.astype(bf16).astype(f32)
    stack_ref[...] = jnp.concatenate([high, basis - high, high], axis=0).T.astype(bf16)
    group = lax.axis_index("group")
    rows = up_ref.shape[1]
    mid = rows // 2
    block = rows + mid
    tiles = up_ref.shape[2] // LANES
    small = small_old_ref.shape[1]

    def flat(start, count, stride):
        at = pl.ds(start, count, stride=stride)
        return old_coef * old_ref[at, :] + mom_coef * mom_ref[at, :]

    def put(start, tile, value):
        send_ref[tile, pl.ds(block + start, rows // 2, stride=2), :] = value

    def put_small(other, own):
        own_terms = (
            old_coef * small_old_ref[...] + mom_coef * small_mom_ref[...] + local_coef * own
        )
        send_ref[:, 2 * block :, :] = jnp.zeros((tiles, 8, LANES), f32)
        for tile, value in enumerate((other, own_terms)):
            for row in range(pl.cdiv(small, LANES)):
                piece = value[:, row * LANES : (row + 1) * LANES]
                at = 2 * block + row
                send_ref[tile, at : at + 1, : piece.shape[1]] = piece

    @pl.when(group == 0)
    def _():
        unflatten_attn(flat, put, rows)
        for k, value in enumerate(attn_tiles(in_ref, out_ref)):
            send_ref[k, block : block + rows, :] += local_coef * value
        base = rows * tiles
        for k in range(tiles):
            columns = slice(k * LANES, (k + 1) * LANES)
            send_ref[k, :mid, :] = up_ref[0, mid:, columns].astype(f32)
            send_ref[k, mid:block, :] = down_ref[0, :, columns].astype(f32)
            send_ref[k, block + rows : 2 * block, :] = flat(base + k, mid, tiles) + (
                local_coef * up_ref[0, :mid, columns].astype(f32)
            )
        values = small_ref[...].astype(f32)
        put_small(values[:, small:], values[:, :small])

    @pl.when(group == 1)
    def _():
        for k, value in enumerate(attn_tiles(in_ref, out_ref)):
            send_ref[k, :rows, :] = value
        for k in range(tiles):
            columns = slice(k * LANES, (k + 1) * LANES)
            send_ref[k, rows:block, :] = up_ref[0, :mid, columns].astype(f32)
            send_ref[k, block : block + mid, :] = flat(k, mid, tiles) + (
                local_coef * up_ref[0, mid:, columns].astype(f32)
            )
        base = mid * tiles
        pairs = tiles * HALF
        low = low_lanes(pairs)
        first, second, third = (flat(base + j, pairs, 3) for j in range(3))
        turned, turned_more = turn(second), turn(third)
        even, odd = pl.ds(0, pairs, stride=2), pl.ds(1, pairs, stride=2)
        wide_ref[0, even, :] = first
        wide_ref[1, even, :] = second
        wide_ref[0, odd, :] = jnp.where(low, turned, turned_more)
        wide_ref[1, odd, :] = turned_more
        start = block + mid
        for k in range(tiles):
            columns = slice(k * LANES, (k + 1) * LANES)
            upper = wide_ref[0, columns, :].T
            lower = wide_ref[1, columns, :].T[:HALF]
            send_ref[k, start : start + LANES, :] = upper + (
                local_coef * down_ref[0, :LANES, columns].astype(f32)
            )
            send_ref[k, start + LANES : 2 * block, :] = lower + (
                local_coef * down_ref[0, LANES:, columns].astype(f32)
            )
        values = small_ref[...].astype(f32)
        put_small(values[:, :small], values[:, small:])


def after_kernel(
    recv_ref, send_ref, in_ref, out_ref, up_ref, down_ref, old_ref, mom_ref, small_ref,
    small_old_ref, small_mom_ref, moment_hbm, *refs,
):
    targets, moment_ref, sources, (sum_ref, wide_ref, sems) = refs[:7], refs[7], refs[8:15], refs[15:]
    (
        in_next_ref, out_next_ref, up_next_ref, down_next_ref, moved_ref, small_next_ref,
        small_moved_ref,
    ) = sources
    copies = [
        pltpu.make_async_copy(source, target, sems.at[k])
        for k, (source, target) in enumerate(zip(sources, targets))
    ]
    copies.append(pltpu.make_async_copy(moment_hbm, moment_ref, sems.at[7]))
    copies[7].start()

    def go(*numbers):
        for k in numbers:
            copies[k].start()

    rows = up_ref.shape[1]
    mid = rows // 2
    block = rows + mid
    tiles = up_ref.shape[2] // LANES
    small = small_old_ref.shape[1]
    group = lax.axis_index("group")

    def put_moved(start, stride, value):
        at = pl.ds(start, value.shape[0], stride=stride)
        moved_ref[at, :] = momentum_coef * mom_ref[at, :] + (old_ref[at, :] - 0.5 * value)

    def get(start, tile):
        return sum_ref[tile, pl.ds(start, rows // 2, stride=2), :]

    def put_attn(tile, value):
        whole = in_ref.shape[-1] // LANES
        if tile < whole:
            in_next_ref[:, tile * LANES : (tile + 1) * LANES] = value
        elif tile == whole:
            in_next_ref[:, tile * LANES :] = value[:, :HALF]
            out_next_ref[:, LANES:] = turn(value)[:, :HALF]
        else:
            out_next_ref[:, :LANES] = value

    def small_row(ref, tile):
        pieces = []
        for row in range(pl.cdiv(small, LANES)):
            at = 2 * block + row
            pieces.append(ref[tile, at : at + 1, : min(LANES, small - row * LANES)])
        return jnp.concatenate(pieces, axis=1)

    def put_small(other, own, first):
        theirs = small_row(recv_ref, 0)
        mine = small_row(send_ref, 1) + local_coef * theirs
        rest = small_row(recv_ref, 1) + local_coef * other
        both = [mine, rest] if first else [rest, mine]
        small_next_ref[...] = jnp.concatenate(both, axis=1).reshape(-1)
        small_moved_ref[...] = momentum_coef * small_mom_ref[...] + (
            small_old_ref[...] - 0.5 * (own + theirs)
        )

    @pl.when(group == 0)
    def _():
        for k, value in enumerate(attn_tiles(in_ref, out_ref)):
            theirs = recv_ref[k, :rows, :]
            put_attn(k, send_ref[k, block : block + rows, :] + local_coef * theirs)
            sum_ref[k, :, :] = value + theirs
        go(0, 1)
        for start, stride, value in flatten_attn(get, rows):
            put_moved(start, stride, value)
        base = rows * tiles
        for k in range(tiles):
            columns = slice(k * LANES, (k + 1) * LANES)
            theirs = recv_ref[k, rows:block, :]
            up_next_ref[:mid, columns] = (
                send_ref[k, block + rows : 2 * block, :] + local_coef * theirs
            )
            put_moved(base + k, tiles, up_ref[0, :mid, columns].astype(f32) + theirs)
            up_next_ref[mid:, columns] = recv_ref[k, block : block + mid, :] + (
                local_coef * up_ref[0, mid:, columns].astype(f32)
            )
            down_next_ref[:, columns] = recv_ref[k, block + mid : 2 * block, :] + (
                local_coef * down_ref[0, :, columns].astype(f32)
            )
        go(2, 3, 4)
        values = small_ref[...].astype(f32)
        put_small(values[:, small:], values[:, :small], True)
        go(5, 6)
        for copy in copies:
            copy.wait()

    @pl.when(group == 1)
    def _():
        for k, value in enumerate(attn_tiles(in_ref, out_ref)):
            put_attn(k, recv_ref[k, block : block + rows, :] + local_coef * value)
        go(0, 1)
        for k in range(tiles):
            columns = slice(k * LANES, (k + 1) * LANES)
            up_next_ref[:mid, columns] = recv_ref[k, block + rows : 2 * block, :] + (
                local_coef * up_ref[0, :mid, columns].astype(f32)
            )
            theirs = recv_ref[k, :mid, :]
            up_next_ref[mid:, columns] = send_ref[k, block : block + mid, :] + local_coef * theirs
            put_moved(k, tiles, up_ref[0, mid:, columns].astype(f32) + theirs)
            theirs = recv_ref[k, mid:block, :]
            down_next_ref[:, columns] = (
                send_ref[k, block + mid : 2 * block, :] + local_coef * theirs
            )
            total = down_ref[0, :, columns].astype(f32) + theirs
            wide_ref[0, columns, :] = total[:LANES].T
            lower = jnp.concatenate([total[LANES:], total[LANES:]], axis=0)
            wide_ref[1, columns, :] = lower.T
        go(2, 3)
        base = mid * tiles
        pairs = tiles * HALF
        low = low_lanes(pairs)
        even, odd = pl.ds(0, pairs, stride=2), pl.ds(1, pairs, stride=2)
        odd_first = turn(wide_ref[0, odd, :])
        put_moved(base, 3, wide_ref[0, even, :])
        put_moved(base + 1, 3, jnp.where(low, wide_ref[1, even, :], odd_first))
        put_moved(base + 2, 3, jnp.where(low, odd_first, wide_ref[1, odd, :]))
        go(4)
        values = small_ref[...].astype(f32)
        put_small(values[:, :small], values[:, small:], False)
        go(5, 6)
        for copy in copies:
            copy.wait()


def dense_before(order, basis_t, operands):
    _, rows, width = operands[2].shape
    rank, depth = basis_t.shape
    return pl.pallas_call(
        before_kernel,
        in_specs=[ANY] + [WHOLE] * 10,
        out_specs=[WHOLE] * 2,
        out_shape=[
            jax.ShapeDtypeStruct((width // LANES, 3 * rows + 8, LANES), f32),
            jax.ShapeDtypeStruct((depth, 3 * rank), bf16),
        ],
        scratch_shapes=[pltpu.VMEM((2, width, LANES), f32)],
        compiler_params=pltpu.CompilerParams(vmem_limit_bytes=4 * 2**20),
        cost_estimate=pl.CostEstimate(
            flops=60000 * rows * width, bytes_accessed=30 * rows * width, transcendentals=0
        ),
        name="dense_before",
    )(order, basis_t, *operands)


def dense_after(received, sent, operands, moment):
    _, rows, width = operands[2].shape
    outs = [matrix.shape[1:] for matrix in operands[:4]]
    outs += [operands[4].shape, operands[6].shape[1:], operands[7].shape]
    return pl.pallas_call(
        after_kernel,
        in_specs=[WHOLE] * 11 + [ANY],
        out_specs=[ANY] * 7 + [WHOLE],
        out_shape=[jax.ShapeDtypeStruct(shape, f32) for shape in (*outs, moment.shape)],
        scratch_shapes=[pltpu.VMEM(shape, f32) for shape in outs]
        + [
            pltpu.VMEM((width // LANES, rows, LANES), f32),
            pltpu.VMEM((2, width, LANES), f32),
            pltpu.SemaphoreType.DMA((8,)),
        ],
        compiler_params=pltpu.CompilerParams(vmem_limit_bytes=8 * 2**20),
        cost_estimate=pl.CostEstimate(
            flops=60000 * rows * width, bytes_accessed=40 * rows * width, transcendentals=0
        ),
        name="dense_after",
    )(received, sent, *operands, *in_hbm([moment]))


def paired(
    attn_in_local,
    attn_out_local,
    ffn_in_local,
    ffn_out_local,
    small_local,
    dense_old,
    dense_momentum,
    small_old,
    small_momentum,
    embed_local,
    embed_old,
    basis,
    coeff_momentum,
):
    swap = [(0, 1), (1, 0)]
    chips = lax.axis_size("shard")

    first, second = (
        [
            (core * chips + chip, (1 - core) * chips + (chip ^ (1 + (core ^ turned(chip) ^ late))))
            for core in range(2)
            for chip in range(chips)
        ]
        for late in range(2)
    )
    axes = ("group", "shard")

    embed = (basis.T, embed_local[0], embed_old)
    theirs = [lax.ppermute(first_part(*embed), "group", swap)]
    late, *mine = other_parts(*embed)
    theirs.append(lax.ppermute(late, "group", swap))

    operands = (
        attn_in_local,
        attn_out_local,
        ffn_in_local,
        jnp.swapaxes(ffn_out_local, 1, 2),
        dense_old.reshape(-1, LANES),
        dense_momentum.reshape(-1, LANES),
        small_local,
        small_old[None, :],
        small_momentum[None, :],
    )
    totals = [add(*pair, flops=10**4) for pair in zip(mine, theirs)]
    moving = [lax.ppermute(total, axes, first) for total in totals]
    sent, stack = dense_before(totals[0], embed[0], operands)
    received = lax.ppermute(sent, "group", swap)
    totals = [
        add(*pair, flops=flops) for *pair, flops in zip(totals, moving, (10**4, 2 * 10**10))
    ]
    moving = [lax.ppermute(total, axes, second) for total in totals]
    *dense, moment = dense_after(received, sent, operands, coeff_momentum)
    moving[0], dense[-1] = lax.optimization_barrier((moving[0], dense[-1]))
    own = [add(totals[0], moving[0], scale=0.5)]
    rest = [lax.ppermute(own[0], "group", swap)]
    early = embed_early(stack, moment, embed_old, own[0])
    own.append(add(totals[1], moving[1], early[:1], scale=0.5))
    rest.append(lax.ppermute(own[1], "group", swap))
    shared = (stack, moment, embed_old)
    done = embed_pieces(
        ((False, 1), (True, 0)), (False, 0), *shared, (own[1], rest[0]), early, ()
    )
    done = embed_pieces(((True, 1),), None, *shared, rest[1:], (), done)
    embed_next, coeff_moved = done

    attn_in_next, attn_out_next, ffn_in_next, ffn_out_next, moved, small_next, small_moved = dense
    return (
        attn_in_next,
        attn_out_next,
        ffn_in_next,
        ffn_out_next.T,
        moved.reshape(dense_old.shape),
        small_next,
        small_moved[0],
        embed_next,
        coeff_moved,
    )


def is_paired(mesh, shapes):
    attn_in, attn_out, ffn_in, ffn_out = (shape[1:] for shape in shapes[:4])
    rows = ffn_in[0]
    return (
        mesh.shape["group"] == 2
        and mesh.shape["shard"] == 4
        and attn_in == (rows, 4 * LANES + HALF)
        and attn_out == (rows, LANES + HALF)
        and ffn_in[1] == 6 * LANES
        and ffn_out == (6 * LANES, rows)
        and rows == LANES + HALF
        and shapes[7][0] <= 8 * LANES
        and shapes[10][1] % (8 * LANES) == 0
    )


def solution(mesh):
    placed = (
        P("group", "shard", "tensor"),
        P("group", "shard", "tensor"),
        P("group", "shard", "tensor"),
        P("group", "shard", "tensor"),
        P("group", None),
        P(("shard", "tensor"), "group"),
        P(("shard", "tensor"), "group"),
        P("group"),
        P("group"),
        P("group", "shard", "tensor"),
        P("shard", "tensor"),
        P("shard", None),
        P(None, "tensor"),
    )

    def shards(*args):
        plan = paired if is_paired(mesh, [arg.shape for arg in args]) else general
        return plan(*args)

    return jax.shard_map(
        shards,
        mesh=mesh,
        in_specs=placed,
        out_specs=(
            P("shard", "tensor"),
            P("shard", "tensor"),
            P("shard", "tensor"),
            P("shard", "tensor"),
            P(("shard", "tensor"), "group"),
            P(),
            P("group"),
            P("shard", "tensor"),
            P(None, "tensor"),
        ),
        check_vma=False,
    )
```

```python
import functools

import jax
import jax.numpy as jnp
from jax import lax
from jax.experimental import pallas as pl
from jax.experimental.pallas import tpu as pltpu
from jax.sharding import PartitionSpec as P

momentum_coef = 0.5
outer_rate = 0.7

f32 = jnp.float32
bf16 = jnp.bfloat16
LANES = 128
HALF = LANES // 2


def nesterov(old_value, momentum, delta):
    moved = momentum_coef * momentum + delta
    return (old_value - outer_rate * (delta + momentum_coef * moved), moved)


def general(
    attn_in_local,
    attn_out_local,
    ffn_in_local,
    ffn_out_local,
    small_local,
    dense_old,
    dense_momentum,
    small_old,
    small_momentum,
    embed_local,
    embed_old,
    basis,
    coeff_momentum,
):
    groups = lax.axis_size("group")
    matrices = (attn_in_local, attn_out_local, ffn_in_local, ffn_out_local)
    local_terms = jnp.concatenate([matrix[0].reshape(-1) for matrix in matrices]).astype(f32)
    small_terms = small_local[0].astype(f32)
    old_flat = dense_old[0]
    momentum_flat = dense_momentum[0]
    dense_part, small_part = (
        lax.psum_scatter(local_terms, "group", scatter_dimension=0, tiled=True),
        lax.psum_scatter(small_terms, "group", scatter_dimension=0, tiled=True),
    )
    dense_new, dense_moved = nesterov(old_flat, momentum_flat, old_flat - dense_part / groups)
    small_new, small_moved = nesterov(small_old, small_momentum, small_old - small_part / groups)
    full_flat, small_next = (
        lax.all_gather(dense_new, "group", axis=0, tiled=True),
        lax.all_gather(small_new, "group", axis=0, tiled=True),
    )
    results = []
    offset = 0
    for matrix in matrices:
        block_size = matrix.shape[1] * matrix.shape[2]
        results.append(
            full_flat[offset : offset + block_size].reshape(matrix.shape[1], matrix.shape[2])
        )
        offset = offset + block_size
    difference = embed_old - embed_local[0].astype(f32)
    partial_coeff = lax.dot_general(
        basis,
        difference,
        (((0,), (0,)), ((), ())),
        precision=lax.Precision.HIGHEST,
        preferred_element_type=f32,
    )
    coeff = lax.psum(partial_coeff, ("group", "shard")) / groups
    coeff_moved = momentum_coef * coeff_momentum + coeff
    update = coeff + momentum_coef * coeff_moved
    embed_next = embed_old - outer_rate * jnp.dot(
        basis, update, precision=lax.Precision.HIGHEST, preferred_element_type=f32
    )
    return (
        results[0],
        results[1],
        results[2],
        results[3],
        dense_moved[None, :],
        small_next,
        small_moved,
        embed_next,
        coeff_moved,
    )


local_coef = outer_rate * (1 + momentum_coef) / 2
old_coef = 1 - outer_rate * (1 + momentum_coef)
mom_coef = -outer_rate * momentum_coef * momentum_coef


def split(value):
    high = value.astype(bf16)
    return high, (value - high.astype(f32)).astype(bf16)


CHUNKS = 2
WHOLE = pl.BlockSpec(memory_space=pltpu.VMEM)
ANY = pl.BlockSpec(memory_space=pl.ANY)


def in_hbm(arrays):
    return [pltpu.with_memory_space_constraint(array, pltpu.HBM) for array in arrays]


def turned(chip):
    return (chip ^ (chip >> 1)) & 1


def side_start(other, columns):
    side = lax.axis_index("group") ^ turned(lax.axis_index("shard"))
    return (1 - side if other else side) * columns


def both_parts(basis):
    return jnp.concatenate(split(basis), axis=0)


def doubled_product(both, local, old):
    rank = both.shape[0] // 2
    diff_high, diff_low = split(2 * old - local.astype(f32))
    first = jnp.dot(both, diff_high, preferred_element_type=f32)
    second = jnp.dot(both[:rank], diff_low, preferred_element_type=f32)
    return first[:rank] + first[rank:] + second


def local_product(both, local):
    rank = both.shape[0] // 2
    first = jnp.dot(both, local, preferred_element_type=f32)
    return -(first[:rank] + first[rank:])


def first_kernel(basis_hbm, local_hbm, out_ref, *refs):
    *held, sems = refs
    columns = out_ref.shape[1]
    there = pl.ds(pl.multiple_of(side_start(True, CHUNKS * columns), columns), columns)
    copies = [
        pltpu.make_async_copy(source, target, sems.at[k])
        for k, (source, target) in enumerate(zip((basis_hbm, local_hbm.at[:, there]), held))
    ]
    for copy in copies:
        copy.start()
    for copy in copies:
        copy.wait()
    basis_ref, local_ref = held
    out_ref[...] = local_product(both_parts(basis_ref[...]), local_ref[...])


def first_part(basis_t, local):
    rank, depth = basis_t.shape
    block = local.shape[1] // (2 * CHUNKS)
    return pl.pallas_call(
        first_kernel,
        in_specs=[ANY] * 2,
        out_specs=WHOLE,
        out_shape=jax.ShapeDtypeStruct((rank, block), f32),
        scratch_shapes=[
            pltpu.VMEM((rank, depth), f32),
            pltpu.VMEM((depth, block), bf16),
            pltpu.SemaphoreType.DMA((2,)),
        ],
        compiler_params=pltpu.CompilerParams(vmem_limit_bytes=4 * 2**20),
        cost_estimate=pl.CostEstimate(
            flops=2 * 10**9, bytes_accessed=2 * depth * block, transcendentals=0
        ),
        name="first_part",
    )(*in_hbm((basis_t, local)))


def other_kernel(basis_ref, local_ref, old_ref, rest_ref, *out_refs):
    block = rest_ref.shape[1]
    columns = CHUNKS * block
    both = both_parts(basis_ref[...])

    def there(other, part):
        start = side_start(other, columns) + part * block
        return pl.ds(pl.multiple_of(start, block), block)

    rest_ref[...] = local_product(both, local_ref[:, there(True, 1)])
    for k, out_ref in enumerate(out_refs):
        here = there(False, k)
        out_ref[...] = doubled_product(both, local_ref[:, here], old_ref[:, here])


def other_parts(basis_t, local, old):
    rank, depth = basis_t.shape
    block = old.shape[1] // (2 * CHUNKS)
    return pl.pallas_call(
        other_kernel,
        in_specs=[WHOLE] * 3,
        out_specs=[WHOLE] * (CHUNKS + 1),
        out_shape=[jax.ShapeDtypeStruct((rank, block), f32)] * (CHUNKS + 1),
        compiler_params=pltpu.CompilerParams(vmem_limit_bytes=4 * 2**20),
        cost_estimate=pl.CostEstimate(
            flops=10**10, bytes_accessed=18 * depth * block, transcendentals=0
        ),
        name="other_parts",
    )(basis_t, local, old)


def add_kernel(scale, first_ref, second_ref, *refs):
    refs[-1][...] = scale * (first_ref[...] + second_ref[...])


def add(first, second, after=(), scale=1.0, flops=2 * 10**10):
    return pl.pallas_call(
        functools.partial(add_kernel, scale),
        in_specs=[WHOLE] * 2 + [ANY] * len(after),
        out_specs=WHOLE,
        out_shape=jax.ShapeDtypeStruct(first.shape, f32),
        compiler_params=pltpu.CompilerParams(vmem_limit_bytes=2 * 2**20),
        cost_estimate=pl.CostEstimate(flops=flops, bytes_accessed=0, transcendentals=0),
        name="add",
    )(first, second, *after)


def embed_piece(start, width, coeff, stack_ref, moment_ref, old_ref):
    there = pl.ds(pl.multiple_of(start, width), width)
    moved = momentum_coef * moment_ref[:, there] + coeff
    up_high, up_low = split(coeff + momentum_coef * moved)
    change = jnp.dot(
        stack_ref[...],
        jnp.concatenate([up_high, up_high, up_low], axis=0),
        preferred_element_type=f32,
    )
    return old_ref[:, there] - outer_rate * change, moved


def early_kernel(stack_ref, moment_ref, old_ref, coeff_ref, embed_ref, moved_ref):
    start = side_start(False, old_ref.shape[1] // 2)
    embed_ref[...], moved_ref[...] = embed_piece(
        start, coeff_ref.shape[1], coeff_ref[...], stack_ref, moment_ref, old_ref
    )


def embed_early(stack, moment, old, coeff):
    depth, (rank, width) = old.shape[0], coeff.shape
    return pl.pallas_call(
        early_kernel,
        in_specs=[WHOLE] * 4,
        out_specs=[WHOLE] * 2,
        out_shape=[
            jax.ShapeDtypeStruct((depth, width), f32),
            jax.ShapeDtypeStruct((rank, width), f32),
        ],
        compiler_params=pltpu.CompilerParams(vmem_limit_bytes=4 * 2**20),
        cost_estimate=pl.CostEstimate(
            flops=6 * rank * depth * width, bytes_accessed=8 * depth * width, transcendentals=0
        ),
        name="embed_early",
    )(stack, moment, old, coeff)


def embed_kernel(pieces, ready, stack_ref, moment_ref, old_ref, *refs):
    count = len(pieces)
    coeffs, refs = refs[:count], refs[count:]
    embed_hbm, moved_hbm, embed_ref, moved_ref, sems = refs[-5:]
    width = coeffs[0].shape[1]
    copies = []

    def start_of(other, part):
        return side_start(other, old_ref.shape[1] // 2) + part * width

    def send(start, embed, moved):
        there = pl.ds(pl.multiple_of(start, width), width)
        for source, target in ((moved, moved_hbm), (embed, embed_hbm)):
            copies.append(
                pltpu.make_async_copy(source, target.at[:, there], sems.at[len(copies)])
            )
            copies[-1].start()

    if ready:
        send(start_of(*ready), refs[0], refs[1])
    for k, piece in enumerate(pieces):
        start = start_of(*piece)
        embed_ref[k], moved_ref[k] = embed_piece(
            start, width, coeffs[k][...], stack_ref, moment_ref, old_ref
        )
        send(start, embed_ref.at[k], moved_ref.at[k])
    for copy in copies:
        copy.wait()


def embed_pieces(pieces, ready, stack, moment, old, coeffs, early, before):
    count = len(pieces)
    rank, width = coeffs[0].shape
    first = 3 + count + len(early)
    return pl.pallas_call(
        functools.partial(embed_kernel, pieces, ready),
        in_specs=[WHOLE] * first + [ANY] * len(before),
        out_specs=[ANY, ANY],
        out_shape=[
            jax.ShapeDtypeStruct(old.shape, f32),
            jax.ShapeDtypeStruct(moment.shape, f32),
        ],
        scratch_shapes=[
            pltpu.VMEM((count, old.shape[0], width), f32),
            pltpu.VMEM((count, rank, width), f32),
            pltpu.SemaphoreType.DMA((2 * count + len(early),)),
        ],
        input_output_aliases={first: 0, first + 1: 1} if before else {},
        compiler_params=pltpu.CompilerParams(vmem_limit_bytes=8 * 2**20),
        cost_estimate=pl.CostEstimate(
            flops=6 * count * rank * old.shape[0] * width,
            bytes_accessed=8 * count * old.shape[0] * width,
            transcendentals=0,
        ),
        name="embed_pieces",
    )(stack, moment, old, *coeffs, *early, *before)


def low_lanes(rows):
    return lax.broadcasted_iota(jnp.int32, (rows, LANES), 1) < HALF


def turn(value):
    return pltpu.roll(value, HALF, 1)


def attn_tiles(in_ref, out_ref):
    whole = in_ref.shape[-1] // LANES
    tiles = [in_ref[0, :, k * LANES : (k + 1) * LANES].astype(f32) for k in range(whole)]
    last = in_ref[0, :, whole * LANES :].astype(f32)
    side = out_ref[0, :, LANES:].astype(f32)
    tiles.append(jnp.concatenate([last, side], axis=-1))
    tiles.append(out_ref[0, :, :LANES].astype(f32))
    return tiles


def unflatten_attn(flat, put, rows):
    pairs = rows // 2
    low = low_lanes(pairs)
    inner = [flat(j, pairs, 9) for j in range(9)]
    base = pairs * 9
    outer = [flat(base + j, pairs, 3) for j in range(3)]
    turned = [turn(inner[j]) for j in range(4, 9)]
    turned_out = [turn(outer[j]) for j in (1, 2)]
    for k in range(4):
        put(0, k, inner[k])
        put(1, k, jnp.where(low, turned[k], turned[k + 1]))
    put(0, 4, jnp.where(low, inner[4], turned_out[0]))
    put(1, 4, jnp.where(low, turned[4], outer[2]))
    put(0, 5, outer[0])
    put(1, 5, jnp.where(low, turned_out[0], turned_out[1]))


def flatten_attn(get, rows):
    pairs = rows // 2
    low = low_lanes(pairs)
    even = [get(0, k) for k in range(6)]
    odd = [get(1, k) for k in range(6)]
    turned = [turn(odd[k]) for k in range(5)]
    pieces = [(k, 9, even[k]) for k in range(4)]
    pieces.append((4, 9, jnp.where(low, even[4], turned[0])))
    for k in range(4):
        pieces.append((5 + k, 9, jnp.where(low, turned[k], turned[k + 1])))
    base = pairs * 9
    pieces.append((base, 3, even[5]))
    turned_out = turn(odd[5])
    pieces.append((base + 1, 3, jnp.where(low, turn(even[4]), turned_out)))
    pieces.append((base + 2, 3, jnp.where(low, turned_out, odd[4])))
    return pieces


def before_kernel(
    order_ref, basis_ref, in_ref, out_ref, up_ref, down_ref, old_ref, mom_ref, small_ref,
    small_old_ref, small_mom_ref, send_ref, stack_ref, wide_ref,
):
    del order_ref
    basis = basis_ref[...]
    high = basis.astype(bf16).astype(f32)
    stack_ref[...] = jnp.concatenate([high, basis - high, high], axis=0).T.astype(bf16)
    group = lax.axis_index("group")
    rows = up_ref.shape[1]
    mid = rows // 2
    block = rows + mid
    tiles = up_ref.shape[2] // LANES
    small = small_old_ref.shape[1]

    def flat(start, count, stride):
        at = pl.ds(start, count, stride=stride)
        return old_coef * old_ref[at, :] + mom_coef * mom_ref[at, :]

    def put(start, tile, value):
        send_ref[tile, pl.ds(block + start, rows // 2, stride=2), :] = value

    def put_small(other, own):
        own_terms = (
            old_coef * small_old_ref[...] + mom_coef * small_mom_ref[...] + local_coef * own
        )
        send_ref[:, 2 * block :, :] = jnp.zeros((tiles, 8, LANES), f32)
        for tile, value in enumerate((other, own_terms)):
            for row in range(pl.cdiv(small, LANES)):
                piece = value[:, row * LANES : (row + 1) * LANES]
                at = 2 * block + row
                send_ref[tile, at : at + 1, : piece.shape[1]] = piece

    @pl.when(group == 0)
    def _():
        unflatten_attn(flat, put, rows)
        for k, value in enumerate(attn_tiles(in_ref, out_ref)):
            send_ref[k, block : block + rows, :] += local_coef * value
        base = rows * tiles
        for k in range(tiles):
            columns = slice(k * LANES, (k + 1) * LANES)
            send_ref[k, :mid, :] = up_ref[0, mid:, columns].astype(f32)
            send_ref[k, mid:block, :] = down_ref[0, :, columns].astype(f32)
            send_ref[k, block + rows : 2 * block, :] = flat(base + k, mid, tiles) + (
                local_coef * up_ref[0, :mid, columns].astype(f32)
            )
        values = small_ref[...].astype(f32)
        put_small(values[:, small:], values[:, :small])

    @pl.when(group == 1)
    def _():
        for k, value in enumerate(attn_tiles(in_ref, out_ref)):
            send_ref[k, :rows, :] = value
        for k in range(tiles):
            columns = slice(k * LANES, (k + 1) * LANES)
            send_ref[k, rows:block, :] = up_ref[0, :mid, columns].astype(f32)
            send_ref[k, block : block + mid, :] = flat(k, mid, tiles) + (
                local_coef * up_ref[0, mid:, columns].astype(f32)
            )
        base = mid * tiles
        pairs = tiles * HALF
        low = low_lanes(pairs)
        first, second, third = (flat(base + j, pairs, 3) for j in range(3))
        turned, turned_more = turn(second), turn(third)
        even, odd = pl.ds(0, pairs, stride=2), pl.ds(1, pairs, stride=2)
        wide_ref[0, even, :] = first
        wide_ref[1, even, :] = second
        wide_ref[0, odd, :] = jnp.where(low, turned, turned_more)
        wide_ref[1, odd, :] = turned_more
        start = block + mid
        for k in range(tiles):
            columns = slice(k * LANES, (k + 1) * LANES)
            upper = wide_ref[0, columns, :].T
            lower = wide_ref[1, columns, :].T[:HALF]
            send_ref[k, start : start + LANES, :] = upper + (
                local_coef * down_ref[0, :LANES, columns].astype(f32)
            )
            send_ref[k, start + LANES : 2 * block, :] = lower + (
                local_coef * down_ref[0, LANES:, columns].astype(f32)
            )
        values = small_ref[...].astype(f32)
        put_small(values[:, :small], values[:, small:])


def after_kernel(
    recv_ref, send_ref, in_ref, out_ref, up_ref, down_ref, old_ref, mom_ref, small_ref,
    small_old_ref, small_mom_ref, moment_hbm, *refs,
):
    targets, moment_ref, sources, (sum_ref, wide_ref, sems) = refs[:7], refs[7], refs[8:15], refs[15:]
    (
        in_next_ref, out_next_ref, up_next_ref, down_next_ref, moved_ref, small_next_ref,
        small_moved_ref,
    ) = sources
    copies = [
        pltpu.make_async_copy(source, target, sems.at[k])
        for k, (source, target) in enumerate(zip(sources, targets))
    ]
    copies.append(pltpu.make_async_copy(moment_hbm, moment_ref, sems.at[7]))
    copies[7].start()

    def go(*numbers):
        for k in numbers:
            copies[k].start()

    rows = up_ref.shape[1]
    mid = rows // 2
    block = rows + mid
    tiles = up_ref.shape[2] // LANES
    small = small_old_ref.shape[1]
    group = lax.axis_index("group")

    def put_moved(start, stride, value):
        at = pl.ds(start, value.shape[0], stride=stride)
        moved_ref[at, :] = momentum_coef * mom_ref[at, :] + (old_ref[at, :] - 0.5 * value)

    def get(start, tile):
        return sum_ref[tile, pl.ds(start, rows // 2, stride=2), :]

    def put_attn(tile, value):
        whole = in_ref.shape[-1] // LANES
        if tile < whole:
            in_next_ref[:, tile * LANES : (tile + 1) * LANES] = value
        elif tile == whole:
            in_next_ref[:, tile * LANES :] = value[:, :HALF]
            out_next_ref[:, LANES:] = turn(value)[:, :HALF]
        else:
            out_next_ref[:, :LANES] = value

    def small_row(ref, tile):
        pieces = []
        for row in range(pl.cdiv(small, LANES)):
            at = 2 * block + row
            pieces.append(ref[tile, at : at + 1, : min(LANES, small - row * LANES)])
        return jnp.concatenate(pieces, axis=1)

    def put_small(other, own, first):
        theirs = small_row(recv_ref, 0)
        mine = small_row(send_ref, 1) + local_coef * theirs
        rest = small_row(recv_ref, 1) + local_coef * other
        both = [mine, rest] if first else [rest, mine]
        small_next_ref[...] = jnp.concatenate(both, axis=1).reshape(-1)
        small_moved_ref[...] = momentum_coef * small_mom_ref[...] + (
            small_old_ref[...] - 0.5 * (own + theirs)
        )

    @pl.when(group == 0)
    def _():
        for k, value in enumerate(attn_tiles(in_ref, out_ref)):
            theirs = recv_ref[k, :rows, :]
            put_attn(k, send_ref[k, block : block + rows, :] + local_coef * theirs)
            sum_ref[k, :, :] = value + theirs
        go(0, 1)
        for start, stride, value in flatten_attn(get, rows):
            put_moved(start, stride, value)
        base = rows * tiles
        for k in range(tiles):
            columns = slice(k * LANES, (k + 1) * LANES)
            theirs = recv_ref[k, rows:block, :]
            up_next_ref[:mid, columns] = (
                send_ref[k, block + rows : 2 * block, :] + local_coef * theirs
            )
            put_moved(base + k, tiles, up_ref[0, :mid, columns].astype(f32) + theirs)
            up_next_ref[mid:, columns] = recv_ref[k, block : block + mid, :] + (
                local_coef * up_ref[0, mid:, columns].astype(f32)
            )
            down_next_ref[:, columns] = recv_ref[k, block + mid : 2 * block, :] + (
                local_coef * down_ref[0, :, columns].astype(f32)
            )
        go(2, 3, 4)
        values = small_ref[...].astype(f32)
        put_small(values[:, small:], values[:, :small], True)
        go(5, 6)
        for copy in copies:
            copy.wait()

    @pl.when(group == 1)
    def _():
        for k, value in enumerate(attn_tiles(in_ref, out_ref)):
            put_attn(k, recv_ref[k, block : block + rows, :] + local_coef * value)
        go(0, 1)
        for k in range(tiles):
            columns = slice(k * LANES, (k + 1) * LANES)
            up_next_ref[:mid, columns] = recv_ref[k, block + rows : 2 * block, :] + (
                local_coef * up_ref[0, :mid, columns].astype(f32)
            )
            theirs = recv_ref[k, :mid, :]
            up_next_ref[mid:, columns] = send_ref[k, block : block + mid, :] + local_coef * theirs
            put_moved(k, tiles, up_ref[0, mid:, columns].astype(f32) + theirs)
            theirs = recv_ref[k, mid:block, :]
            down_next_ref[:, columns] = (
                send_ref[k, block + mid : 2 * block, :] + local_coef * theirs
            )
            total = down_ref[0, :, columns].astype(f32) + theirs
            wide_ref[0, columns, :] = total[:LANES].T
            lower = jnp.concatenate([total[LANES:], total[LANES:]], axis=0)
            wide_ref[1, columns, :] = lower.T
        go(2, 3)
        base = mid * tiles
        pairs = tiles * HALF
        low = low_lanes(pairs)
        even, odd = pl.ds(0, pairs, stride=2), pl.ds(1, pairs, stride=2)
        odd_first = turn(wide_ref[0, odd, :])
        put_moved(base, 3, wide_ref[0, even, :])
        put_moved(base + 1, 3, jnp.where(low, wide_ref[1, even, :], odd_first))
        put_moved(base + 2, 3, jnp.where(low, odd_first, wide_ref[1, odd, :]))
        go(4)
        values = small_ref[...].astype(f32)
        put_small(values[:, :small], values[:, small:], False)
        go(5, 6)
        for copy in copies:
            copy.wait()


def dense_before(order, basis_t, operands):
    _, rows, width = operands[2].shape
    rank, depth = basis_t.shape
    return pl.pallas_call(
        before_kernel,
        in_specs=[ANY] + [WHOLE] * 10,
        out_specs=[WHOLE] * 2,
        out_shape=[
            jax.ShapeDtypeStruct((width // LANES, 3 * rows + 8, LANES), f32),
            jax.ShapeDtypeStruct((depth, 3 * rank), bf16),
        ],
        scratch_shapes=[pltpu.VMEM((2, width, LANES), f32)],
        compiler_params=pltpu.CompilerParams(vmem_limit_bytes=4 * 2**20),
        cost_estimate=pl.CostEstimate(
            flops=60000 * rows * width, bytes_accessed=30 * rows * width, transcendentals=0
        ),
        name="dense_before",
    )(order, basis_t, *operands)


def dense_after(received, sent, operands, moment):
    _, rows, width = operands[2].shape
    outs = [matrix.shape[1:] for matrix in operands[:4]]
    outs += [operands[4].shape, operands[6].shape[1:], operands[7].shape]
    return pl.pallas_call(
        after_kernel,
        in_specs=[WHOLE] * 11 + [ANY],
        out_specs=[ANY] * 7 + [WHOLE],
        out_shape=[jax.ShapeDtypeStruct(shape, f32) for shape in (*outs, moment.shape)],
        scratch_shapes=[pltpu.VMEM(shape, f32) for shape in outs]
        + [
            pltpu.VMEM((width // LANES, rows, LANES), f32),
            pltpu.VMEM((2, width, LANES), f32),
            pltpu.SemaphoreType.DMA((8,)),
        ],
        compiler_params=pltpu.CompilerParams(vmem_limit_bytes=8 * 2**20),
        cost_estimate=pl.CostEstimate(
            flops=60000 * rows * width, bytes_accessed=40 * rows * width, transcendentals=0
        ),
        name="dense_after",
    )(received, sent, *operands, *in_hbm([moment]))


def paired(
    attn_in_local,
    attn_out_local,
    ffn_in_local,
    ffn_out_local,
    small_local,
    dense_old,
    dense_momentum,
    small_old,
    small_momentum,
    embed_local,
    embed_old,
    basis,
    coeff_momentum,
):
    swap = [(0, 1), (1, 0)]
    chips = lax.axis_size("shard")

    first, second = (
        [
            (core * chips + chip, (1 - core) * chips + (chip ^ (1 + (core ^ turned(chip) ^ late))))
            for core in range(2)
            for chip in range(chips)
        ]
        for late in range(2)
    )
    axes = ("group", "shard")

    embed = (basis.T, embed_local[0], embed_old)
    theirs = [lax.ppermute(first_part(*embed[:2]), "group", swap)]
    late, *mine = other_parts(*embed)
    theirs.append(lax.ppermute(late, "group", swap))

    operands = (
        attn_in_local,
        attn_out_local,
        ffn_in_local,
        jnp.swapaxes(ffn_out_local, 1, 2),
        dense_old.reshape(-1, LANES),
        dense_momentum.reshape(-1, LANES),
        small_local,
        small_old[None, :],
        small_momentum[None, :],
    )
    totals = [add(*pair, flops=10**4) for pair in zip(mine, theirs)]
    moving = [lax.ppermute(total, axes, first) for total in totals]
    sent, stack = dense_before(totals[0], embed[0], operands)
    received = lax.ppermute(sent, "group", swap)
    totals = [
        add(*pair, flops=flops) for *pair, flops in zip(totals, moving, (10**4, 2 * 10**10))
    ]
    moving = [lax.ppermute(total, axes, second) for total in totals]
    *dense, moment = dense_after(received, sent, operands, coeff_momentum)
    moving[0], dense[-1] = lax.optimization_barrier((moving[0], dense[-1]))
    own = [add(totals[0], moving[0], scale=0.5)]
    rest = [lax.ppermute(own[0], "group", swap)]
    early = embed_early(stack, moment, embed_old, own[0])
    own.append(add(totals[1], moving[1], early[:1], scale=0.5))
    rest.append(lax.ppermute(own[1], "group", swap))
    shared = (stack, moment, embed_old)
    done = embed_pieces(
        ((False, 1), (True, 0)), (False, 0), *shared, (own[1], rest[0]), early, ()
    )
    done = embed_pieces(((True, 1),), None, *shared, rest[1:], (), done)
    embed_next, coeff_moved = done

    attn_in_next, attn_out_next, ffn_in_next, ffn_out_next, moved, small_next, small_moved = dense
    return (
        attn_in_next,
        attn_out_next,
        ffn_in_next,
        ffn_out_next.T,
        moved.reshape(dense_old.shape),
        small_next,
        small_moved[0],
        embed_next,
        coeff_moved,
    )


def is_paired(mesh, shapes):
    attn_in, attn_out, ffn_in, ffn_out = (shape[1:] for shape in shapes[:4])
    rows = ffn_in[0]
    return (
        mesh.shape["group"] == 2
        and mesh.shape["shard"] == 4
        and attn_in == (rows, 4 * LANES + HALF)
        and attn_out == (rows, LANES + HALF)
        and ffn_in[1] == 6 * LANES
        and ffn_out == (6 * LANES, rows)
        and rows == LANES + HALF
        and shapes[7][0] <= 8 * LANES
        and shapes[10][1] % (8 * LANES) == 0
    )


def solution(mesh):
    placed = (
        P("group", "shard", "tensor"),
        P("group", "shard", "tensor"),
        P("group", "shard", "tensor"),
        P("group", "shard", "tensor"),
        P("group", None),
        P(("shard", "tensor"), "group"),
        P(("shard", "tensor"), "group"),
        P("group"),
        P("group"),
        P("group", "shard", "tensor"),
        P("shard", "tensor"),
        P("shard", None),
        P(None, "tensor"),
    )

    def shards(*args):
        plan = paired if is_paired(mesh, [arg.shape for arg in args]) else general
        return plan(*args)

    return jax.shard_map(
        shards,
        mesh=mesh,
        in_specs=placed,
        out_specs=(
            P("shard", "tensor"),
            P("shard", "tensor"),
            P("shard", "tensor"),
            P("shard", "tensor"),
            P(("shard", "tensor"), "group"),
            P(),
            P("group"),
            P("shard", "tensor"),
            P(None, "tensor"),
        ),
        check_vma=False,
    )
```

```python
import functools

import jax
import jax.numpy as jnp
from jax import lax
from jax.experimental import pallas as pl
from jax.experimental.pallas import tpu as pltpu
from jax.sharding import PartitionSpec as P

momentum_coef = 0.5
outer_rate = 0.7

f32 = jnp.float32
bf16 = jnp.bfloat16
LANES = 128
HALF = LANES // 2


def nesterov(old_value, momentum, delta):
    moved = momentum_coef * momentum + delta
    return (old_value - outer_rate * (delta + momentum_coef * moved), moved)


def general(
    attn_in_local,
    attn_out_local,
    ffn_in_local,
    ffn_out_local,
    small_local,
    dense_old,
    dense_momentum,
    small_old,
    small_momentum,
    embed_local,
    embed_old,
    basis,
    coeff_momentum,
):
    groups = lax.axis_size("group")
    matrices = (attn_in_local, attn_out_local, ffn_in_local, ffn_out_local)
    local_terms = jnp.concatenate([matrix[0].reshape(-1) for matrix in matrices]).astype(f32)
    small_terms = small_local[0].astype(f32)
    old_flat = dense_old[0]
    momentum_flat = dense_momentum[0]
    dense_part, small_part = (
        lax.psum_scatter(local_terms, "group", scatter_dimension=0, tiled=True),
        lax.psum_scatter(small_terms, "group", scatter_dimension=0, tiled=True),
    )
    dense_new, dense_moved = nesterov(old_flat, momentum_flat, old_flat - dense_part / groups)
    small_new, small_moved = nesterov(small_old, small_momentum, small_old - small_part / groups)
    full_flat, small_next = (
        lax.all_gather(dense_new, "group", axis=0, tiled=True),
        lax.all_gather(small_new, "group", axis=0, tiled=True),
    )
    results = []
    offset = 0
    for matrix in matrices:
        block_size = matrix.shape[1] * matrix.shape[2]
        results.append(
            full_flat[offset : offset + block_size].reshape(matrix.shape[1], matrix.shape[2])
        )
        offset = offset + block_size
    difference = embed_old - embed_local[0].astype(f32)
    partial_coeff = lax.dot_general(
        basis,
        difference,
        (((0,), (0,)), ((), ())),
        precision=lax.Precision.HIGHEST,
        preferred_element_type=f32,
    )
    coeff = lax.psum(partial_coeff, ("group", "shard")) / groups
    coeff_moved = momentum_coef * coeff_momentum + coeff
    update = coeff + momentum_coef * coeff_moved
    embed_next = embed_old - outer_rate * jnp.dot(
        basis, update, precision=lax.Precision.HIGHEST, preferred_element_type=f32
    )
    return (
        results[0],
        results[1],
        results[2],
        results[3],
        dense_moved[None, :],
        small_next,
        small_moved,
        embed_next,
        coeff_moved,
    )


local_coef = outer_rate * (1 + momentum_coef) / 2
old_coef = 1 - outer_rate * (1 + momentum_coef)
mom_coef = -outer_rate * momentum_coef * momentum_coef


def split(value):
    high = value.astype(bf16)
    return high, (value - high.astype(f32)).astype(bf16)


CHUNKS = 2
WHOLE = pl.BlockSpec(memory_space=pltpu.VMEM)
ANY = pl.BlockSpec(memory_space=pl.ANY)


def in_hbm(arrays):
    return [pltpu.with_memory_space_constraint(array, pltpu.HBM) for array in arrays]


def turned(chip):
    return (chip ^ (chip >> 1)) & 1


def side_start(other, columns):
    side = lax.axis_index("group") ^ turned(lax.axis_index("shard"))
    return (1 - side if other else side) * columns


def both_parts(basis):
    return jnp.concatenate(split(basis), axis=0)


def doubled_product(both, local, old):
    rank = both.shape[0] // 2
    diff_high, diff_low = split(2 * old - local.astype(f32))
    first = jnp.dot(both, diff_high, preferred_element_type=f32)
    second = jnp.dot(both[:rank], diff_low, preferred_element_type=f32)
    return first[:rank] + first[rank:] + second


def local_product(both, local):
    rank = both.shape[0] // 2
    first = jnp.dot(both, local, preferred_element_type=f32)
    return -(first[:rank] + first[rank:])


def first_kernel(basis_hbm, local_hbm, out_ref, *refs):
    *held, sems = refs
    columns = out_ref.shape[1]
    there = pl.ds(pl.multiple_of(side_start(True, CHUNKS * columns), columns), columns)
    copies = [
        pltpu.make_async_copy(source, target, sems.at[k])
        for k, (source, target) in enumerate(zip((basis_hbm, local_hbm.at[:, there]), held))
    ]
    for copy in copies:
        copy.start()
    for copy in copies:
        copy.wait()
    basis_ref, local_ref = held
    out_ref[...] = local_product(both_parts(basis_ref[...]), local_ref[...])


def first_part(basis_t, local):
    rank, depth = basis_t.shape
    block = local.shape[1] // (2 * CHUNKS)
    return pl.pallas_call(
        first_kernel,
        in_specs=[ANY] * 2,
        out_specs=WHOLE,
        out_shape=jax.ShapeDtypeStruct((rank, block), f32),
        scratch_shapes=[
            pltpu.VMEM((rank, depth), f32),
            pltpu.VMEM((depth, block), bf16),
            pltpu.SemaphoreType.DMA((2,)),
        ],
        compiler_params=pltpu.CompilerParams(vmem_limit_bytes=4 * 2**20),
        cost_estimate=pl.CostEstimate(
            flops=2 * 10**9, bytes_accessed=2 * depth * block, transcendentals=0
        ),
        name="first_part",
    )(*in_hbm((basis_t, local)))


def other_kernel(basis_ref, local_ref, old_ref, rest_ref, *out_refs):
    block = rest_ref.shape[1]
    columns = CHUNKS * block
    both = both_parts(basis_ref[...])

    def there(other, part):
        start = side_start(other, columns) + part * block
        return pl.ds(pl.multiple_of(start, block), block)

    rest_ref[...] = local_product(both, local_ref[:, there(True, 1)])
    for k, out_ref in enumerate(out_refs):
        here = there(False, k)
        out_ref[...] = doubled_product(both, local_ref[:, here], old_ref[:, here])


def other_parts(basis_t, local, old):
    rank, depth = basis_t.shape
    block = old.shape[1] // (2 * CHUNKS)
    return pl.pallas_call(
        other_kernel,
        in_specs=[WHOLE] * 3,
        out_specs=[WHOLE] * (CHUNKS + 1),
        out_shape=[jax.ShapeDtypeStruct((rank, block), f32)] * (CHUNKS + 1),
        compiler_params=pltpu.CompilerParams(vmem_limit_bytes=4 * 2**20),
        cost_estimate=pl.CostEstimate(
            flops=10**10, bytes_accessed=18 * depth * block, transcendentals=0
        ),
        name="other_parts",
    )(basis_t, local, old)


def add_kernel(scale, first_ref, second_ref, *refs):
    refs[-1][...] = scale * (first_ref[...] + second_ref[...])


def add(first, second, after=(), scale=1.0, flops=2 * 10**10):
    return pl.pallas_call(
        functools.partial(add_kernel, scale),
        in_specs=[WHOLE] * 2 + [ANY] * len(after),
        out_specs=WHOLE,
        out_shape=jax.ShapeDtypeStruct(first.shape, f32),
        compiler_params=pltpu.CompilerParams(vmem_limit_bytes=2 * 2**20),
        cost_estimate=pl.CostEstimate(flops=flops, bytes_accessed=0, transcendentals=0),
        name="add",
    )(first, second, *after)


def moved_piece(there, coeff, moment_ref):
    return momentum_coef * moment_ref[:, there] + coeff


def embed_piece(there, coeff, moved, stack_ref, old_ref):
    up_high, up_low = split(coeff + momentum_coef * moved)
    change = jnp.dot(
        stack_ref[...],
        jnp.concatenate([up_high, up_high, up_low], axis=0),
        preferred_element_type=f32,
    )
    return old_ref[:, there] - outer_rate * change


def early_kernel(stack_ref, moment_ref, old_ref, coeff_ref, embed_ref, moved_ref):
    width = coeff_ref.shape[1]
    start = side_start(False, old_ref.shape[1] // 2)
    there = pl.ds(pl.multiple_of(start, width), width)
    coeff = coeff_ref[...]
    moved = moved_piece(there, coeff, moment_ref)
    moved_ref[...] = moved
    embed_ref[...] = embed_piece(there, coeff, moved, stack_ref, old_ref)


def embed_early(stack, moment, old, coeff):
    depth, (rank, width) = old.shape[0], coeff.shape
    return pl.pallas_call(
        early_kernel,
        in_specs=[WHOLE] * 4,
        out_specs=[WHOLE] * 2,
        out_shape=[
            jax.ShapeDtypeStruct((depth, width), f32),
            jax.ShapeDtypeStruct((rank, width), f32),
        ],
        compiler_params=pltpu.CompilerParams(vmem_limit_bytes=4 * 2**20),
        cost_estimate=pl.CostEstimate(
            flops=6 * rank * depth * width, bytes_accessed=8 * depth * width, transcendentals=0
        ),
        name="embed_early",
    )(stack, moment, old, coeff)


def embed_kernel(pieces, ready, stack_ref, moment_ref, old_ref, *refs):
    count = len(pieces)
    coeffs, refs = refs[:count], refs[count:]
    embed_hbm, moved_hbm, embed_ref, moved_ref, sems = refs[-5:]
    width = coeffs[0].shape[1]
    copies = []

    def place(other, part):
        start = side_start(other, old_ref.shape[1] // 2) + part * width
        return pl.ds(pl.multiple_of(start, width), width)

    def send(source, target, there):
        copies.append(pltpu.make_async_copy(source, target.at[:, there], sems.at[len(copies)]))
        copies[-1].start()

    if ready:
        there = place(*ready)
        send(refs[0], embed_hbm, there)
        send(refs[1], moved_hbm, there)
    for k, piece in enumerate(pieces):
        there = place(*piece)
        coeff = coeffs[k][...]
        moved = moved_piece(there, coeff, moment_ref)
        moved_ref[k] = moved
        send(moved_ref.at[k], moved_hbm, there)
        embed_ref[k] = embed_piece(there, coeff, moved, stack_ref, old_ref)
        send(embed_ref.at[k], embed_hbm, there)
    for copy in copies:
        copy.wait()


def embed_pieces(pieces, ready, stack, moment, old, coeffs, early, before):
    count = len(pieces)
    rank, width = coeffs[0].shape
    first = 3 + count + len(early)
    return pl.pallas_call(
        functools.partial(embed_kernel, pieces, ready),
        in_specs=[WHOLE] * first + [ANY] * len(before),
        out_specs=[ANY, ANY],
        out_shape=[
            jax.ShapeDtypeStruct(old.shape, f32),
            jax.ShapeDtypeStruct(moment.shape, f32),
        ],
        scratch_shapes=[
            pltpu.VMEM((count, old.shape[0], width), f32),
            pltpu.VMEM((count, rank, width), f32),
            pltpu.SemaphoreType.DMA((2 * count + len(early),)),
        ],
        input_output_aliases={first: 0, first + 1: 1} if before else {},
        compiler_params=pltpu.CompilerParams(vmem_limit_bytes=8 * 2**20),
        cost_estimate=pl.CostEstimate(
            flops=6 * count * rank * old.shape[0] * width,
            bytes_accessed=8 * count * old.shape[0] * width,
            transcendentals=0,
        ),
        name="embed_pieces",
    )(stack, moment, old, *coeffs, *early, *before)


def low_lanes(rows):
    return lax.broadcasted_iota(jnp.int32, (rows, LANES), 1) < HALF


def turn(value):
    return pltpu.roll(value, HALF, 1)


def attn_tiles(in_ref, out_ref):
    whole = in_ref.shape[-1] // LANES
    tiles = [in_ref[0, :, k * LANES : (k + 1) * LANES].astype(f32) for k in range(whole)]
    last = in_ref[0, :, whole * LANES :].astype(f32)
    side = out_ref[0, :, LANES:].astype(f32)
    tiles.append(jnp.concatenate([last, side], axis=-1))
    tiles.append(out_ref[0, :, :LANES].astype(f32))
    return tiles


def unflatten_attn(flat, put, rows):
    pairs = rows // 2
    low = low_lanes(pairs)
    inner = [flat(j, pairs, 9) for j in range(9)]
    base = pairs * 9
    outer = [flat(base + j, pairs, 3) for j in range(3)]
    turned = [turn(inner[j]) for j in range(4, 9)]
    turned_out = [turn(outer[j]) for j in (1, 2)]
    for k in range(4):
        put(0, k, inner[k])
        put(1, k, jnp.where(low, turned[k], turned[k + 1]))
    put(0, 4, jnp.where(low, inner[4], turned_out[0]))
    put(1, 4, jnp.where(low, turned[4], outer[2]))
    put(0, 5, outer[0])
    put(1, 5, jnp.where(low, turned_out[0], turned_out[1]))


def flatten_attn(get, rows):
    pairs = rows // 2
    low = low_lanes(pairs)
    even = [get(0, k) for k in range(6)]
    odd = [get(1, k) for k in range(6)]
    turned = [turn(odd[k]) for k in range(5)]
    pieces = [(k, 9, even[k]) for k in range(4)]
    pieces.append((4, 9, jnp.where(low, even[4], turned[0])))
    for k in range(4):
        pieces.append((5 + k, 9, jnp.where(low, turned[k], turned[k + 1])))
    base = pairs * 9
    pieces.append((base, 3, even[5]))
    turned_out = turn(odd[5])
    pieces.append((base + 1, 3, jnp.where(low, turn(even[4]), turned_out)))
    pieces.append((base + 2, 3, jnp.where(low, turned_out, odd[4])))
    return pieces


def before_kernel(
    order_ref, basis_ref, in_ref, out_ref, up_ref, down_ref, old_ref, mom_ref, small_ref,
    small_old_ref, small_mom_ref, send_ref, stack_ref, wide_ref,
):
    del order_ref
    basis = basis_ref[...]
    high = basis.astype(bf16).astype(f32)
    stack_ref[...] = jnp.concatenate([high, basis - high, high], axis=0).T.astype(bf16)
    group = lax.axis_index("group")
    rows = up_ref.shape[1]
    mid = rows // 2
    block = rows + mid
    tiles = up_ref.shape[2] // LANES
    small = small_old_ref.shape[1]

    def flat(start, count, stride):
        at = pl.ds(start, count, stride=stride)
        return old_coef * old_ref[at, :] + mom_coef * mom_ref[at, :]

    def put(start, tile, value):
        send_ref[tile, pl.ds(block + start, rows // 2, stride=2), :] = value

    def put_small(other, own):
        own_terms = (
            old_coef * small_old_ref[...] + mom_coef * small_mom_ref[...] + local_coef * own
        )
        send_ref[:, 2 * block :, :] = jnp.zeros((tiles, 8, LANES), f32)
        for tile, value in enumerate((other, own_terms)):
            for row in range(pl.cdiv(small, LANES)):
                piece = value[:, row * LANES : (row + 1) * LANES]
                at = 2 * block + row
                send_ref[tile, at : at + 1, : piece.shape[1]] = piece

    @pl.when(group == 0)
    def _():
        unflatten_attn(flat, put, rows)
        for k, value in enumerate(attn_tiles(in_ref, out_ref)):
            send_ref[k, block : block + rows, :] += local_coef * value
        base = rows * tiles
        for k in range(tiles):
            columns = slice(k * LANES, (k + 1) * LANES)
            send_ref[k, :mid, :] = up_ref[0, mid:, columns].astype(f32)
            send_ref[k, mid:block, :] = down_ref[0, :, columns].astype(f32)
            send_ref[k, block + rows : 2 * block, :] = flat(base + k, mid, tiles) + (
                local_coef * up_ref[0, :mid, columns].astype(f32)
            )
        values = small_ref[...].astype(f32)
        put_small(values[:, small:], values[:, :small])

    @pl.when(group == 1)
    def _():
        for k, value in enumerate(attn_tiles(in_ref, out_ref)):
            send_ref[k, :rows, :] = value
        for k in range(tiles):
            columns = slice(k * LANES, (k + 1) * LANES)
            send_ref[k, rows:block, :] = up_ref[0, :mid, columns].astype(f32)
            send_ref[k, block : block + mid, :] = flat(k, mid, tiles) + (
                local_coef * up_ref[0, mid:, columns].astype(f32)
            )
        base = mid * tiles
        pairs = tiles * HALF
        low = low_lanes(pairs)
        first, second, third = (flat(base + j, pairs, 3) for j in range(3))
        turned, turned_more = turn(second), turn(third)
        even, odd = pl.ds(0, pairs, stride=2), pl.ds(1, pairs, stride=2)
        wide_ref[0, even, :] = first
        wide_ref[1, even, :] = second
        wide_ref[0, odd, :] = jnp.where(low, turned, turned_more)
        wide_ref[1, odd, :] = turned_more
        start = block + mid
        for k in range(tiles):
            columns = slice(k * LANES, (k + 1) * LANES)
            upper = wide_ref[0, columns, :].T
            lower = wide_ref[1, columns, :].T[:HALF]
            send_ref[k, start : start + LANES, :] = upper + (
                local_coef * down_ref[0, :LANES, columns].astype(f32)
            )
            send_ref[k, start + LANES : 2 * block, :] = lower + (
                local_coef * down_ref[0, LANES:, columns].astype(f32)
            )
        values = small_ref[...].astype(f32)
        put_small(values[:, :small], values[:, small:])


def after_kernel(
    recv_ref, send_ref, in_ref, out_ref, up_ref, down_ref, old_ref, mom_ref, small_ref,
    small_old_ref, small_mom_ref, moment_hbm, *refs,
):
    targets, moment_ref, sources, (sum_ref, wide_ref, sems) = refs[:7], refs[7], refs[8:15], refs[15:]
    (
        in_next_ref, out_next_ref, up_next_ref, down_next_ref, moved_ref, small_next_ref,
        small_moved_ref,
    ) = sources
    copies = [
        pltpu.make_async_copy(source, target, sems.at[k])
        for k, (source, target) in enumerate(zip(sources, targets))
    ]
    copies.append(pltpu.make_async_copy(moment_hbm, moment_ref, sems.at[7]))
    copies[7].start()

    def go(*numbers):
        for k in numbers:
            copies[k].start()

    rows = up_ref.shape[1]
    mid = rows // 2
    block = rows + mid
    tiles = up_ref.shape[2] // LANES
    small = small_old_ref.shape[1]
    group = lax.axis_index("group")

    def put_moved(start, stride, value):
        at = pl.ds(start, value.shape[0], stride=stride)
        moved_ref[at, :] = momentum_coef * mom_ref[at, :] + (old_ref[at, :] - 0.5 * value)

    def get(start, tile):
        return sum_ref[tile, pl.ds(start, rows // 2, stride=2), :]

    def put_attn(tile, value):
        whole = in_ref.shape[-1] // LANES
        if tile < whole:
            in_next_ref[:, tile * LANES : (tile + 1) * LANES] = value
        elif tile == whole:
            in_next_ref[:, tile * LANES :] = value[:, :HALF]
            out_next_ref[:, LANES:] = turn(value)[:, :HALF]
        else:
            out_next_ref[:, :LANES] = value

    def small_row(ref, tile):
        pieces = []
        for row in range(pl.cdiv(small, LANES)):
            at = 2 * block + row
            pieces.append(ref[tile, at : at + 1, : min(LANES, small - row * LANES)])
        return jnp.concatenate(pieces, axis=1)

    def put_small(other, own, first):
        theirs = small_row(recv_ref, 0)
        mine = small_row(send_ref, 1) + local_coef * theirs
        rest = small_row(recv_ref, 1) + local_coef * other
        both = [mine, rest] if first else [rest, mine]
        small_next_ref[...] = jnp.concatenate(both, axis=1).reshape(-1)
        small_moved_ref[...] = momentum_coef * small_mom_ref[...] + (
            small_old_ref[...] - 0.5 * (own + theirs)
        )

    @pl.when(group == 0)
    def _():
        for k, value in enumerate(attn_tiles(in_ref, out_ref)):
            theirs = recv_ref[k, :rows, :]
            put_attn(k, send_ref[k, block : block + rows, :] + local_coef * theirs)
            sum_ref[k, :, :] = value + theirs
        go(0, 1)
        for start, stride, value in flatten_attn(get, rows):
            put_moved(start, stride, value)
        base = rows * tiles
        for k in range(tiles):
            columns = slice(k * LANES, (k + 1) * LANES)
            theirs = recv_ref[k, rows:block, :]
            up_next_ref[:mid, columns] = (
                send_ref[k, block + rows : 2 * block, :] + local_coef * theirs
            )
            put_moved(base + k, tiles, up_ref[0, :mid, columns].astype(f32) + theirs)
            up_next_ref[mid:, columns] = recv_ref[k, block : block + mid, :] + (
                local_coef * up_ref[0, mid:, columns].astype(f32)
            )
            down_next_ref[:, columns] = recv_ref[k, block + mid : 2 * block, :] + (
                local_coef * down_ref[0, :, columns].astype(f32)
            )
        go(2, 3, 4)
        values = small_ref[...].astype(f32)
        put_small(values[:, small:], values[:, :small], True)
        go(5, 6)
        for copy in copies:
            copy.wait()

    @pl.when(group == 1)
    def _():
        for k, value in enumerate(attn_tiles(in_ref, out_ref)):
            put_attn(k, recv_ref[k, block : block + rows, :] + local_coef * value)
        go(0, 1)
        for k in range(tiles):
            columns = slice(k * LANES, (k + 1) * LANES)
            up_next_ref[:mid, columns] = recv_ref[k, block + rows : 2 * block, :] + (
                local_coef * up_ref[0, :mid, columns].astype(f32)
            )
            theirs = recv_ref[k, :mid, :]
            up_next_ref[mid:, columns] = send_ref[k, block : block + mid, :] + local_coef * theirs
            put_moved(k, tiles, up_ref[0, mid:, columns].astype(f32) + theirs)
            theirs = recv_ref[k, mid:block, :]
            down_next_ref[:, columns] = (
                send_ref[k, block + mid : 2 * block, :] + local_coef * theirs
            )
            total = down_ref[0, :, columns].astype(f32) + theirs
            wide_ref[0, columns, :] = total[:LANES].T
            lower = jnp.concatenate([total[LANES:], total[LANES:]], axis=0)
            wide_ref[1, columns, :] = lower.T
        go(2, 3)
        base = mid * tiles
        pairs = tiles * HALF
        low = low_lanes(pairs)
        even, odd = pl.ds(0, pairs, stride=2), pl.ds(1, pairs, stride=2)
        odd_first = turn(wide_ref[0, odd, :])
        put_moved(base, 3, wide_ref[0, even, :])
        put_moved(base + 1, 3, jnp.where(low, wide_ref[1, even, :], odd_first))
        put_moved(base + 2, 3, jnp.where(low, odd_first, wide_ref[1, odd, :]))
        go(4)
        values = small_ref[...].astype(f32)
        put_small(values[:, :small], values[:, small:], False)
        go(5, 6)
        for copy in copies:
            copy.wait()


def dense_before(order, basis_t, operands):
    _, rows, width = operands[2].shape
    rank, depth = basis_t.shape
    return pl.pallas_call(
        before_kernel,
        in_specs=[ANY] + [WHOLE] * 10,
        out_specs=[WHOLE] * 2,
        out_shape=[
            jax.ShapeDtypeStruct((width // LANES, 3 * rows + 8, LANES), f32),
            jax.ShapeDtypeStruct((depth, 3 * rank), bf16),
        ],
        scratch_shapes=[pltpu.VMEM((2, width, LANES), f32)],
        compiler_params=pltpu.CompilerParams(vmem_limit_bytes=4 * 2**20),
        cost_estimate=pl.CostEstimate(
            flops=60000 * rows * width, bytes_accessed=30 * rows * width, transcendentals=0
        ),
        name="dense_before",
    )(order, basis_t, *operands)


def dense_after(received, sent, operands, moment):
    _, rows, width = operands[2].shape
    outs = [matrix.shape[1:] for matrix in operands[:4]]
    outs += [operands[4].shape, operands[6].shape[1:], operands[7].shape]
    return pl.pallas_call(
        after_kernel,
        in_specs=[WHOLE] * 11 + [ANY],
        out_specs=[ANY] * 7 + [WHOLE],
        out_shape=[jax.ShapeDtypeStruct(shape, f32) for shape in (*outs, moment.shape)],
        scratch_shapes=[pltpu.VMEM(shape, f32) for shape in outs]
        + [
            pltpu.VMEM((width // LANES, rows, LANES), f32),
            pltpu.VMEM((2, width, LANES), f32),
            pltpu.SemaphoreType.DMA((8,)),
        ],
        compiler_params=pltpu.CompilerParams(vmem_limit_bytes=8 * 2**20),
        cost_estimate=pl.CostEstimate(
            flops=60000 * rows * width, bytes_accessed=40 * rows * width, transcendentals=0
        ),
        name="dense_after",
    )(received, sent, *operands, *in_hbm([moment]))


def paired(
    attn_in_local,
    attn_out_local,
    ffn_in_local,
    ffn_out_local,
    small_local,
    dense_old,
    dense_momentum,
    small_old,
    small_momentum,
    embed_local,
    embed_old,
    basis,
    coeff_momentum,
):
    swap = [(0, 1), (1, 0)]
    chips = lax.axis_size("shard")

    first, second = (
        [
            (core * chips + chip, (1 - core) * chips + (chip ^ (1 + (core ^ turned(chip) ^ late))))
            for core in range(2)
            for chip in range(chips)
        ]
        for late in range(2)
    )
    axes = ("group", "shard")

    embed = (basis.T, embed_local[0], embed_old)
    theirs = [lax.ppermute(first_part(*embed[:2]), "group", swap)]
    late, *mine = other_parts(*embed)
    theirs.append(lax.ppermute(late, "group", swap))

    operands = (
        attn_in_local,
        attn_out_local,
        ffn_in_local,
        jnp.swapaxes(ffn_out_local, 1, 2),
        dense_old.reshape(-1, LANES),
        dense_momentum.reshape(-1, LANES),
        small_local,
        small_old[None, :],
        small_momentum[None, :],
    )
    totals = [add(*pair, flops=10**4) for pair in zip(mine, theirs)]
    moving = [lax.ppermute(total, axes, first) for total in totals]
    sent, stack = dense_before(totals[0], embed[0], operands)
    received = lax.ppermute(sent, "group", swap)
    totals = [
        add(*pair, flops=flops) for *pair, flops in zip(totals, moving, (10**4, 2 * 10**10))
    ]
    moving = [lax.ppermute(total, axes, second) for total in totals]
    *dense, moment = dense_after(received, sent, operands, coeff_momentum)
    moving[0], dense[-1] = lax.optimization_barrier((moving[0], dense[-1]))
    own = [add(totals[0], moving[0], scale=0.5)]
    rest = [lax.ppermute(own[0], "group", swap)]
    early = embed_early(stack, moment, embed_old, own[0])
    own.append(add(totals[1], moving[1], early[:1], scale=0.5))
    rest.append(lax.ppermute(own[1], "group", swap))
    shared = (stack, moment, embed_old)
    done = embed_pieces(
        ((False, 1), (True, 0)), (False, 0), *shared, (own[1], rest[0]), early, ()
    )
    done = embed_pieces(((True, 1),), None, *shared, rest[1:], (), done)
    embed_next, coeff_moved = done

    attn_in_next, attn_out_next, ffn_in_next, ffn_out_next, moved, small_next, small_moved = dense
    return (
        attn_in_next,
        attn_out_next,
        ffn_in_next,
        ffn_out_next.T,
        moved.reshape(dense_old.shape),
        small_next,
        small_moved[0],
        embed_next,
        coeff_moved,
    )


def is_paired(mesh, shapes):
    attn_in, attn_out, ffn_in, ffn_out = (shape[1:] for shape in shapes[:4])
    rows = ffn_in[0]
    return (
        mesh.shape["group"] == 2
        and mesh.shape["shard"] == 4
        and attn_in == (rows, 4 * LANES + HALF)
        and attn_out == (rows, LANES + HALF)
        and ffn_in[1] == 6 * LANES
        and ffn_out == (6 * LANES, rows)
        and rows == LANES + HALF
        and shapes[7][0] <= 8 * LANES
        and shapes[10][1] % (8 * LANES) == 0
    )


def solution(mesh):
    placed = (
        P("group", "shard", "tensor"),
        P("group", "shard", "tensor"),
        P("group", "shard", "tensor"),
        P("group", "shard", "tensor"),
        P("group", None),
        P(("shard", "tensor"), "group"),
        P(("shard", "tensor"), "group"),
        P("group"),
        P("group"),
        P("group", "shard", "tensor"),
        P("shard", "tensor"),
        P("shard", None),
        P(None, "tensor"),
    )

    def shards(*args):
        plan = paired if is_paired(mesh, [arg.shape for arg in args]) else general
        return plan(*args)

    return jax.shard_map(
        shards,
        mesh=mesh,
        in_specs=placed,
        out_specs=(
            P("shard", "tensor"),
            P("shard", "tensor"),
            P("shard", "tensor"),
            P("shard", "tensor"),
            P(("shard", "tensor"), "group"),
            P(),
            P("group"),
            P("shard", "tensor"),
            P(None, "tensor"),
        ),
        check_vma=False,
    )
```
